32 devices in a mesh: dp: 8 (over z, x), mp: 4 (over y, core).
Axes of the slice: x: 2, y: 2, z: 4, core: 2. Of those that a mesh axis runs over, the one named last changes fastest.
Arguments:
- block_input: bfloat16 [32768, 768], P('dp'), may hold values from -6 to 6
- cotangent: bfloat16 [32768, 768], P(('dp', 'mp')), may hold values from -6 to 6
- lengths: int32 [64, 4], P('dp'), may hold values from 1 to 256, 512 in all within a row
- partner: int32 [256], P('dp'), may hold values from 0 to 255, as said below
- qkv_weight: float32 [3, 768, 768], P(None, 'dp', 'mp')
- out_weight: float32 [768, 768], P('mp', 'dp')
- up_weight: float32 [768, 3072], P('dp', 'mp')
- down_weight: float32 [3072, 768], P('mp', 'dp')
- qkv_first: float32 [3, 768, 768], P(None, 'dp', 'mp'), may hold values from -512 to 512
- out_first: float32 [768, 768], P('mp', 'dp'), may hold values from -112 to 112
- up_first: float32 [768, 3072], P('dp', 'mp'), may hold values from -224 to 224
- down_first: float32 [3072, 768], P('mp', 'dp'), may hold values from -384 to 384
- qkv_second: float32 [3, 768, 768], P(None, 'dp', 'mp'), as said below
- out_second: float32 [768, 768], P('mp', 'dp'), as said below
- up_second: float32 [768, 3072], P('dp', 'mp'), as said below
- down_second: float32 [3072, 768], P('mp', 'dp'), as said below
- vectors: float32 [9216], replicated, as said below
- vector_first: float32 [9216], replicated, may hold values from -1024 to 1024
- vector_second: float32 [9216], replicated, may hold values from 32768 to 131072
Outputs:
- block_output: bfloat16 [32768, 768], P(('dp', 'mp'))
- input_grad: float32 [32768, 768], P(('dp', 'mp'))
- qkv_grad: float32 [3, 768, 768], P(None, 'dp', 'mp')
- out_grad: float32 [768, 768], P('mp', 'dp')
- up_grad: float32 [768, 3072], P('dp', 'mp')
- down_grad: float32 [3072, 768], P('mp', 'dp')
- qkv_second_new: float32 [3, 768, 768], P(None, 'dp', 'mp')
- out_second_new: float32 [768, 768], P('mp', 'dp')
- up_second_new: float32 [768, 3072], P('dp', 'mp')
- down_second_new: float32 [3072, 768], P('mp', 'dp')
- qkv_new: float32 [3, 768, 768], P(None, 'dp', 'mp')
- out_new: float32 [768, 768], P('mp', 'dp')
- up_new: float32 [768, 3072], P('dp', 'mp')
- down_new: float32 [3072, 768], P('mp', 'dp')
- qkv_copy: bfloat16 [3, 768, 768], P(None, 'dp', 'mp')
- out_copy: bfloat16 [768, 768], P('mp', 'dp')
- up_copy: bfloat16 [768, 3072], P('dp', 'mp')
- down_copy: bfloat16 [3072, 768], P('mp', 'dp')
- vector_grad: float32 [9216], replicated
- vector_second_new: float32 [9216], replicated
- vector_new: float32 [9216], replicated
- norms: float32 [6, 2], replicated
The draws below stay inside these ranges and needn't reach their ends.
Inputs may be any that keep to these rules, and one draw needn't show every extreme that they name: partner[partner[a]] = a and partner[a] != a for every passage a. `qkv_second`: entries are positive. `out_second`: entries are positive. `up_second`: entries are positive. `down_second`: entries are positive. `vectors`: gains g1 and g2 are positive.
All inputs are finite; a program needn't handle non-finite values.
Results may differ from the reference program's by a relative error of at most 0.025.
The reference program's roundings to bfloat16 on the way count: a program that leaves them out, or rounds other values in their place, can miss the bound.
Values may be sent and summed in bfloat16 or wider, within the bound.
No kernel may reach another device: no remote copies, remote signals or barrier semaphores. Data moves between devices by JAX's collectives and lax.ppermute only.
A program may use at most 192 MiB of HBM per device.

```python
import math
from functools import partial
import jax
import jax.numpy as jnp
import numpy as np
from jax import lax

D = 768
HEADS = 12
HD = 64
FF = 3072
L = 512
PASS = 4
MOST = 256
STEP = 10
ROWS_DEV = 8
NROWS = 64
TOKENS = 32768
N_CLS = 256
VEC = 9216


def rising(rows, cols, power):
    upper = jnp.arange(rows, dtype=jnp.float32) / max(rows - 1, 1)
    lower = jnp.arange(cols, dtype=jnp.float32) / max(cols - 1, 1)
    return jnp.exp(power * (upper[:, None] + lower[None, :]))


def scaled_weight(noise, power, fan_in):
    spread = (math.exp(2.0 * power) - 1.0) / (2.0 * power)
    return noise * rising(noise.shape[-2], noise.shape[-1], power) * fan_in ** (-0.5) / spread


def scaled_second(key, shape, scale, power):
    factor = jnp.exp(jax.random.uniform(key, shape, jnp.float32, 0.0, math.log(4.0)))
    return scale * scale * factor * rising(shape[-2], shape[-1], -2.0 * power)


def draw_qkv_weight(key, part):
    key = jax.random.fold_in(key, 1)
    noise = jax.random.normal(key, (3, D, D), jnp.float32)
    return scaled_weight(noise, 0.5 * math.log(3.0), D)


def draw_out_weight(key, part):
    key = jax.random.fold_in(key, 2)
    noise = jax.random.normal(key, (D, D), jnp.float32)
    return scaled_weight(noise, 0.5 * math.log(3.0), D // 16)


def draw_up_weight(key, part):
    key = jax.random.fold_in(key, 3)
    noise = jax.random.normal(key, (D, FF), jnp.float32)
    return scaled_weight(noise, 0.5 * math.log(3.0), D)


def draw_down_weight(key, part):
    key = jax.random.fold_in(key, 4)
    noise = jax.random.normal(key, (FF, D), jnp.float32)
    return scaled_weight(noise, 0.5 * math.log(3.0), FF)


def draw_qkv_second(key, part):
    key = jax.random.fold_in(key, 5)
    return scaled_second(key, (3, D, D), 0.5 * TOKENS ** 0.5, 0.5 * math.log(3.0))


def draw_out_second(key, part):
    key = jax.random.fold_in(key, 6)
    return scaled_second(key, (D, D), 0.1 * TOKENS ** 0.5, 0.5 * math.log(3.0))


def draw_up_second(key, part):
    key = jax.random.fold_in(key, 7)
    return scaled_second(key, (D, FF), 0.2 * TOKENS ** 0.5, 0.5 * math.log(3.0))


def draw_down_second(key, part):
    key = jax.random.fold_in(key, 8)
    return scaled_second(key, (FF, D), 0.35 * TOKENS ** 0.5, 0.5 * math.log(3.0))


def draw_vectors(key, part):
    key = jax.random.fold_in(key, 9)
    bias_key, gain_key = jax.random.split(key)
    places = jnp.arange(8 * D + FF)
    gain_start = 4 * D + FF
    is_gain = (places >= gain_start) & (places < gain_start + D) | (places >= gain_start + 2 * D) & (places < gain_start + 3 * D)
    biases = 0.5 * jax.random.normal(bias_key, (8 * D + FF,), jnp.float32)
    gains = 1.0 + jax.random.uniform(gain_key, (8 * D + FF,), jnp.float32, -0.25, 0.25)
    return jnp.where(is_gain, gains, biases)


def draw_partner(key, part):
    key = jax.random.fold_in(key, 10)
    order = jax.random.permutation(key, N_CLS).astype(jnp.int32)
    pairs = order.reshape(N_CLS // 2, 2)
    result = jnp.zeros((N_CLS,), jnp.int32)
    result = result.at[pairs[:, 0]].set(pairs[:, 1])
    return result.at[pairs[:, 1]].set(pairs[:, 0])


def levels(rng, shape, cuts, low, top_value):
    def one(position, blocks):
        heights = jax.random.uniform(jax.random.fold_in(jax.random.fold_in(rng, 6), position), (blocks,), jnp.float32, low / len(cuts), top_value / len(cuts))
        return jnp.repeat(jnp.exp(heights), shape[position] // blocks).reshape((-1,) + (1,) * (len(shape) - position - 1))

    level = one(*cuts[0])
    for cut in cuts[1:]:
        level = level * one(*cut)
    return level


def profile(amount, total, limit, lean):
    portions = [(1 << 20) // math.isqrt(standing ** lean) + 1 for standing in range(2, amount + 1)]
    rest, given = total - limit - (amount - 1), [1] * (amount - 1)
    while rest > 0:
        free = [i for i in range(amount - 1) if given[i] < limit]
        pool, remaining = sum([portions[i] for i in free]), rest
        for i in free:
            addition = min(limit - given[i], max(1, remaining * portions[i] // pool), rest)
            given[i] = given[i] + addition
            rest = rest - addition
    return np.array([limit] + given)


def uneven_parts(own_key, number_of, total, limit, skew):
    if number_of == 2:
        one = jax.random.randint(own_key, (), max(1, total - limit), min(limit, total - 1) + 1)
        return jnp.stack([one, total - one])
    sizes = jnp.asarray(profile(number_of, total, limit, skew), jnp.int32)
    couples = (number_of - 1) // 2
    giver, receiver = sizes[1:1 + 2 * couples:2], sizes[2:2 + 2 * couples:2]
    margin = jnp.minimum(giver - 1, limit - receiver)
    shifted = jax.random.randint(jax.random.fold_in(own_key, 1), (couples,), 0, 1 << 20) % (margin + 1)
    sizes = sizes.at[1:1 + 2 * couples:2].set(giver - shifted).at[2:2 + 2 * couples:2].set(receiver + shifted)
    return sizes[jax.random.permutation(jax.random.fold_in(own_key, 2), number_of)]


def scatter_about(key, dims, scale, bound, cuts=(), held_as=jnp.bfloat16):
    level = levels(key, dims, cuts, -0.22, 0.18) if cuts else 1.0
    drawn = jax.random.normal(key, dims, jnp.float32) * scale * level
    return jnp.minimum(jnp.maximum(drawn, -bound), bound).astype(held_as)


def setup_inputs(seed: int = 0) -> dict:
    key_of = jax.random.split(jax.random.key(seed), 20)
    return {
        "block_input": scatter_about(key_of[0], (TOKENS, D), 1.3, 6.0, ((0, 8),)),
        "cotangent": scatter_about(key_of[1], (TOKENS, D), 1.0, 6.0, ((0, 32),)),
        "lengths": jax.vmap(lambda own: uneven_parts(own, PASS, L, MOST, 2))(jax.random.split(key_of[2], NROWS)).reshape((NROWS, PASS)).astype(jnp.int32),
        "partner": draw_partner(jax.random.fold_in(key_of[19], 71), 0),
        "qkv_weight": draw_qkv_weight(jax.random.fold_in(key_of[19], 71), 0),
        "out_weight": draw_out_weight(jax.random.fold_in(key_of[19], 71), 0),
        "up_weight": draw_up_weight(jax.random.fold_in(key_of[19], 71), 0),
        "down_weight": draw_down_weight(jax.random.fold_in(key_of[19], 71), 0),
        "qkv_first": scatter_about(key_of[8], (3, D, D), (0.5 * TOKENS ** 0.5), 512.0, ((1, 8), (2, 4)), jnp.float32),
        "out_first": scatter_about(key_of[9], (D, D), (0.1 * TOKENS ** 0.5), 112.0, ((0, 4), (1, 8)), jnp.float32),
        "up_first": scatter_about(key_of[10], (D, FF), (0.2 * TOKENS ** 0.5), 224.0, ((0, 8), (1, 4)), jnp.float32),
        "down_first": scatter_about(key_of[11], (FF, D), (0.35 * TOKENS ** 0.5), 384.0, ((0, 4), (1, 8)), jnp.float32),
        "qkv_second": draw_qkv_second(jax.random.fold_in(key_of[19], 71), 0),
        "out_second": draw_out_second(jax.random.fold_in(key_of[19], 71), 0),
        "up_second": draw_up_second(jax.random.fold_in(key_of[19], 71), 0),
        "down_second": draw_down_second(jax.random.fold_in(key_of[19], 71), 0),
        "vectors": draw_vectors(jax.random.fold_in(key_of[19], 71), 0),
        "vector_first": scatter_about(key_of[17], (VEC,), (TOKENS ** 0.5), 1024.0, (), jnp.float32),
        "vector_second": jnp.clip(jnp.exp(jax.random.uniform(key_of[18], (VEC,), jnp.float32, math.log(32768.0), math.log(131072.0))), 32768.0, 131072.0),
    }


@jax.custom_vjp
def low(v):
    return lax.optimization_barrier(v.astype(jnp.bfloat16)).astype(jnp.float32)

@jax.custom_vjp
def low_back(v):
    return v

def low_keep(v):
    return (low(v), None)

def low_pass(kept, grad):
    return (grad,)

def back_keep(v):
    return (v, None)

def back_low(kept, grad):
    return (low(grad),)
low.defvjp(low_keep, low_pass)
low_back.defvjp(back_keep, back_low)
masked_value = -1e+30
grid_weight = 4.0
norm_eps = 1e-12
beta_decay = 0.5
adam_eps = 1e-06
norm_guard = 1e-06
weight_decay = 0.01
rate_matrix = 1.0
rate_vector = 0.2

def product(left, right):
    return jnp.matmul(left, right, precision=lax.Precision.HIGHEST)

def rounded_both(value):
    return low_back(low(value))

def layer_norm(value, gain, shift):
    center = lax.optimization_barrier(jnp.mean(value, axis=-1, keepdims=True))
    offsets = value - center
    spread = lax.optimization_barrier(jnp.mean(offsets * offsets, axis=-1, keepdims=True))
    return offsets * lax.rsqrt(spread + norm_eps) * gain + shift

def passage_ids(lengths):
    starts = (jnp.cumsum(lengths, axis=1) - lengths).astype(jnp.int32)
    positions = jnp.arange(L, dtype=jnp.int32)
    return lax.optimization_barrier(jnp.sum((positions[None, :, None] >= starts[:, None, :]).astype(jnp.int32), axis=2)) - 1

def split_vectors(vectors):
    tail = 2 * D + FF
    return (vectors[0:D], vectors[D:2 * D], vectors[2 * D:tail], vectors[tail:tail + D], vectors[tail + D:tail + 2 * D], vectors[tail + 2 * D:tail + 3 * D], vectors[tail + 3 * D:tail + 4 * D], vectors[tail + 4 * D:tail + 5 * D], vectors[tail + 5 * D:tail + 6 * D])

def attend_row(pieces):
    queries, keys, values, passage = pieces
    scores = low_back(jnp.einsum('qhd,khd->hqk', queries, keys, precision=lax.Precision.HIGHEST) * HD ** (-0.5))
    same_passage = passage[:, None] == passage[None, :]
    scores = jnp.where(same_passage[None], scores, masked_value)
    highest = lax.optimization_barrier(jnp.max(scores, axis=-1, keepdims=True))
    weights = jnp.exp(scores - highest)
    shares = weights / lax.optimization_barrier(jnp.sum(weights, axis=-1, keepdims=True))
    return jnp.einsum('hqk,khd->qhd', low(shares), values, precision=lax.Precision.HIGHEST)

def layer(inputs, passages, params):
    qkv_weight, out_weight, up_weight, down_weight, vectors = params
    bias_query, bias_value, bias_up, bias_out, bias_down, gain_first, shift_first, gain_second, shift_second = split_vectors(vectors)
    queries = rounded_both(product(inputs, low(qkv_weight[0])) + bias_query)
    keys = rounded_both(product(inputs, low(qkv_weight[1])))
    values = rounded_both(product(inputs, low(qkv_weight[2])) + bias_value)
    row_shape = (ROWS_DEV, L, HEADS, HD)
    context = lax.map(jax.checkpoint(attend_row), (queries.reshape(row_shape), keys.reshape(row_shape), values.reshape(row_shape), passages))
    context = rounded_both(context.reshape(ROWS_DEV * L, D))
    attended = low_back(product(context, low(out_weight)) + bias_out)
    normed = layer_norm(inputs + attended, gain_first, shift_first)
    hidden = low_back(product(low(normed), low(up_weight)) + bias_up)
    activated = low(jax.nn.gelu(hidden, approximate=False))
    branch = low_back(product(activated, low(down_weight)) + bias_down)
    return layer_norm(normed + branch, gain_second, shift_second)

def grid_loss(cls_rows, partner):
    low_cls = low(cls_rows)
    scores = low_back(product(low_cls, low_cls.T) * (2.0 / math.sqrt(D)))
    places = jnp.arange(N_CLS, dtype=jnp.int32)
    masked = jnp.where(places[:, None] == places[None, :], masked_value, scores)
    highest = lax.optimization_barrier(jnp.max(masked, axis=1, keepdims=True))
    log_totals = jnp.log(lax.optimization_barrier(jnp.sum(jnp.exp(masked - highest), axis=1))) + highest[:, 0]
    targets = lax.optimization_barrier(jnp.sum(jnp.where(partner[:, None] == places[None, :], scores, 0.0), axis=1))
    return grid_weight * jnp.sum(log_totals - targets)

def adapt(grad, earlier, second):
    moment = beta_decay * earlier + (1.0 - beta_decay) * grad
    second_new = beta_decay * second + (1.0 - beta_decay) * grad * grad
    ratio = moment / (1.0 - beta_decay ** STEP) / (jnp.sqrt(second_new / (1.0 - beta_decay ** STEP)) + adam_eps)
    return (second_new, ratio)

def reference(block_input, cotangent, lengths, partner, qkv_weight, out_weight, up_weight, down_weight, qkv_first, out_first, up_first, down_first, qkv_second, out_second, up_second, down_second, vectors, vector_first, vector_second):
    groups = NROWS // ROWS_DEV
    group_tokens = ROWS_DEV * L
    params = (qkv_weight, out_weight, up_weight, down_weight, vectors)
    inputs = block_input.astype(jnp.float32).reshape(groups, group_tokens, D)
    passages = passage_ids(lengths).reshape(groups, ROWS_DEV, L)

    def forward_group(pieces):
        return layer(pieces[0], pieces[1], params)
    outputs = lax.map(forward_group, (inputs, passages)).reshape(TOKENS, D)
    starts = (jnp.cumsum(lengths, axis=1) - lengths).astype(jnp.int32)
    positions = (jnp.arange(NROWS, dtype=jnp.int32)[:, None] * L + starts).reshape(N_CLS)
    cls_rows = outputs[positions]
    _, grid_back = jax.vjp(partial(grid_loss, partner=partner), cls_rows)
    cls_grad = grid_back(jnp.ones((), jnp.float32))[0]
    output_grad = cotangent.astype(jnp.float32).reshape(TOKENS, D).at[positions].add(cls_grad)
    output_grad = output_grad.reshape(groups, group_tokens, D)

    def accumulate(running, pieces):
        group_input, group_passage, group_grad = pieces

        def run_layer(layer_input, *weights):
            return layer(layer_input, group_passage, weights)
        _, layer_back = jax.vjp(run_layer, group_input, *params)
        grads = layer_back(group_grad)
        return (jax.tree.map(jnp.add, running, tuple(grads[1:])), grads[0])
    starting = jax.tree.map(jnp.zeros_like, params)
    running, input_grads = lax.scan(accumulate, starting, (inputs, passages, output_grad))
    qkv_grad, out_grad, up_grad, down_grad, vector_grad = running
    qkv_second_new, qkv_ratio = adapt(qkv_grad, qkv_first, qkv_second)
    out_second_new, out_ratio = adapt(out_grad, out_first, out_second)
    up_second_new, up_ratio = adapt(up_grad, up_first, up_second)
    down_second_new, down_ratio = adapt(down_grad, down_first, down_second)
    qkv_update = qkv_ratio + weight_decay * qkv_weight
    out_update = out_ratio + weight_decay * out_weight
    up_update = up_ratio + weight_decay * up_weight
    down_update = down_ratio + weight_decay * down_weight
    weight_norms = jnp.sqrt(jnp.concatenate([lax.optimization_barrier(jnp.sum(qkv_weight * qkv_weight, axis=(1, 2))), jnp.sum(out_weight * out_weight)[None], jnp.sum(up_weight * up_weight)[None], jnp.sum(down_weight * down_weight)[None]]))
    update_norms = jnp.sqrt(jnp.concatenate([lax.optimization_barrier(jnp.sum(qkv_update * qkv_update, axis=(1, 2))), jnp.sum(out_update * out_update)[None], jnp.sum(up_update * up_update)[None], jnp.sum(down_update * down_update)[None]]))
    trust = weight_norms / (update_norms + norm_guard)
    qkv_new = qkv_weight - rate_matrix * trust[0:3, None, None] * qkv_update
    out_new = out_weight - rate_matrix * trust[3] * out_update
    up_new = up_weight - rate_matrix * trust[4] * up_update
    down_new = down_weight - rate_matrix * trust[5] * down_update
    vector_second_new, vector_ratio = adapt(vector_grad, vector_first, vector_second)
    vector_new = vectors - rate_vector * vector_ratio
    norms = jnp.stack([weight_norms, update_norms], axis=1)
    return (outputs.astype(jnp.bfloat16), input_grads.reshape(TOKENS, D), qkv_grad, out_grad, up_grad, down_grad, qkv_second_new, out_second_new, up_second_new, down_second_new, qkv_new, out_new, up_new, down_new, qkv_new.astype(jnp.bfloat16), out_new.astype(jnp.bfloat16), up_new.astype(jnp.bfloat16), down_new.astype(jnp.bfloat16), vector_grad, vector_second_new, vector_new, norms)
```

```python
from functools import partial
import math

import jax
import jax.numpy as jnp
from jax import lax
from jax.experimental import pallas as pl
from jax.experimental.pallas import tpu as pltpu
from jax.sharding import PartitionSpec as P

D = 768
HEADS = 12
HD = 64
FF = 3072
L = 512
PASS = 4
STEP = 10
ROWS_DEV = 8
MIB = 1 << 20
TAIL = 2 * D + FF


masked_value = -1e30
grid_weight = 4.0
norm_eps = 1e-12
beta_decay = 0.5
adam_eps = 1e-06
norm_guard = 1e-06
weight_decay = 0.01
rate_matrix = 1.0
rate_vector = 0.2


def passage_ids(lengths):
    starts = jnp.cumsum(lengths, axis=1) - lengths
    positions = jnp.arange(L, dtype=jnp.int32)
    return jnp.sum((positions[None, :, None] >= starts[:, None, :]).astype(jnp.int32), axis=2) - 1


def adapt(grad, earlier, second):
    moment = beta_decay * earlier + (1.0 - beta_decay) * grad
    second_new = beta_decay * second + (1.0 - beta_decay) * grad * grad
    ratio = (
        moment
        / (1.0 - beta_decay**STEP)
        / (jnp.sqrt(second_new / (1.0 - beta_decay**STEP)) + adam_eps)
    )
    return (second_new, ratio)


AXES = ("dp", "mp")
GRID = (8, 4)


def links(move):
    pairs = []
    for z in range(4):
        for x in range(2):
            for y in range(2):
                for c in range(2):
                    tz, tx, ty, tc = move(z, x, y, c)
                    pairs.append(
                        ((z * 2 + x) * 4 + y * 2 + c, (tz % 4 * 2 + tx) * 4 + ty * 2 + tc)
                    )
    return pairs


CORE = links(lambda z, x, y, c: (z, x, y, 1 - c))
OVER_X = links(lambda z, x, y, c: (z, 1 - x, y, c))
OVER_Y = links(lambda z, x, y, c: (z, x, 1 - y, c))
UP_Z = [links(lambda z, x, y, c, s=s: (z + s, x, y, c)) for s in range(4)]


def send(value, pairs):
    return lax.ppermute(value, AXES, pairs)


def on_grid():
    return (lax.axis_size("dp"), lax.axis_size("mp")) == GRID


def place():
    dp_index = lax.axis_index("dp")
    mp_index = lax.axis_index("mp")
    return jnp.stack([dp_index // 2, dp_index % 2, mp_index // 2, mp_index % 2])


ITEMS = (
    [(x, 0, z) for x in (0, 1) for z in (0, 1)]
    + [(0, y, z) for y in (0, 1) for z in (2, 3)]
    + [(x, 1, z) for x in (0, 1) for z in (0, 1)]
    + [(1, y, z) for y in (0, 1) for z in (2, 3)]
)


def settle_kernel(where, *refs):
    pieces, out, sems = refs[:8], refs[8], refs[9]
    z0, x0, y0, c0 = where[0], where[1], where[2], where[3]
    copies = []
    for core in range(2):
        for item, (x, y, z) in enumerate(ITEMS):
            source = pieces[core * 4 + item // 4].at[item % 4]
            block = (y0 + y) % 2 * 2 + (c0 + core) % 2
            row = (z0 + 4 - z) % 4 * 2 + (x0 + x) % 2
            copy = pltpu.make_async_copy(source, out.at[block, row], sems.at[core * 16 + item])
            copy.start()
            copies.append(copy)
    for copy in copies:
        copy.wait()


def gather(shard):
    rows, width = shard.shape
    if not on_grid():
        return lax.all_gather(shard, ("mp", "dp"), axis=0, tiled=True).reshape(
            lax.axis_size("mp"), -1, width
        )
    first = jnp.stack([shard, send(shard, UP_Z[1])])
    second = jnp.stack([send(shard, UP_Z[2]), send(shard, UP_Z[3])])
    first = jnp.concatenate([first, send(first, OVER_X)])
    second = jnp.concatenate([second, send(second, OVER_Y)])
    pieces = [first, second, send(first, OVER_Y), send(second, OVER_X)]
    pieces = pieces + [send(piece, CORE) for piece in pieces]
    whole = pl.pallas_call(
        settle_kernel,
        grid_spec=pltpu.PrefetchScalarGridSpec(
            num_scalar_prefetch=1,
            grid=(1,),
            in_specs=[pl.BlockSpec(memory_space=pl.ANY)] * 8,
            out_specs=pl.BlockSpec((4, 8, rows, width), lambda i, where: (0, 0, 0, 0)),
            scratch_shapes=[pltpu.SemaphoreType.DMA((32,))],
        ),
        out_shape=jax.ShapeDtypeStruct((4, 8, rows, width), shard.dtype),
        compiler_params=pltpu.CompilerParams(vmem_limit_bytes=24 * MIB),
        name="settle",
    )(place(), *pieces)
    return whole.reshape(4, 8 * rows, width)


def plus(left, right):
    return (left.astype(jnp.float32) + right.astype(jnp.float32)).astype(jnp.bfloat16)


def scatter_sum(items):
    if not on_grid():
        return lax.psum_scatter(
            items.reshape(-1, items.shape[-1]), ("mp", "dp"), scatter_dimension=0, tiled=True
        ).astype(jnp.float32)
    items = plus(items[0], send(items[1], CORE))
    first = plus(items[0, :, :2], send(items[1, :, :2], OVER_Y))
    second = plus(items[:, 0, 2:], send(items[:, 1, 2:], OVER_X))
    first = plus(first[0], send(first[1], OVER_X))
    second = plus(second[0], send(second[1], OVER_Y))
    parts = [first[0]]
    for step, part in ((1, first[1]), (2, second[0]), (3, second[1])):
        parts.append(send(part, UP_Z[step]))
    return sum(part.astype(jnp.float32) for part in parts)


def summand(mp_size, dp_size):
    rows = D // dp_size
    if not on_grid():

        def write_plain(out, value, where):
            out[0] = value

        return (mp_size, D, D), (1, D, D), lambda g, where: (g, 0, 0), write_plain, lambda g, where: g

    def write(out, value, where):
        z0, x0 = where[0], where[1]
        for index in range(dp_size):
            z, x = index // 2, index % 2
            out[0, 0, (x + x0) % 2, (z + 4 - z0) % 4] = value[index * rows : (index + 1) * rows]

    def block(g, where):
        return ((where[2] + g % 2) % 2) * 2 + (where[3] + g // 2) % 2

    return (
        (2, 2, 2, 4, rows, D),
        (1, 1, 2, 4, rows, D),
        lambda g, where: (g // 2, g % 2, 0, 0, 0, 0),
        write,
        block,
    )


def share(value):
    if not on_grid():
        dp_size, mp_size = lax.axis_size("dp"), lax.axis_size("mp")
        whole = lax.all_gather(value, AXES, axis=0, tiled=True)
        own = lax.axis_index("dp") * mp_size + lax.axis_index("mp")
        return jnp.roll(whole, -own * value.shape[0], axis=0)
    for pairs in (CORE, OVER_X, OVER_Y):
        value = jnp.concatenate([value, send(value, pairs)])
    return jnp.concatenate([value] + [send(value, UP_Z[s]) for s in (1, 2, 3)])


def total(value):
    if not on_grid():
        return lax.psum(value, AXES)
    for pairs in (CORE, OVER_X, OVER_Y):
        value = value + send(value, pairs)
    pair = value + send(value, UP_Z[2])
    return pair + send(pair, UP_Z[1])

LOW = jnp.bfloat16
WIDE = jnp.float32
B1, BO, B2, G1, C1, G2, C2 = 2 * D, TAIL, TAIL + D, TAIL + 2 * D, TAIL + 3 * D, TAIL + 4 * D, TAIL + 5 * D
VEC = 8 * D + FF


def dot(left, right, over=(1, 0)):
    return lax.dot_general(
        left, right, (((over[0],), (over[1],)), ((), ())), preferred_element_type=WIDE
    )


def call(kernel, name, grid, in_specs, out_specs, out_shape, scratch=(), limit=48, flops=0, args=()):
    return pl.pallas_call(
        kernel,
        grid_spec=pltpu.PrefetchScalarGridSpec(
            num_scalar_prefetch=1,
            grid=grid,
            in_specs=in_specs,
            out_specs=out_specs,
            scratch_shapes=list(scratch),
        ),
        out_shape=out_shape,
        compiler_params=pltpu.CompilerParams(vmem_limit_bytes=limit * MIB),
        cost_estimate=pl.CostEstimate(flops=flops, bytes_accessed=MIB, transcendentals=0),
        name=name,
    )(*args)


def whole(*shape):
    zeros = (0,) * len(shape)
    return pl.BlockSpec(shape, lambda *_: zeros)


def once(*shape):
    zeros = (0,) * len(shape)
    return pl.BlockSpec(shape, lambda *_: zeros, pipeline_mode=pl.Buffered(1))


def stepped(place, *shape):
    def index(step, *_):
        return tuple(step if i == place else 0 for i in range(len(shape)))

    return pl.BlockSpec(shape, index)


def array(dtype, *shape):
    return jax.ShapeDtypeStruct(shape, dtype)


def normalize(value):
    center = jnp.mean(value, axis=1, keepdims=True)
    offsets = value - center
    inverse = lax.rsqrt(jnp.mean(offsets * offsets, axis=1, keepdims=True) + norm_eps)
    return offsets * inverse, inverse


def norm_back(grad, unit, inverse, gain):
    scaled = grad * gain
    return inverse * (
        scaled
        - jnp.mean(scaled, axis=1, keepdims=True)
        - unit * jnp.mean(scaled * unit, axis=1, keepdims=True)
    )


def column_sum(value):
    return jnp.sum(value, axis=0, keepdims=True)


def add_to(first, ref, value):
    @pl.when(first)
    def _():
        ref[...] = jnp.zeros_like(ref)

    ref[...] += value


def attend_kernel(
    blocks, where, x_ref, w_ref, bias_ref, vec_ref, seg_ref,
    q_out, k_out, v_out, context_out, unit_out, inverse_out, low_out, sum_ref,
):
    heads = HEADS // blocks
    width = HD * heads
    x = x_ref[...]
    lanes = lax.broadcasted_iota(jnp.int32, (L, 2 * HD), 1)
    passage = jnp.broadcast_to(seg_ref[...], (L, 2 * HD)) + HD
    is_passage = (lanes >= HD) & (lanes < HD + PASS)
    q_mask = jnp.where(is_passage & (lanes != passage), masked_value, 0.0)
    k_mask = jnp.where(
        (lanes == passage) | ((lanes >= HD + PASS) & (lanes < HD + PASS + 3)), 1.0, 0.0
    ).astype(LOW)[:, HD:]
    sum_ref[...] = x.astype(WIDE) + vec_ref[:, BO : BO + D]

    def block(m, carry):
        projected = (dot(x, w_ref[m]) + bias_ref[m]).astype(LOW)
        parts = []
        for h in range(heads):
            at = width + h * HD
            query = projected[:, at : at + HD] * jnp.asarray(HD ** (-0.5), LOW)
            key = projected[:, at + width : at + width + HD]
            value = projected[:, at + 2 * width : at + 2 * width + HD]
            keys = jnp.concatenate([key, k_mask], axis=1)
            queries = jnp.concatenate([query, q_mask[:, HD:].astype(LOW)], axis=1)
            scores = dot(keys, queries, (1, 1))
            highest = jnp.max(scores, axis=0, keepdims=True)
            weights = jnp.exp(scores - highest)
            totals = jnp.sum(weights, axis=0, keepdims=True)
            mixed = dot(value.T, weights.astype(LOW)) * (1.0 / totals)
            left = -(highest + jnp.log(totals))
            high = left.astype(LOW).astype(WIDE)
            middle = (left - high).astype(LOW).astype(WIDE)
            lowest = left - high - middle
            rows = lax.broadcasted_iota(jnp.int32, (HD, L), 0)
            split = jnp.where(rows == PASS, high, 0.0)
            split = jnp.where(rows == PASS + 1, middle, split)
            split = jnp.where(rows == PASS + 2, lowest, split)
            turned = jnp.concatenate([mixed, split], axis=0).T
            parts.append(turned[:, :HD].astype(LOW))
            q_out[m * heads + h] = jnp.concatenate(
                [query, (q_mask + turned)[:, HD:].astype(LOW)], axis=1
            )
            k_out[m * heads + h] = keys
            v_out[m * heads + h] = value
        context = jnp.concatenate(parts, axis=1)
        context_out[m] = context
        sum_ref[...] += dot(context, w_ref[m, :, :width], (1, 1))
        return carry

    lax.fori_loop(0, blocks, block, 0)
    unit, inverse = normalize(sum_ref[...])
    unit_out[...] = unit
    inverse_out[...] = inverse
    low_out[...] = (unit * vec_ref[:, G1 : G1 + D] + vec_ref[:, C1 : C1 + D]).astype(LOW)


def attend(where, inputs, weights, bias, vectors, segments):
    tokens = inputs.shape[0]
    blocks = weights.shape[0]
    width = D // blocks
    return call(
        partial(attend_kernel, blocks),
        "attend",
        (tokens // L,),
        [
            stepped(0, L, D),
            once(blocks, D, D),
            whole(blocks, 1, D),
            whole(1, VEC),
            stepped(0, L, 1),
        ],
        [
            stepped(1, HEADS, L, 2 * HD),
            stepped(1, HEADS, L, 2 * HD),
            stepped(1, HEADS, L, HD),
            stepped(1, blocks, L, width),
            stepped(0, L, D),
            stepped(0, L, 1),
            stepped(0, L, D),
        ],
        [
            array(LOW, HEADS, tokens, 2 * HD),
            array(LOW, HEADS, tokens, 2 * HD),
            array(LOW, HEADS, tokens, HD),
            array(LOW, blocks, tokens, width),
            array(WIDE, tokens, D),
            array(WIDE, tokens, 1),
            array(LOW, tokens, D),
        ],
        [pltpu.VMEM((L, D), WIDE)],
        flops=24 * 10**9,
        args=(where, inputs, weights, bias, vectors, segments),
    )


def widen_kernel(where, h_ref, w_ref, vec_ref, active_out, slope_out):
    step = pl.program_id(0)
    hidden = dot(h_ref[...], w_ref[0]) + vec_ref[0]
    half = 0.5 * (1.0 + lax.erf(hidden * math.sqrt(0.5)))
    active_out[0] = (hidden * half).astype(LOW)
    density = jnp.exp(-0.5 * hidden * hidden) * (1.0 / math.sqrt(2.0 * math.pi))
    slope_out[0] = (half + hidden * density).astype(LOW)


def widen(where, normed_low, weights, bias):
    tokens = normed_low.shape[0]
    blocks = weights.shape[0]
    return call(
        widen_kernel,
        "widen",
        (blocks,),
        [whole(tokens, D), stepped(0, 1, D, D), stepped(0, 1, 1, D)],
        [stepped(0, 1, tokens, D)] * 2,
        [array(LOW, blocks, tokens, D)] * 2,
        flops=10 * 10**9,
        args=(where, normed_low, weights, bias),
    )


def narrow_kernel(blocks, where, active_ref, w_ref, vec_ref, unit_ref, starts_ref, out, unit_out, inverse_out, cls_out, y_ref):
    row = pl.program_id(0)
    total_sum = unit_ref[...] * vec_ref[:, G1 : G1 + D] + (
        vec_ref[:, C1 : C1 + D] + vec_ref[:, B2 : B2 + D]
    )
    for m in range(blocks):
        total_sum += dot(active_ref[m], w_ref[m], (1, 1))
    unit, inverse = normalize(total_sum)
    unit_out[...] = unit
    inverse_out[...] = inverse
    output = unit * vec_ref[:, G2 : G2 + D] + vec_ref[:, C2 : C2 + D]
    out[...] = output.astype(LOW)
    y_ref[...] = output
    for p in range(PASS):
        cls_out[pl.ds(row * PASS + p, 1), :] = y_ref[pl.ds(starts_ref[row * PASS + p], 1), :]


def narrow(where, active, weights, vectors, unit, starts):
    blocks, tokens, _ = active.shape
    rows = tokens // L
    return call(
        partial(narrow_kernel, blocks),
        "narrow",
        (rows,),
        [
            stepped(1, blocks, L, D),
            once(blocks, D, D),
            whole(1, VEC),
            stepped(0, L, D),
            pl.BlockSpec(memory_space=pltpu.SMEM),
        ],
        [stepped(0, L, D), stepped(0, L, D), stepped(0, L, 1), whole(rows * PASS, D)],
        [
            array(LOW, tokens, D),
            array(WIDE, tokens, D),
            array(WIDE, tokens, 1),
            array(WIDE, rows * PASS, D),
        ],
        [pltpu.VMEM((L, D), WIDE)],
        flops=5 * 10**9,
        args=(where, active, weights, vectors, unit, starts),
    )


def contrast_kernel(
    where, cot_ref, unit_ref, inverse_ref, vec_ref, starts_ref,
    own_ref, all_ref, ids_ref, partners_ref, ids_own_ref, partners_own_ref,
    grad_out, low_out, bias_out, gain_out, shift_out, cls_ref, y_ref,
):
    row = pl.program_id(0)
    scale = 2.0 / math.sqrt(D)

    @pl.when(row == 0)
    def _():
        everyone = all_ref[...]
        own = own_ref[...].astype(LOW)
        count = everyone.shape[0]
        scores = dot(everyone, everyone, (1, 1)) * scale
        diagonal = lax.broadcasted_iota(jnp.int32, (count, count), 0) == lax.broadcasted_iota(
            jnp.int32, (count, count), 1
        )
        scores = jnp.where(diagonal, masked_value, scores)
        highest = jnp.max(scores, axis=0, keepdims=True)
        log_all = highest + jnp.log(jnp.sum(jnp.exp(scores - highest), axis=0, keepdims=True))
        here = dot(own, everyone, (1, 1)) * scale
        ids = ids_ref[...]
        here = jnp.where(ids_own_ref[...] == ids, masked_value, here)
        top = jnp.max(here, axis=1, keepdims=True)
        log_own = top + jnp.log(jnp.sum(jnp.exp(here - top), axis=1, keepdims=True))
        out_pair = (partners_own_ref[...] == ids).astype(WIDE)
        in_pair = (ids_own_ref[...] == partners_ref[...]).astype(WIDE)
        out_grad = grid_weight * (jnp.exp(here - log_own) - out_pair)
        in_grad = grid_weight * (jnp.exp(here - log_all) - in_pair)
        cls_ref[...] = scale * (
            dot(out_grad.astype(LOW), everyone) + dot(in_grad.astype(LOW), everyone)
        )

    y_ref[...] = cot_ref[...].astype(WIDE)
    for p in range(PASS):
        y_ref[pl.ds(starts_ref[row * PASS + p], 1), :] += cls_ref[pl.ds(row * PASS + p, 1), :]
    grad = y_ref[...]
    unit = unit_ref[...]
    first = row == 0
    add_to(first, gain_out, column_sum(grad * unit))
    add_to(first, shift_out, column_sum(grad))
    back = norm_back(grad, unit, inverse_ref[...], vec_ref[:, G2 : G2 + D])
    grad_out[...] = back
    low = back.astype(LOW)
    low_out[...] = low
    add_to(first, bias_out, column_sum(low.astype(WIDE)))


def contrast(where, cotangent, unit, inverse, vectors, starts, own, everyone, ids, partners, ids_own, partners_own):
    tokens = cotangent.shape[0]
    count = everyone.shape[0]
    few = own.shape[0]
    return call(
        contrast_kernel,
        "contrast",
        (tokens // L,),
        [
            stepped(0, L, D),
            stepped(0, L, D),
            stepped(0, L, 1),
            whole(1, VEC),
            pl.BlockSpec(memory_space=pltpu.SMEM),
            whole(few, D),
            whole(count, D),
            whole(1, count),
            whole(1, count),
            whole(few, 1),
            whole(few, 1),
        ],
        [stepped(0, L, D), stepped(0, L, D), whole(1, D), whole(1, D), whole(1, D)],
        [
            array(WIDE, tokens, D),
            array(LOW, tokens, D),
            array(WIDE, 1, D),
            array(WIDE, 1, D),
            array(WIDE, 1, D),
        ],
        [pltpu.VMEM((few, D), WIDE), pltpu.VMEM((L, D), WIDE)],
        args=(where, cotangent, unit, inverse, vectors, starts, own, everyone, ids, partners, ids_own, partners_own),
    )


def down_grad_kernel(write, where, grad_ref, active_ref, out, turned):
    @pl.when(pl.program_id(0) == 0)
    def _():
        turned[...] = grad_ref[...].T

    write(out, dot(turned[...], active_ref[0]).astype(LOW), where)


def grad_of_down(where, grad_low, active, dp_size):
    blocks, tokens, _ = active.shape
    shape, block, index, write, pick = summand(blocks, dp_size)
    return call(
        partial(down_grad_kernel, write),
        "grad_of_down",
        (blocks,),
        [
            whole(tokens, D),
            pl.BlockSpec((1, tokens, D), lambda g, where: (pick(g, where), 0, 0)),
        ],
        pl.BlockSpec(block, index),
        array(LOW, *shape),
        [pltpu.VMEM((D, tokens), LOW)],
        flops=5 * 10**9,
        args=(where, grad_low, active),
    )


def up_grad_kernel(write, where, grad_ref, w_ref, slope_ref, h_ref, grad_out, bias_out, out, turned):
    @pl.when(pl.program_id(0) == 0)
    def _():
        turned[...] = h_ref[...].T

    hidden_grad = (dot(grad_ref[...], w_ref[0]) * slope_ref[0].astype(WIDE)).astype(LOW)
    grad_out[0] = hidden_grad
    bias_out[0] = column_sum(hidden_grad.astype(WIDE))
    write(out, dot(turned[...], hidden_grad).astype(LOW), where)


def grad_of_up(where, grad_low, down, slope, normed_low, dp_size):
    blocks, tokens, _ = slope.shape
    shape, block, index, write, pick = summand(blocks, dp_size)

    def at(*shape):
        return pl.BlockSpec(shape, lambda g, where: (pick(g, where), 0, 0))

    return call(
        partial(up_grad_kernel, write),
        "grad_of_up",
        (blocks,),
        [whole(tokens, D), at(1, D, D), at(1, tokens, D), whole(tokens, D)],
        [at(1, tokens, D), at(1, 1, D), pl.BlockSpec(block, index)],
        [array(LOW, blocks, tokens, D), array(WIDE, blocks, 1, D), array(LOW, *shape)],
        [pltpu.VMEM((D, tokens), LOW)],
        flops=10 * 10**9,
        args=(where, grad_low, down, slope, normed_low),
    )


def middle_kernel(
    blocks, where, hidden_ref, up_ref, sum_ref, unit_ref, inverse_ref, vec_ref, w_ref,
    grad_out, low_out, bias_out, gain_out, shift_out, context_out,
):
    first = pl.program_id(0) == 0
    width = D // blocks
    grad = sum_ref[...]
    for m in range(blocks):
        grad += dot(hidden_ref[m], up_ref[m], (1, 1))
    unit = unit_ref[...]
    add_to(first, gain_out, column_sum(grad * unit))
    add_to(first, shift_out, column_sum(grad))
    back = norm_back(grad, unit, inverse_ref[...], vec_ref[:, G1 : G1 + D])
    grad_out[...] = back
    low = back.astype(LOW)
    low_out[...] = low
    add_to(first, bias_out, column_sum(low.astype(WIDE)))
    for m in range(blocks):
        context_out[m] = dot(low, w_ref[m, :, :width]).astype(LOW)


def middle(where, hidden_grad, up, sum_grad, unit, inverse, vectors, weights):
    blocks, tokens, _ = hidden_grad.shape
    width = D // blocks
    return call(
        partial(middle_kernel, blocks),
        "middle",
        (tokens // L,),
        [
            stepped(1, blocks, L, D),
            once(blocks, D, D),
            stepped(0, L, D),
            stepped(0, L, D),
            stepped(0, L, 1),
            whole(1, VEC),
            once(blocks, D, D),
        ],
        [
            stepped(0, L, D),
            stepped(0, L, D),
            whole(1, D),
            whole(1, D),
            whole(1, D),
            stepped(1, blocks, L, width),
        ],
        [
            array(WIDE, tokens, D),
            array(LOW, tokens, D),
            array(WIDE, 1, D),
            array(WIDE, 1, D),
            array(WIDE, 1, D),
            array(LOW, blocks, tokens, width),
        ],
        flops=6 * 10**9,
        args=(where, hidden_grad, up, sum_grad, unit, inverse, vectors, weights),
    )


def attend_back_kernel(blocks, where, q_ref, k_ref, v_ref, grad_ref, out):
    heads = HEADS // blocks
    width = HD * heads

    def block(m, carry):
        out[m, :, :width] = jnp.zeros((L, width), LOW)
        for h in range(heads):
            queries, keys, value = q_ref[m * heads + h], k_ref[m * heads + h], v_ref[m * heads + h]
            grad = grad_ref[m, :, h * HD : (h + 1) * HD]
            weights = jnp.exp(dot(keys, queries, (1, 1)))
            weight_grad = dot(value, grad, (1, 1))
            middle_sum = jnp.sum(weight_grad * weights, axis=0, keepdims=True)
            score_grad = (weights * (weight_grad - middle_sum)).astype(LOW)
            at = width + h * HD
            query_grad = (dot(keys.T, score_grad)[:HD] * HD ** (-0.5)).T
            out[m, :, at : at + HD] = query_grad.astype(LOW)
            out[m, :, at + width : at + width + HD] = dot(score_grad, queries)[:, :HD].astype(LOW)
            out[m, :, at + 2 * width : at + 2 * width + HD] = dot(
                weights.astype(LOW), grad
            ).astype(LOW)
        return carry

    lax.fori_loop(0, blocks, block, 0)


def attend_back(where, queries, keys, values, context_grad):
    blocks, tokens, width = context_grad.shape
    return call(
        partial(attend_back_kernel, blocks),
        "attend_back",
        (tokens // L,),
        [
            stepped(1, HEADS, L, 2 * HD),
            stepped(1, HEADS, L, 2 * HD),
            stepped(1, HEADS, L, HD),
            stepped(1, blocks, L, width),
        ],
        stepped(1, blocks, L, D),
        array(LOW, blocks, tokens, D),
        flops=30 * 10**9,
        args=(where, queries, keys, values, context_grad),
    )


def attention_grad_kernel(write, where, x_ref, low_ref, grad_ref, context_ref, bias_out, out, x_turned, low_turned):
    @pl.when(pl.program_id(0) == 0)
    def _():
        x_turned[...] = x_ref[...].T
        low_turned[...] = low_ref[...].T

    width = context_ref.shape[2]
    grads = grad_ref[0]
    bias_out[0] = column_sum(grads.astype(WIDE))
    value = dot(x_turned[...], grads)
    own = dot(low_turned[...], context_ref[0])
    write(out, jnp.concatenate([own, value[:, width:]], axis=1).astype(LOW), where)


def grad_of_attention(where, inputs, grad_low, grads, context, dp_size):
    blocks, tokens, _ = grads.shape
    width = context.shape[2]
    shape, block, index, write, pick = summand(blocks, dp_size)

    def at(*shape):
        return pl.BlockSpec(shape, lambda g, where: (pick(g, where), 0, 0))

    return call(
        partial(attention_grad_kernel, write),
        "grad_of_attention",
        (blocks,),
        [whole(tokens, D), whole(tokens, D), at(1, tokens, D), at(1, tokens, width)],
        [at(1, 1, D), pl.BlockSpec(block, index)],
        [array(WIDE, blocks, 1, D), array(LOW, *shape)],
        [pltpu.VMEM((D, tokens), LOW)] * 2,
        flops=5 * 10**9,
        args=(where, inputs, grad_low, grads, context),
    )


def input_grad_kernel(blocks, where, grads_ref, w_ref, first_ref, out):
    total_sum = first_ref[...]
    for m in range(blocks):
        total_sum += dot(grads_ref[m], w_ref[m], (1, 1))
    out[...] = total_sum


def grad_of_input(where, grads, weights, first_grad):
    blocks, tokens, _ = grads.shape
    return call(
        partial(input_grad_kernel, blocks),
        "grad_of_input",
        (tokens // L,),
        [stepped(1, blocks, L, D), once(blocks, D, D), stepped(0, L, D)],
        stepped(0, L, D),
        array(WIDE, tokens, D),
        flops=5 * 10**9,
        args=(where, grads, weights, first_grad),
    )


def shards(
    block_input,
    cotangent,
    lengths,
    partner,
    qkv_weight,
    out_weight,
    up_weight,
    down_weight,
    qkv_first,
    out_first,
    up_first,
    down_first,
    qkv_second,
    out_second,
    up_second,
    down_second,
    vectors,
    vector_first,
    vector_second,
):
    mp_size = lax.axis_size("mp")
    dp_size = lax.axis_size("dp")
    mp_index = lax.axis_index("mp")
    dp_index = lax.axis_index("dp")
    tokens = cotangent.shape[0]
    rows = tokens // L
    own_rows = rows * PASS
    width = D // mp_size
    where = place()
    weights = gather(
        jnp.concatenate(
            [out_weight.T, qkv_weight[0], qkv_weight[1], qkv_weight[2]], axis=1
        ).astype(LOW)
    )
    up = gather(up_weight.astype(LOW))
    down = gather(down_weight.T.astype(LOW))
    local_lengths = lax.dynamic_slice_in_dim(lengths, mp_index * rows, rows, 0)
    inputs = lax.dynamic_slice_in_dim(block_input, mp_index * tokens, tokens, 0)
    segments = passage_ids(local_lengths).reshape(tokens, 1)
    starts = (jnp.cumsum(local_lengths, axis=1) - local_lengths).reshape(own_rows)
    partner_own = lax.dynamic_slice_in_dim(partner, mp_index * own_rows, own_rows, 0)
    ids_own = (dp_index * mp_size + mp_index) * own_rows + jnp.arange(own_rows, dtype=jnp.int32)
    partner_all = share(partner_own)
    ids_all = share(ids_own)
    vec = vectors.reshape(1, VEC)
    none = jnp.zeros((mp_size, width), WIDE)
    bias = jnp.concatenate(
        [none, vectors[:D].reshape(mp_size, width), none, vectors[D : 2 * D].reshape(mp_size, width)],
        axis=1,
    ).reshape(mp_size, 1, D)
    bias_up = vectors[2 * D : TAIL].reshape(mp_size, 1, D)

    queries, keys, values, context, unit_first, inverse_first, normed_low = attend(
        where, inputs, weights, bias, vec, segments
    )
    active, slope = widen(where, normed_low, up, bias_up)
    block_output, unit_second, inverse_second, cls_own = narrow(
        where, active, down, vec, unit_first, starts
    )
    cls_all = share(cls_own.astype(LOW))
    sum_grad, branch_low, down_bias_grad, gain_second_grad, shift_second_grad = contrast(
        where, cotangent, unit_second, inverse_second, vec, starts, cls_own, cls_all,
        ids_all[None, :], partner_all[None, :], ids_own[:, None], partner_own[:, None],
    )
    down_grad = scatter_sum(grad_of_down(where, branch_low, active, dp_size)).T
    hidden_grad, up_bias_grad, up_part = grad_of_up(where, branch_low, down, slope, normed_low, dp_size)
    up_grad = scatter_sum(up_part)
    first_grad, attended_low, out_bias_grad, gain_first_grad, shift_first_grad, context_grad = middle(
        where, hidden_grad, up, sum_grad, unit_first, inverse_first, vec, weights
    )
    grads = attend_back(where, queries, keys, values, context_grad)
    bias_grad, attention_part = grad_of_attention(
        where, inputs, attended_low, grads, context, dp_size
    )
    mixed = scatter_sum(attention_part)
    input_grad = grad_of_input(where, grads, weights, first_grad)
    qkv_grad = jnp.stack([mixed[:, i * width : (i + 1) * width] for i in (1, 2, 3)])
    out_grad = mixed[:, :width].T
    bias_grad = bias_grad.reshape(mp_size, D)
    vector_local = jnp.concatenate(
        [
            bias_grad[:, width : 2 * width].reshape(D),
            bias_grad[:, 3 * width :].reshape(D),
            up_bias_grad.reshape(FF),
            out_bias_grad[0],
            down_bias_grad[0],
            gain_first_grad[0],
            shift_first_grad[0],
            gain_second_grad[0],
            shift_second_grad[0],
        ]
    )
    vector_grad = total(vector_local)
    qkv_second_new, qkv_ratio = adapt(qkv_grad, qkv_first, qkv_second)
    out_second_new, out_ratio = adapt(out_grad, out_first, out_second)
    up_second_new, up_ratio = adapt(up_grad, up_first, up_second)
    down_second_new, down_ratio = adapt(down_grad, down_first, down_second)
    qkv_update = qkv_ratio + weight_decay * qkv_weight
    out_update = out_ratio + weight_decay * out_weight
    up_update = up_ratio + weight_decay * up_weight
    down_update = down_ratio + weight_decay * down_weight
    weight_squares = jnp.concatenate(
        [
            jnp.sum(qkv_weight * qkv_weight, axis=(1, 2)),
            jnp.sum(out_weight * out_weight)[None],
            jnp.sum(up_weight * up_weight)[None],
            jnp.sum(down_weight * down_weight)[None],
        ]
    )
    update_squares = jnp.concatenate(
        [
            jnp.sum(qkv_update * qkv_update, axis=(1, 2)),
            jnp.sum(out_update * out_update)[None],
            jnp.sum(up_update * up_update)[None],
            jnp.sum(down_update * down_update)[None],
        ]
    )
    weight_norms = jnp.sqrt(total(weight_squares))
    update_norms = jnp.sqrt(total(update_squares))
    trust = weight_norms / (update_norms + norm_guard)
    qkv_new = qkv_weight - rate_matrix * trust[0:3, None, None] * qkv_update
    out_new = out_weight - rate_matrix * trust[3] * out_update
    up_new = up_weight - rate_matrix * trust[4] * up_update
    down_new = down_weight - rate_matrix * trust[5] * down_update
    vector_second_new, vector_ratio = adapt(vector_grad, vector_first, vector_second)
    vector_new = vectors - rate_vector * vector_ratio
    norms = jnp.stack([weight_norms, update_norms], axis=1)
    return (
        block_output,
        input_grad,
        qkv_grad,
        out_grad,
        up_grad,
        down_grad,
        qkv_second_new,
        out_second_new,
        up_second_new,
        down_second_new,
        qkv_new,
        out_new,
        up_new,
        down_new,
        qkv_new.astype(jnp.bfloat16),
        out_new.astype(jnp.bfloat16),
        up_new.astype(jnp.bfloat16),
        down_new.astype(jnp.bfloat16),
        vector_grad,
        vector_second_new,
        vector_new,
        norms,
    )


def solution(mesh):
    in_specs = (
        P("dp", None),
        P(("dp", "mp"), None),
        P("dp", None),
        P("dp"),
        P(None, "dp", "mp"),
        P("mp", "dp"),
        P("dp", "mp"),
        P("mp", "dp"),
        P(None, "dp", "mp"),
        P("mp", "dp"),
        P("dp", "mp"),
        P("mp", "dp"),
        P(None, "dp", "mp"),
        P("mp", "dp"),
        P("dp", "mp"),
        P("mp", "dp"),
        P(),
        P(),
        P(),
    )
    out_specs = (
        P(("dp", "mp"), None),
        P(("dp", "mp"), None),
        P(None, "dp", "mp"),
        P("mp", "dp"),
        P("dp", "mp"),
        P("mp", "dp"),
        P(None, "dp", "mp"),
        P("mp", "dp"),
        P("dp", "mp"),
        P("mp", "dp"),
        P(None, "dp", "mp"),
        P("mp", "dp"),
        P("dp", "mp"),
        P("mp", "dp"),
        P(None, "dp", "mp"),
        P("mp", "dp"),
        P("dp", "mp"),
        P("mp", "dp"),
        P(),
        P(),
        P(),
        P(),
    )
    return jax.shard_map(shards, mesh=mesh, in_specs=in_specs, out_specs=out_specs, check_vma=False)
```

```python
from functools import partial
import math

import jax
import jax.numpy as jnp
from jax import lax
from jax.experimental import pallas as pl
from jax.experimental.pallas import tpu as pltpu
from jax.sharding import PartitionSpec as P

D = 768
HEADS = 12
HD = 64
FF = 3072
L = 512
PASS = 4
STEP = 10
ROWS_DEV = 8
MIB = 1 << 20
PART = 256
TAIL = 2 * D + FF


masked_value = -1e30
grid_weight = 4.0
norm_eps = 1e-12
beta_decay = 0.5
adam_eps = 1e-06
norm_guard = 1e-06
weight_decay = 0.01
rate_matrix = 1.0
rate_vector = 0.2


def passage_ids(lengths):
    starts = jnp.cumsum(lengths, axis=1) - lengths
    positions = jnp.arange(L, dtype=jnp.int32)
    return jnp.sum((positions[None, :, None] >= starts[:, None, :]).astype(jnp.int32), axis=2) - 1


AXES = ("dp", "mp")
GRID = (8, 4)


def links(move):
    pairs = []
    for z in range(4):
        for x in range(2):
            for y in range(2):
                for c in range(2):
                    tz, tx, ty, tc = move(z, x, y, c)
                    pairs.append(
                        ((z * 2 + x) * 4 + y * 2 + c, (tz % 4 * 2 + tx) * 4 + ty * 2 + tc)
                    )
    return pairs


CORE = links(lambda z, x, y, c: (z, x, y, 1 - c))
OVER_X = links(lambda z, x, y, c: (z, 1 - x, y, c))
OVER_Y = links(lambda z, x, y, c: (z, x, 1 - y, c))
OVER_XY = links(lambda z, x, y, c: (z, 1 - x, 1 - y, c))
UP_Z = [links(lambda z, x, y, c, s=s: (z + s, x, y, c)) for s in range(4)]


def after(value, *earlier):
    return lax.optimization_barrier((value, earlier))[0] if earlier else value


def send(value, pairs, *beside):
    return after(lax.ppermute(value, AXES, pairs), *beside)


def on_grid():
    return (lax.axis_size("dp"), lax.axis_size("mp")) == GRID


def place():
    dp_index = lax.axis_index("dp")
    mp_index = lax.axis_index("mp")
    return jnp.stack([dp_index // 2, dp_index % 2, mp_index // 2, mp_index % 2, mp_index])


ITEMS = (
    [(x, 0, z) for x in (0, 1) for z in (0, 1)]
    + [(0, y, z) for y in (0, 1) for z in (2, 3)]
    + [(x, 1, z) for x in (0, 1) for z in (0, 1)]
    + [(1, y, z) for y in (0, 1) for z in (2, 3)]
)


def gather_z(shard, *beside):
    return [shard] + [send(shard, UP_Z[s], *beside) for s in (1, 2, 3)]


def gather_near(parts, *beside):
    first, second = jnp.stack(parts[:2]), jnp.stack(parts[2:])
    return [
        jnp.concatenate([first, send(first, OVER_X, *beside)]),
        jnp.concatenate([second, send(second, OVER_Y, *beside)]),
    ]


def gather_far(near, *beside):
    return [send(near[0], OVER_Y, *beside), send(near[1], OVER_X, *beside)]


def gather_core(parts, *beside):
    return [send(part, CORE, *beside) for part in parts]


def gather_plain(shard):
    mp_size = lax.axis_size("mp")
    return lax.all_gather(shard, ("mp", "dp"), axis=0, tiled=True).reshape(mp_size, D, D)


def block_of(g, where):
    if not on_grid():
        return g
    return ((where[2] + g % 2) % 2) * 2 + (where[3] + g // 2) % 2


def scatter_plain(parts):
    whole = parts[0]
    return lax.psum_scatter(
        whole.reshape(-1, whole.shape[-1]), ("mp", "dp"), scatter_dimension=0, tiled=True
    )


class Summand:
    def __init__(self, blocks, dp_size):
        rows = D // dp_size
        self.groups = dp_size
        self.rows = rows
        self.blocks = blocks
        self.split = on_grid()
        if self.split:
            self.shapes = [jax.ShapeDtypeStruct((2, 2, 2, 2, rows, D), jnp.bfloat16)] * 2
        else:
            self.shapes = [jax.ShapeDtypeStruct((blocks, D, D), jnp.bfloat16)]

    def write(self, outs, value, g, where):
        if not self.split:
            outs[0][g] = value
            return
        core, y = g // 2, g % 2
        for index in range(self.groups):
            x = (index % 2 + where[1]) % 2
            z = (index // 2 + 4 - where[0]) % 4
            half = z // 2
            over_y = half == 0
            first, second = jnp.where(over_y, y, x), jnp.where(over_y, x, y)
            outs[core][half, first, second, z % 2] = value[
                index * self.rows : (index + 1) * self.rows
            ]


def share(value):
    if not on_grid():
        dp_size, mp_size = lax.axis_size("dp"), lax.axis_size("mp")
        whole = lax.all_gather(value, AXES, axis=0, tiled=True)
        own = lax.axis_index("dp") * mp_size + lax.axis_index("mp")
        return jnp.roll(whole, -own * value.shape[0], axis=0)
    value = jnp.concatenate([value, send(value, CORE)])
    value = jnp.concatenate([value] + [send(value, pairs) for pairs in (OVER_X, OVER_Y, OVER_XY)])
    return jnp.concatenate([value] + [send(value, UP_Z[s]) for s in (1, 2, 3)])


def shared_ids(own_rows):
    dp_size, mp_size = lax.axis_size("dp"), lax.axis_size("mp")
    dp_index, mp_index = lax.axis_index("dp"), lax.axis_index("mp")
    count = dp_size * mp_size * own_rows
    n = jnp.arange(count, dtype=jnp.int32)
    if not on_grid():
        return (n + (dp_index * mp_size + mp_index) * own_rows) % count
    item = n // own_rows
    core, side, up = item % 2, item // 2 % 4, item // 8
    z, x = (dp_index // 2 + 4 - up) % 4, (dp_index + side) % 2
    y, c = (mp_index // 2 + side // 2) % 2, (mp_index + core) % 2
    return ((z * 2 + x) * mp_size + y * 2 + c) * own_rows + n % own_rows


def total(value):
    if not on_grid():
        return lax.psum(value, AXES)
    value = value + send(value, CORE)
    value = value + sum(send(value, pairs) for pairs in (OVER_X, OVER_Y, OVER_XY))
    return value + sum(send(value, UP_Z[s]) for s in (1, 2, 3))


LOW = jnp.bfloat16
WIDE = jnp.float32
B1, BO, B2, G1, C1, G2, C2 = 2 * D, TAIL, TAIL + D, TAIL + 2 * D, TAIL + 3 * D, TAIL + 4 * D, TAIL + 5 * D
VEC = 8 * D + FF


def dot(left, right, over=(1, 0)):
    return lax.dot_general(
        left, right, (((over[0],), (over[1],)), ((), ())), preferred_element_type=WIDE
    )


def call(kernel, name, where, operands, outs, scratch=(), limit=24, wait_for=()):
    count = len(operands)
    many = len(outs)

    def body(where, *refs):
        results = refs[count + len(wait_for) :]
        results[many][...] = jnp.zeros((8, 128), WIDE)
        kernel(where, *refs[:count], *results[:many], *results[many + 1 :])

    def spec(operand):
        integers = operand.dtype == jnp.int32 and operand.ndim == 1
        return pl.BlockSpec(memory_space=pltpu.SMEM if integers else pltpu.VMEM)

    return pl.pallas_call(
        body,
        in_specs=[pl.BlockSpec(memory_space=pltpu.SMEM)]
        + [spec(operand) for operand in operands]
        + [pl.BlockSpec(memory_space=pl.ANY)] * len(wait_for),
        out_specs=[pl.BlockSpec(memory_space=pltpu.VMEM)] * (many + 1),
        out_shape=list(outs) + [array(WIDE, 8, 128)],
        scratch_shapes=list(scratch),
        compiler_params=pltpu.CompilerParams(vmem_limit_bytes=limit * MIB),
        cost_estimate=pl.CostEstimate(flops=3 * 10**10, bytes_accessed=MIB, transcendentals=0),
        name=name,
    )(where, *operands, *wait_for)


def array(dtype, *shape):
    return jax.ShapeDtypeStruct(shape, dtype)


def normalize(value):
    center = jnp.mean(value, axis=1, keepdims=True)
    offsets = value - center
    inverse = lax.rsqrt(jnp.mean(offsets * offsets, axis=1, keepdims=True) + norm_eps)
    return offsets * inverse, inverse


def norm_back(grad, unit, inverse, gain):
    scaled = grad * gain
    return inverse * (
        scaled
        - jnp.mean(scaled, axis=1, keepdims=True)
        - unit * jnp.mean(scaled * unit, axis=1, keepdims=True)
    )


def column_sum(value):
    return jnp.sum(value, axis=0, keepdims=True)


def settle_kernel(where, *refs):
    pieces, out = refs[:8], refs[8]
    for core in range(2):
        for item, (x, y, z) in enumerate(ITEMS):
            block = (where[2] + y) % 2 * 2 + (where[3] + core) % 2
            row = (where[0] + 4 - z) % 4 * 2 + (where[1] + x) % 2
            out[block, row] = pieces[core * 4 + item // 4][item % 4]


def settle(where, pieces):
    rows = pieces[0].shape[1]
    whole = call(settle_kernel, "settle", where, pieces, [array(LOW, 4, 8, rows, D)], limit=8)[0]
    return whole.reshape(4, D, D)


def add_kernel(plan, where, *refs):
    count = max(max(pair[0], pair[2]) for pair in plan) + 1
    for out, (left, left_at, right, right_at) in zip(refs[count:], plan):
        out[...] = (
            refs[left][left_at].astype(WIDE) + refs[right][right_at].astype(WIDE)
        ).astype(LOW)


def add(where, operands, plan):
    outs = []
    for left, left_at, _, _ in plan:
        outs.append(array(LOW, *operands[left].shape[len(left_at) :]))
    return call(partial(add_kernel, plan), "add", where, operands, outs, limit=8)


def scatter_core(where, parts, *beside):
    arrived = send(parts[1], CORE, *beside)
    plan = [(0, (half, near), 1, (half, near)) for half in (0, 1) for near in (0, 1)]
    return add(where, [parts[0], arrived], plan)


def scatter_far(where, sums, *beside):
    arrived = [send(sums[1], OVER_Y, *beside), send(sums[3], OVER_X, *beside)]
    plan = [(half, (far,), half + 2, (far,)) for half in (0, 1) for far in (0, 1)]
    return add(where, [sums[0], sums[2], *arrived], plan)


def scatter_near(where, sums, *beside):
    arrived = [send(sums[1], OVER_X, *beside), send(sums[3], OVER_Y, *beside)]
    plan = [(half, (z,), half + 2, (z,)) for half in (0, 1) for z in (0, 1)]
    return add(where, [sums[0], sums[2], *arrived], plan)


def scatter_z(sums, *beside):
    return [sums[0]] + [send(sums[s], UP_Z[s], *beside) for s in (1, 2, 3)]


def attend_kernel(blocks, where, x_ref, w_ref, bias_ref, vec_ref, seg_ref, *refs):
    q_out, k_out, v_out, context_out, unit_out, inverse_out, low_out, sum_ref = refs
    heads = HEADS // blocks
    width = HD * heads
    x = x_ref[...]
    lanes = lax.broadcasted_iota(jnp.int32, (L, 2 * HD), 1)
    passage = jnp.broadcast_to(seg_ref[...], (L, 2 * HD)) + HD
    is_passage = (lanes >= HD) & (lanes < HD + PASS)
    q_tail = jnp.where(is_passage & (lanes != passage), masked_value, 0.0)
    k_tail = (lanes == passage) | ((lanes >= HD + PASS) & (lanes < HD + PASS + 3))
    k_tail = jnp.where(k_tail, 1.0, 0.0).astype(LOW)
    k_scale = jnp.where(lanes < HD, 1.0, 0.0).astype(LOW)
    q_scale = jnp.where(lanes < HD, HD ** (-0.5), 0.0).astype(LOW)
    q_tail = q_tail.astype(LOW)
    sum_ref[...] = x.astype(WIDE) + vec_ref[:, BO : BO + D]

    def block(m, carry):
        projected = (dot(x, w_ref[m]) + bias_ref[m]).astype(LOW)
        parts = []
        for h in range(heads):
            at = width + h * HD
            query = projected[:, at : at + 2 * HD] * q_scale + q_tail
            keys = projected[:, at + width : at + width + 2 * HD] * k_scale + k_tail
            value = projected[:, at + 2 * width : at + 2 * width + HD]
            scores = dot(keys, query, (1, 1))
            highest = jnp.max(scores, axis=0, keepdims=True)
            weights = jnp.exp(scores - highest)
            totals = jnp.sum(weights, axis=0, keepdims=True)
            mixed = dot(value.T, weights.astype(LOW)) * (1.0 / totals)
            left = -(highest + jnp.log(totals))
            high = left.astype(LOW).astype(WIDE)
            middle = (left - high).astype(LOW).astype(WIDE)
            rows = lax.broadcasted_iota(jnp.int32, (HD, L), 0)
            split = jnp.where(rows == PASS, high, 0.0)
            split = jnp.where(rows == PASS + 1, middle, split)
            split = jnp.where(rows == PASS + 2, left - high - middle, split)
            turned = jnp.concatenate([mixed, split], axis=0).T.astype(LOW)
            parts.append(turned[:, :HD])
            q_out[m * heads + h] = jnp.where(lanes < HD, query, query + turned)
            k_out[m * heads + h] = keys
            v_out[m * heads + h] = value
        context = jnp.concatenate(parts, axis=1)
        context_out[m] = context
        sum_ref[...] += dot(context, w_ref[m, :, :width], (1, 1))
        return carry

    lax.fori_loop(0, blocks, block, 0)
    unit, inverse = normalize(sum_ref[...])
    unit_out[...] = unit
    inverse_out[...] = inverse
    low_out[...] = (unit * vec_ref[:, G1 : G1 + D] + vec_ref[:, C1 : C1 + D]).astype(LOW)


def attend(where, inputs, weight, bias, vectors, segments, wait_for=()):
    blocks = bias.shape[0]
    return call(
        partial(attend_kernel, blocks),
        "attend",
        where,
        [inputs, weight, bias, vectors, segments],
        [
            array(LOW, HEADS, L, 2 * HD),
            array(LOW, HEADS, L, 2 * HD),
            array(LOW, HEADS, L, HD),
            array(LOW, blocks, L, D // blocks),
            array(WIDE, L, D),
            array(WIDE, L, 1),
            array(LOW, L, D),
        ],
        [pltpu.VMEM((L, D), WIDE)],
        wait_for=wait_for,
    )


def widen_kernel(rows, where, *refs):
    lows, (w_ref, bias_ref, active_out, slope_out) = refs[:rows], refs[rows:]

    def block(m, carry):
        for row in range(rows):
            hidden = dot(lows[row][...], w_ref[m]) + bias_ref[m]
            half = 0.5 * (1.0 + lax.erf(hidden * math.sqrt(0.5)))
            active_out[m, row * L : (row + 1) * L] = (hidden * half).astype(LOW)
            density = jnp.exp(-0.5 * hidden * hidden) * (1.0 / math.sqrt(2.0 * math.pi))
            slope_out[m, row * L : (row + 1) * L] = (half + hidden * density).astype(LOW)
        return carry

    lax.fori_loop(0, w_ref.shape[0], block, 0)


def widen(where, lows, weight, bias, wait_for=()):
    blocks = bias.shape[0]
    rows = len(lows)
    return call(
        partial(widen_kernel, rows),
        "widen",
        where,
        [*lows, weight, bias],
        [array(LOW, blocks, rows * L, D)] * 2,
        wait_for=wait_for,
    )


def narrow_kernel(rows, where, active_ref, w_ref, vec_ref, starts_ref, *refs):
    units, (out, unit_out, inverse_out, cls_out, y_ref) = refs[:rows], refs[rows:]
    for row in range(rows):
        at = slice(row * L, (row + 1) * L)
        y_ref[at] = units[row][...] * vec_ref[:, G1 : G1 + D] + (
            vec_ref[:, C1 : C1 + D] + vec_ref[:, B2 : B2 + D]
        )

        def block(m, carry):
            y_ref[at] += dot(active_ref[m, at], w_ref[m], (1, 1))
            return carry

        lax.fori_loop(0, w_ref.shape[0], block, 0)
        unit, inverse = normalize(y_ref[at])
        unit_out[at] = unit
        inverse_out[at] = inverse
        output = unit * vec_ref[:, G2 : G2 + D] + vec_ref[:, C2 : C2 + D]
        out[at] = output.astype(LOW)
        y_ref[at] = output
    for p in range(cls_out.shape[0]):
        cls_out[p : p + 1, :] = y_ref[pl.ds(starts_ref[p], 1), :]


def narrow(where, active, weight, vectors, starts, units):
    tokens = active.shape[1]
    few = starts.shape[0]
    return call(
        partial(narrow_kernel, len(units)),
        "narrow",
        where,
        [active, weight, vectors, starts, *units],
        [
            array(LOW, tokens, D),
            array(WIDE, tokens, D),
            array(WIDE, tokens, 1),
            array(WIDE, few, D),
        ],
        [pltpu.VMEM((tokens, D), WIDE)],
    )


def contrast_kernel(
    where, cot_ref, unit_ref, inverse_ref, vec_ref, starts_ref,
    own_ref, all_ref, ids_ref, ids_own_ref, partners_own_ref,
    grad_out, low_out, bias_out, gain_out, shift_out, y_ref,
):
    scale = 2.0 / math.sqrt(D)
    everyone = all_ref[...]
    own = own_ref[...].astype(LOW)
    count = everyone.shape[0]
    scores = dot(everyone, everyone, (1, 1)) * scale
    diagonal = lax.broadcasted_iota(jnp.int32, (count, count), 0) == lax.broadcasted_iota(
        jnp.int32, (count, count), 1
    )
    scores = jnp.where(diagonal, masked_value, scores)
    highest = jnp.max(scores, axis=0, keepdims=True)
    log_all = highest + jnp.log(jnp.sum(jnp.exp(scores - highest), axis=0, keepdims=True))
    here = dot(own, everyone, (1, 1)) * scale
    ids = ids_ref[...]
    here = jnp.where(ids_own_ref[...] == ids, masked_value, here)
    top = jnp.max(here, axis=1, keepdims=True)
    log_own = top + jnp.log(jnp.sum(jnp.exp(here - top), axis=1, keepdims=True))
    pair = (partners_own_ref[...] == ids).astype(WIDE)
    out_grad = grid_weight * (jnp.exp(here - log_own) - pair)
    in_grad = grid_weight * (jnp.exp(here - log_all) - pair)
    cls_grad = scale * (dot(out_grad.astype(LOW), everyone) + dot(in_grad.astype(LOW), everyone))
    y_ref[...] = cot_ref[...].astype(WIDE)
    for p in range(cls_grad.shape[0]):
        y_ref[pl.ds(starts_ref[p], 1), :] += cls_grad[p : p + 1]
    for ref in (bias_out, gain_out, shift_out):
        ref[...] = jnp.zeros_like(ref)
    for part in range(y_ref.shape[0] // PART):
        at = slice(part * PART, (part + 1) * PART)
        grad = y_ref[at]
        unit = unit_ref[at]
        gain_out[...] += column_sum(grad * unit)
        shift_out[...] += column_sum(grad)
        back = norm_back(grad, unit, inverse_ref[at], vec_ref[:, G2 : G2 + D])
        grad_out[at] = back
        low = back.astype(LOW)
        low_out[at] = low
        bias_out[...] += column_sum(low.astype(WIDE))


def contrast(where, cotangent, unit, inverse, vectors, starts, own, everyone, ids, ids_own, partners_own):
    tokens = cotangent.shape[0]
    return call(
        contrast_kernel,
        "contrast",
        where,
        [
            cotangent, unit, inverse, vectors, starts, own, everyone, ids, ids_own, partners_own,
        ],
        [
            array(WIDE, tokens, D),
            array(LOW, tokens, D),
            array(WIDE, 1, D),
            array(WIDE, 1, D),
            array(WIDE, 1, D),
        ],
        [pltpu.VMEM((tokens, D), WIDE)],
    )


def down_grad_kernel(summand, where, grad_ref, active_ref, *refs):
    outs, turned = refs[:-1], refs[-1]
    turned[...] = grad_ref[...].T
    for g in range(summand.blocks):
        value = dot(turned[...], active_ref[block_of(g, where)]).astype(LOW)
        summand.write(outs, value, g, where)


def grad_of_down(where, grad_low, active, summand):
    tokens = active.shape[1]
    return call(
        partial(down_grad_kernel, summand),
        "grad_of_down",
        where,
        [grad_low, active],
        summand.shapes,
        [pltpu.VMEM((D, tokens), LOW)],
    )


def up_grad_kernel(summand, rows, where, grad_ref, w_ref, slope_ref, *refs):
    lows, (grad_out, bias_out), refs = refs[:rows], refs[rows : rows + 2], refs[rows + 2 :]
    outs, turned = refs[:-1], refs[-1]
    for row in range(rows):
        turned[:, row * L : (row + 1) * L] = lows[row][...].T
    for g in range(summand.blocks):
        m = block_of(g, where)
        bias = jnp.zeros((1, D), WIDE)
        for row in range(rows):
            at = slice(row * L, (row + 1) * L)
            grad = dot(grad_ref[at], w_ref[m]) * slope_ref[m, at].astype(WIDE)
            grad = grad.astype(LOW)
            grad_out[m, at] = grad
            bias += column_sum(grad.astype(WIDE))
        bias_out[m] = bias
        summand.write(outs, dot(turned[...], grad_out[m]).astype(LOW), g, where)


def grad_of_up(where, grad_low, weight, slope, lows, summand, wait_for=()):
    blocks, tokens, _ = slope.shape
    return call(
        partial(up_grad_kernel, summand, len(lows)),
        "grad_of_up",
        where,
        [grad_low, weight, slope, *lows],
        [array(LOW, blocks, tokens, D), array(WIDE, blocks, 1, D)] + summand.shapes,
        [pltpu.VMEM((D, tokens), LOW)],
        wait_for=wait_for,
    )


def middle_kernel(blocks, rows, where, hidden_ref, up_ref, sum_ref, vec_ref, w_ref, *refs):
    units, inverses, refs = refs[:rows], refs[rows : 2 * rows], refs[2 * rows :]
    grad_out, low_out, bias_out, gain_out, shift_out, context_out = refs
    width = D // blocks
    for ref in (bias_out, gain_out, shift_out):
        ref[...] = jnp.zeros_like(ref)
    for row in range(rows):
        at = slice(row * L, (row + 1) * L)
        grad_out[at] = sum_ref[at]

        def block(m, carry):
            grad_out[at] += dot(hidden_ref[m, at], up_ref[m], (1, 1))
            return carry

        lax.fori_loop(0, blocks, block, 0)
        for part in range(L // PART):
            inner = slice(part * PART, (part + 1) * PART)
            outer = slice(row * L + part * PART, row * L + (part + 1) * PART)
            grad = grad_out[outer]
            unit = units[row][inner]
            gain_out[...] += column_sum(grad * unit)
            shift_out[...] += column_sum(grad)
            back = norm_back(grad, unit, inverses[row][inner], vec_ref[:, G1 : G1 + D])
            grad_out[outer] = back
            low = back.astype(LOW)
            low_out[outer] = low
            bias_out[...] += column_sum(low.astype(WIDE))
        for m in range(blocks):
            context_out[row * blocks + m] = dot(low_out[at], w_ref[m, :, :width]).astype(LOW)


def middle(where, hidden_grad, up, sum_grad, units, inverses, vectors, weight, wait_for=()):
    blocks, tokens, _ = hidden_grad.shape
    rows = len(units)
    return call(
        partial(middle_kernel, blocks, rows),
        "middle",
        where,
        [hidden_grad, up, sum_grad, vectors, weight, *units, *inverses],
        [
            array(WIDE, tokens, D),
            array(LOW, tokens, D),
            array(WIDE, 1, D),
            array(WIDE, 1, D),
            array(WIDE, 1, D),
            array(LOW, rows * blocks, L, D // blocks),
        ],
        wait_for=wait_for,
    )


def attend_back_kernel(blocks, row, where, q_ref, k_ref, v_ref, grad_ref, out):
    heads = HEADS // blocks
    width = HD * heads

    def block(m, carry):
        out[m, :, :width] = jnp.zeros((L, width), LOW)
        for h in range(heads):
            queries, keys, value = q_ref[m * heads + h], k_ref[m * heads + h], v_ref[m * heads + h]
            grad = grad_ref[row * blocks + m, :, h * HD : (h + 1) * HD]
            weights = jnp.exp(dot(keys, queries, (1, 1)))
            weight_grad = dot(value, grad, (1, 1))
            middle_sum = jnp.sum(weight_grad * weights, axis=0, keepdims=True)
            score_grad = (weights * (weight_grad - middle_sum)).astype(LOW)
            at = width + h * HD
            query_grad = (dot(keys.T, score_grad)[:HD] * HD ** (-0.5)).T
            out[m, :, at : at + HD] = query_grad.astype(LOW)
            out[m, :, at + width : at + width + HD] = dot(score_grad, queries)[:, :HD].astype(LOW)
            out[m, :, at + 2 * width : at + 2 * width + HD] = dot(
                weights.astype(LOW), grad
            ).astype(LOW)
        return carry

    lax.fori_loop(0, blocks, block, 0)


def attend_back(where, row, blocks, queries, keys, values, context_grad, wait_for=()):
    return call(
        partial(attend_back_kernel, blocks, row),
        "attend_back",
        where,
        [queries, keys, values, context_grad],
        [array(LOW, blocks, L, D)],
        wait_for=wait_for,
    )


def attention_grad_kernel(summand, rows, where, x_ref, low_ref, *refs):
    grads, contexts, refs = refs[:rows], refs[rows : 2 * rows], refs[2 * rows :]
    bias_out, outs, (x_turned, low_turned) = refs[0], refs[1:-2], refs[-2:]
    x_turned[...] = x_ref[...].T
    low_turned[...] = low_ref[...].T
    width = contexts[0].shape[2]
    for g in range(summand.blocks):
        m = block_of(g, where)
        bias = jnp.zeros((1, D), WIDE)
        value = jnp.zeros((D, D), WIDE)
        own = jnp.zeros((D, width), WIDE)
        for row in range(rows):
            at = slice(row * L, (row + 1) * L)
            grad = grads[row][m]
            bias += column_sum(grad.astype(WIDE))
            value += dot(x_turned[:, at], grad)
            own += dot(low_turned[:, at], contexts[row][m])
        bias_out[m] = bias
        value = jnp.concatenate([own, value[:, width:]], axis=1).astype(LOW)
        summand.write(outs, value, g, where)


def grad_of_attention(where, inputs, grad_low, grads, contexts, summand, wait_for=()):
    tokens = inputs.shape[0]
    return call(
        partial(attention_grad_kernel, summand, len(grads)),
        "grad_of_attention",
        where,
        [inputs, grad_low, *grads, *contexts],
        [array(WIDE, summand.blocks, 1, D)] + summand.shapes,
        [pltpu.VMEM((D, tokens), LOW)] * 2,
        wait_for=wait_for,
    )


def input_grad_kernel(rows, where, w_ref, first_ref, *refs):
    grads, out = refs[:rows], refs[rows]
    for row in range(rows):
        at = slice(row * L, (row + 1) * L)
        out[at] = first_ref[at]

        def block(m, carry):
            out[at] += dot(grads[row][m], w_ref[m], (1, 1))
            return carry

        lax.fori_loop(0, w_ref.shape[0], block, 0)


def grad_of_input(where, grads, weight, first_grad, wait_for=()):
    return call(
        partial(input_grad_kernel, len(grads)),
        "grad_of_input",
        where,
        [weight, first_grad, *grads],
        [array(WIDE, *first_grad.shape)],
        wait_for=wait_for,
    )


def pack_kernel(where, bias_ref, up_ref, *refs):
    out = refs[-1]
    blocks = bias_ref.shape[0]
    width = D // blocks
    rows = [bias_ref[m] for m in range(blocks)]
    out[:, :D] = jnp.concatenate([row[:, width : 2 * width] for row in rows], axis=1)
    out[:, D : 2 * D] = jnp.concatenate([row[:, 3 * width :] for row in rows], axis=1)
    units = FF // blocks
    for m in range(blocks):
        out[:, 2 * D + m * units : 2 * D + (m + 1) * units] = up_ref[m]
    for i, ref in enumerate(refs[:-1]):
        out[:, TAIL + i * D : TAIL + (i + 1) * D] = ref[...]


def pack(where, bias_grad, up_bias_grad, *others):
    return call(
        pack_kernel, "pack", where, [bias_grad, up_bias_grad, *others], [array(WIDE, 1, VEC)], limit=8
    )[0]


def ratio_of(grad, first, second):
    moment = beta_decay * first + (1.0 - beta_decay) * grad
    second_new = beta_decay * second + (1.0 - beta_decay) * grad * grad
    ratio = (
        moment
        / (1.0 - beta_decay**STEP)
        / (jnp.sqrt(second_new / (1.0 - beta_decay**STEP)) + adam_eps)
    )
    return second_new, ratio


def squares(value):
    return jnp.sum(jnp.sum(value * value, axis=0, keepdims=True), axis=1, keepdims=True)


def adapt_kernel(cut, parts, where, *refs):
    total_sum = refs[0][...].astype(WIDE)
    for ref in refs[1:parts]:
        total_sum += ref[...].astype(WIDE)
    refs = refs[parts:]
    count = len(cut)
    firsts, seconds, weights = refs[:count], refs[count : 2 * count], refs[2 * count : 3 * count]
    outs = refs[3 * count :]
    lines = []
    for i, pick in enumerate(cut):
        for part, grad in pick(total_sum):
            def at(ref):
                return ref if part is None else ref.at[part]

            second_new, ratio = ratio_of(grad, at(firsts[i])[...], at(seconds[i])[...])
            weight = at(weights[i])[...]
            update = ratio + weight_decay * weight
            at(outs[3 * i])[...] = grad
            at(outs[3 * i + 1])[...] = second_new
            at(outs[3 * i + 2])[...] = update
            lines.append((squares(weight), squares(update)))
    lanes = lax.broadcasted_iota(jnp.int32, (1, 128), 1)
    held = jnp.zeros((1, 128), WIDE)
    for i, (weight_square, update_square) in enumerate(lines):
        held = jnp.where(lanes == 2 * i, weight_square, held)
        held = jnp.where(lanes == 2 * i + 1, update_square, held)
    outs[-1][...] = held


def adapt(name, where, parts, cut, firsts, seconds, weights):
    outs = [array(WIDE, *w.shape) for w in weights for _ in range(3)] + [array(WIDE, 1, 128)]
    operands = [*parts, *firsts, *seconds, *weights]
    return call(
        partial(adapt_kernel, cut, len(parts)),
        name,
        where,
        operands,
        outs,
    )[:-1]


def renew_kernel(counts, where, sums_ref, grad_ref, first_ref, second_ref, vec_ref, *refs):
    many = len(counts)
    weights, updates, outs = refs[:many], refs[many : 2 * many], refs[2 * many :]
    norms = jnp.sqrt(sums_ref[...])
    outs[-1][...] = norms
    slot = 0
    for i, count in enumerate(counts):
        for part in range(count):
            trust = norms[:, 2 * slot : 2 * slot + 1] / (
                norms[:, 2 * slot + 1 : 2 * slot + 2] + norm_guard
            )
            slot += 1

            def at(ref):
                return ref if count == 1 else ref.at[part]

            new = at(weights[i])[...] - rate_matrix * trust * at(updates[i])[...]
            at(outs[2 * i])[...] = new
            at(outs[2 * i + 1])[...] = new.astype(LOW)
    second_new, ratio = ratio_of(grad_ref[...], first_ref[...], second_ref[...])
    outs[-3][...] = second_new
    outs[-2][...] = vec_ref[...] - rate_vector * ratio


def renew(where, sums, vector_grad, vector_first, vector_second, vectors, weights, updates):
    counts = [3 if w.ndim == 3 else 1 for w in weights]
    outs = [array(dtype, *w.shape) for w in weights for dtype in (WIDE, LOW)]
    outs += [array(WIDE, 1, VEC), array(WIDE, 1, VEC), array(WIDE, 1, 128)]
    operands = [sums, vector_grad, vector_first, vector_second, vectors, *weights, *updates]
    return call(
        partial(renew_kernel, counts),
        "renew",
        where,
        operands,
        outs,
    )[:-1]


def shards(
    block_input,
    cotangent,
    lengths,
    partner,
    qkv_weight,
    out_weight,
    up_weight,
    down_weight,
    qkv_first,
    out_first,
    up_first,
    down_first,
    qkv_second,
    out_second,
    up_second,
    down_second,
    vectors,
    vector_first,
    vector_second,
):
    mp_size = lax.axis_size("mp")
    dp_size = lax.axis_size("dp")
    mp_index = lax.axis_index("mp")
    dp_index = lax.axis_index("dp")
    tokens = cotangent.shape[0]
    rows = tokens // L
    own_rows = rows * PASS
    width = D // mp_size
    where = place()
    weight_shard = jnp.concatenate(
        [out_weight.T, qkv_weight[0], qkv_weight[1], qkv_weight[2]], axis=1
    ).astype(LOW)
    up_shard = up_weight.astype(LOW)
    down_shard = down_weight.T.astype(LOW)
    local_lengths = lax.dynamic_slice_in_dim(lengths, mp_index * rows, rows, 0)
    inputs = lax.dynamic_slice_in_dim(block_input, mp_index * tokens, tokens, 0)
    segments = passage_ids(local_lengths).reshape(tokens, 1)
    starts = jnp.cumsum(local_lengths, axis=1) - local_lengths
    starts = (starts + L * jnp.arange(rows, dtype=jnp.int32)[:, None]).reshape(own_rows)
    partner_own = lax.dynamic_slice_in_dim(partner, mp_index * own_rows, own_rows, 0)
    ids_own = (dp_index * mp_size + mp_index) * own_rows + jnp.arange(own_rows, dtype=jnp.int32)
    ids_all = shared_ids(own_rows)
    vec = vectors.reshape(1, VEC)
    none = jnp.zeros((mp_size, width), WIDE)
    bias = jnp.concatenate(
        [none, vectors[:D].reshape(mp_size, width), none, vectors[D : 2 * D].reshape(mp_size, width)],
        axis=1,
    ).reshape(mp_size, 1, D)
    bias_up = vectors[2 * D : TAIL].reshape(mp_size, 1, D)

    summand = Summand(mp_size, dp_size)

    def attend_row(row, weight, *wait_for):
        at = slice(row * L, (row + 1) * L)
        return attend(where, inputs[at], weight, bias, vec, segments[at], wait_for=wait_for)

    if on_grid():
        weight_z = gather_z(weight_shard)
        weight_near = gather_near(weight_z)
        up_z = gather_z(after(up_shard, *weight_z))
        weight_far = gather_far(weight_near)
        weight_parts = weight_near + weight_far
        weight = settle(where, weight_parts + gather_core(weight_parts))
        up_z = after(up_z, *weight_far)
        kept = [attend_row(0, weight, *up_z)]
        up_near = gather_near(up_z, kept[0][-1])
        down_z = gather_z(after(down_shard, *up_z), kept[0][-1])
        kept.append(attend_row(1, weight, *up_near, *down_z))
        up_far = gather_far(up_near, kept[1][-1])
        up_parts = up_near + up_far
        up = settle(where, up_parts + gather_core(up_parts))
        down_near = gather_near(down_z, kept[1][-1])
    else:
        weight = gather_plain(weight_shard)
        up = gather_plain(up_shard)
        down_near = []
        kept = [attend_row(row, weight) for row in range(rows)]
    queries, keys, values, contexts, units_first, inverses_first, lows, _ = zip(*kept)
    active, slope, widened = widen(where, lows, up, bias_up, wait_for=down_near)
    if on_grid():
        down_far = gather_far(after(down_near, *up_far), widened)
        down_parts = down_near + down_far
        down = settle(where, down_parts + gather_core(down_near, widened) + gather_core(down_far))
    else:
        down = gather_plain(down_shard)
    block_output, unit_second, inverse_second, cls_own, _ = narrow(
        where, active, down, vec, starts, units_first
    )
    cls_all = share(cls_own.astype(LOW))
    sum_grad, branch_low, down_bias_grad, gain_second_grad, shift_second_grad, _ = contrast(
        where, cotangent, unit_second, inverse_second, vec, starts, cls_own, cls_all,
        ids_all[None, :], ids_own[:, None], partner_own[:, None],
    )
    *down_part, ended = grad_of_down(where, branch_low, active, summand)
    hidden_grad, up_bias_grad, *up_part, _ = grad_of_up(
        where, branch_low, down, slope, lows, summand, wait_for=(ended,)
    )
    if on_grid():
        *down_sum, added = scatter_core(where, down_part)
    (
        first_grad, attended_low, out_bias_grad, gain_first_grad, shift_first_grad, context_grad, _,
    ) = middle(
        where, hidden_grad, up, sum_grad, units_first, inverses_first, vec, weight,
        wait_for=(added,) if on_grid() else (),
    )

    def back_row(row, *wait_for):
        return attend_back(
            where, row, mp_size, queries[row], keys[row], values[row], context_grad, wait_for=wait_for
        )

    if on_grid():
        *down_sum, down_added = scatter_far(where, down_sum)
        *up_sum, up_added = scatter_core(where, up_part)
        first_row, ended = back_row(0, down_added, up_added)
        *down_sum, down_added = scatter_near(where, down_sum, ended)
        second_row, ended = back_row(1, down_added)
        *up_sum, up_added = scatter_far(where, up_sum, ended)
        grads = [first_row, second_row]
        ties = (up_added,)
    else:
        grads = [back_row(row)[0] for row in range(rows)]
        ties = ()
    bias_grad, *attention_part, ended = grad_of_attention(
        where, inputs, attended_low, grads, contexts, summand, wait_for=ties
    )
    if on_grid():
        down_parts = scatter_z(down_sum, ended)
        *up_sum, up_added = scatter_near(where, up_sum, ended)
        *attention_sum, added = scatter_core(where, attention_part)
        input_grad, ended = grad_of_input(
            where, grads, weight, first_grad, wait_for=(added, up_added)
        )
        up_parts = scatter_z(up_sum, ended)
        *attention_sum, _ = scatter_far(where, attention_sum, ended)
        *attention_sum, _ = scatter_near(where, attention_sum)
        attention_parts = scatter_z(attention_sum)
    else:
        down_parts = [scatter_plain(down_part)]
        up_parts = [scatter_plain(up_part)]
        attention_parts = [scatter_plain(attention_part)]
        input_grad, _ = grad_of_input(where, grads, weight, first_grad)
    vector_local = pack(
        where,
        bias_grad,
        up_bias_grad,
        out_bias_grad,
        down_bias_grad,
        gain_first_grad,
        shift_first_grad,
        gain_second_grad,
        shift_second_grad,
    )
    down_grad, down_second_new, down_update, down_squares = adapt(
        "adapt_down", where, down_parts, [lambda g: [(None, g.T)]],
        [down_first], [down_second], [down_weight],
    )
    up_grad, up_second_new, up_update, up_squares = adapt(
        "adapt_up", where, up_parts, [lambda g: [(None, g)]], [up_first], [up_second], [up_weight]
    )
    (
        qkv_grad, qkv_second_new, qkv_update,
        out_grad, out_second_new, out_update, attention_squares,
    ) = adapt(
        "adapt_attention",
        where,
        attention_parts,
        [
            lambda g: [(i, g[:, (i + 1) * width : (i + 2) * width]) for i in range(3)],
            lambda g: [(None, g[:, :width].T)],
        ],
        [qkv_first, out_first],
        [qkv_second, out_second],
        [qkv_weight, out_weight],
    )
    summed = total(
        jnp.concatenate(
            [
                vector_local,
                attention_squares[:, :8],
                up_squares[:, :2],
                down_squares[:, :2],
                jnp.zeros((1, 116), WIDE),
            ],
            axis=1,
        )
    )
    vector_grad, sums = summed[:, :VEC], summed[:, VEC:]
    weights = [qkv_weight, out_weight, up_weight, down_weight]
    updates = [qkv_update, out_update, up_update, down_update]
    (
        qkv_new, qkv_copy, out_new, out_copy, up_new, up_copy, down_new, down_copy,
        vector_second_new, vector_new, norms,
    ) = renew(
        where, sums, vector_grad, vector_first.reshape(1, VEC), vector_second.reshape(1, VEC), vec,
        weights, updates,
    )
    return (
        block_output,
        input_grad,
        qkv_grad,
        out_grad,
        up_grad,
        down_grad,
        qkv_second_new,
        out_second_new,
        up_second_new,
        down_second_new,
        qkv_new,
        out_new,
        up_new,
        down_new,
        qkv_copy,
        out_copy,
        up_copy,
        down_copy,
        vector_grad.reshape(VEC),
        vector_second_new.reshape(VEC),
        vector_new.reshape(VEC),
        norms[0, :12].reshape(6, 2),
    )


def solution(mesh):
    in_specs = (
        P("dp", None),
        P(("dp", "mp"), None),
        P("dp", None),
        P("dp"),
        P(None, "dp", "mp"),
        P("mp", "dp"),
        P("dp", "mp"),
        P("mp", "dp"),
        P(None, "dp", "mp"),
        P("mp", "dp"),
        P("dp", "mp"),
        P("mp", "dp"),
        P(None, "dp", "mp"),
        P("mp", "dp"),
        P("dp", "mp"),
        P("mp", "dp"),
        P(),
        P(),
        P(),
    )
    out_specs = (
        P(("dp", "mp"), None),
        P(("dp", "mp"), None),
        P(None, "dp", "mp"),
        P("mp", "dp"),
        P("dp", "mp"),
        P("mp", "dp"),
        P(None, "dp", "mp"),
        P("mp", "dp"),
        P("dp", "mp"),
        P("mp", "dp"),
        P(None, "dp", "mp"),
        P("mp", "dp"),
        P("dp", "mp"),
        P("mp", "dp"),
        P(None, "dp", "mp"),
        P("mp", "dp"),
        P("dp", "mp"),
        P("mp", "dp"),
        P(),
        P(),
        P(),
        P(),
    )
    return jax.shard_map(shards, mesh=mesh, in_specs=in_specs, out_specs=out_specs, check_vma=False)
```

```python
from functools import partial
import math

import jax
import jax.numpy as jnp
from jax import lax
from jax.experimental import pallas as pl
from jax.experimental.pallas import tpu as pltpu
from jax.sharding import PartitionSpec as P

D = 768
HEADS = 12
HD = 64
FF = 3072
L = 512
PASS = 4
STEP = 10
ROWS_DEV = 8
MIB = 1 << 20
PART = 256
TAIL = 2 * D + FF


masked_value = -1e30
grid_weight = 4.0
norm_eps = 1e-12
beta_decay = 0.5
adam_eps = 1e-06
norm_guard = 1e-06
weight_decay = 0.01
rate_matrix = 1.0
rate_vector = 0.2


def passage_ids(lengths):
    starts = jnp.cumsum(lengths, axis=1) - lengths
    positions = jnp.arange(L, dtype=jnp.int32)
    return jnp.sum((positions[None, :, None] >= starts[:, None, :]).astype(jnp.int32), axis=2) - 1


AXES = ("dp", "mp")
GRID = (8, 4)


def links(move):
    pairs = []
    for z in range(4):
        for x in range(2):
            for y in range(2):
                for c in range(2):
                    tz, tx, ty, tc = move(z, x, y, c)
                    pairs.append(
                        ((z * 2 + x) * 4 + y * 2 + c, (tz % 4 * 2 + tx) * 4 + ty * 2 + tc)
                    )
    return pairs


CORE = links(lambda z, x, y, c: (z, x, y, 1 - c))
OVER_X = links(lambda z, x, y, c: (z, 1 - x, y, c))
OVER_Y = links(lambda z, x, y, c: (z, x, 1 - y, c))
OVER_XY = links(lambda z, x, y, c: (z, 1 - x, 1 - y, c))
UP_Z = [links(lambda z, x, y, c, s=s: (z + s, x, y, c)) for s in range(4)]


def after(value, *earlier):
    return lax.optimization_barrier((value, earlier))[0] if earlier else value


def send(value, pairs, *beside):
    return after(lax.ppermute(value, AXES, pairs), *beside)


def on_grid():
    return (lax.axis_size("dp"), lax.axis_size("mp")) == GRID


def place():
    dp_index = lax.axis_index("dp")
    mp_index = lax.axis_index("mp")
    return jnp.stack([dp_index // 2, dp_index % 2, mp_index // 2, mp_index % 2, mp_index])


ITEMS = (
    [(x, 0, z) for x in (0, 1) for z in (0, 1)]
    + [(0, y, z) for y in (0, 1) for z in (2, 3)]
    + [(x, 1, z) for x in (0, 1) for z in (0, 1)]
    + [(1, y, z) for y in (0, 1) for z in (2, 3)]
)


def gather_z(shard, *beside):
    return [shard] + [send(shard, UP_Z[s], *beside) for s in (1, 2, 3)]


def gather_near(parts, *beside):
    first, second = jnp.stack(parts[:2]), jnp.stack(parts[2:])
    return [
        jnp.concatenate([first, send(first, OVER_X, *beside)]),
        jnp.concatenate([second, send(second, OVER_Y, *beside)]),
    ]


def gather_far(near, *beside):
    return [send(near[0], OVER_Y, *beside), send(near[1], OVER_X, *beside)]


def gather_core(parts, *beside):
    return [send(part, CORE, *beside) for part in parts]


def gather_plain(shard):
    mp_size = lax.axis_size("mp")
    return lax.all_gather(shard, ("mp", "dp"), axis=0, tiled=True).reshape(mp_size, D, D)


def block_of(g, where):
    if not on_grid():
        return g
    return ((where[2] + g % 2) % 2) * 2 + (where[3] + g // 2) % 2


def scatter_plain(parts):
    whole = parts[0]
    return lax.psum_scatter(
        whole.reshape(-1, whole.shape[-1]), ("mp", "dp"), scatter_dimension=0, tiled=True
    )


class Summand:
    def __init__(self, blocks, dp_size):
        rows = D // dp_size
        self.groups = dp_size
        self.rows = rows
        self.blocks = blocks
        self.split = on_grid()
        if self.split:
            self.shapes = [jax.ShapeDtypeStruct((2, 2, 2, 2, rows, D), jnp.bfloat16)] * 2
        else:
            self.shapes = [jax.ShapeDtypeStruct((blocks, D, D), jnp.bfloat16)]

    def write(self, outs, value, g, where):
        if not self.split:
            outs[0][g] = value
            return
        core, y = g // 2, g % 2
        for index in range(self.groups):
            x = (index % 2 + where[1]) % 2
            z = (index // 2 + 4 - where[0]) % 4
            half = z // 2
            over_y = half == 0
            first, second = jnp.where(over_y, y, x), jnp.where(over_y, x, y)
            outs[core % len(outs)][half, first, second, z % 2] = value[
                index * self.rows : (index + 1) * self.rows
            ]


def share_plain(value):
    whole = lax.all_gather(value, AXES, axis=0, tiled=True)
    own = lax.axis_index("dp") * lax.axis_size("mp") + lax.axis_index("mp")
    return jnp.roll(whole, -own * value.shape[0], axis=0)


def share_core(value, *beside):
    return jnp.concatenate([value, send(value, CORE, *beside)])


def share_plane(value, *beside):
    sides = [send(value, pairs, *beside) for pairs in (OVER_X, OVER_Y, OVER_XY)]
    return jnp.concatenate([value] + sides)


def share_line(value, *beside):
    return jnp.concatenate([value] + [send(value, UP_Z[s], *beside) for s in (1, 2, 3)])


def shared_ids(own_rows):
    dp_size, mp_size = lax.axis_size("dp"), lax.axis_size("mp")
    dp_index, mp_index = lax.axis_index("dp"), lax.axis_index("mp")
    count = dp_size * mp_size * own_rows
    n = jnp.arange(count, dtype=jnp.int32)
    if not on_grid():
        return (n + (dp_index * mp_size + mp_index) * own_rows) % count
    item = n // own_rows
    core, side, up = item % 2, item // 2 % 4, item // 8
    z, x = (dp_index // 2 + 4 - up) % 4, (dp_index + side) % 2
    y, c = (mp_index // 2 + side // 2) % 2, (mp_index + core) % 2
    return ((z * 2 + x) * mp_size + y * 2 + c) * own_rows + n % own_rows


def total(value):
    if not on_grid():
        return lax.psum(value, AXES)
    value = value + send(value, CORE)
    value = value + sum(send(value, pairs) for pairs in (OVER_X, OVER_Y, OVER_XY))
    return value + sum(send(value, UP_Z[s]) for s in (1, 2, 3))


LOW = jnp.bfloat16
WIDE = jnp.float32
B1, BO, B2, G1, C1, G2, C2 = 2 * D, TAIL, TAIL + D, TAIL + 2 * D, TAIL + 3 * D, TAIL + 4 * D, TAIL + 5 * D
VEC = 8 * D + FF


def dot(left, right, over=(1, 0)):
    return lax.dot_general(
        left, right, (((over[0],), (over[1],)), ((), ())), preferred_element_type=WIDE
    )


def call(kernel, name, where, operands, outs, scratch=(), limit=14, wait_for=()):
    count = len(operands)
    many = len(outs)

    def body(where, *refs):
        results = refs[count + len(wait_for) :]
        results[many][...] = jnp.zeros((8, 128), WIDE)
        kernel(where, *refs[:count], *results[:many], *results[many + 1 :])

    def spec(operand):
        integers = operand.dtype == jnp.int32 and operand.ndim == 1
        return pl.BlockSpec(memory_space=pltpu.SMEM if integers else pltpu.VMEM)

    return pl.pallas_call(
        body,
        in_specs=[pl.BlockSpec(memory_space=pltpu.SMEM)]
        + [spec(operand) for operand in operands]
        + [pl.BlockSpec(memory_space=pl.ANY)] * len(wait_for),
        out_specs=[pl.BlockSpec(memory_space=pltpu.VMEM)] * (many + 1),
        out_shape=list(outs) + [array(WIDE, 8, 128)],
        scratch_shapes=list(scratch),
        compiler_params=pltpu.CompilerParams(vmem_limit_bytes=limit * MIB),
        cost_estimate=pl.CostEstimate(flops=3 * 10**10, bytes_accessed=MIB, transcendentals=0),
        name=name,
    )(where, *operands, *wait_for)


def array(dtype, *shape):
    return jax.ShapeDtypeStruct(shape, dtype)


def normalize(value):
    center = jnp.mean(value, axis=1, keepdims=True)
    offsets = value - center
    inverse = lax.rsqrt(jnp.mean(offsets * offsets, axis=1, keepdims=True) + norm_eps)
    return offsets * inverse, inverse


def norm_back(grad, unit, inverse, gain):
    scaled = grad * gain
    return inverse * (
        scaled
        - jnp.mean(scaled, axis=1, keepdims=True)
        - unit * jnp.mean(scaled * unit, axis=1, keepdims=True)
    )


def column_sum(value):
    return jnp.sum(value, axis=0, keepdims=True)


def settle_kernel(where, *refs):
    pieces, out = refs[:8], refs[8]
    for core in range(2):
        for item, (x, y, z) in enumerate(ITEMS):
            block = (where[2] + y) % 2 * 2 + (where[3] + core) % 2
            row = (where[0] + 4 - z) % 4 * 2 + (where[1] + x) % 2
            out[block, row] = pieces[core * 4 + item // 4][item % 4]


def settle(where, pieces):
    rows = pieces[0].shape[1]
    whole = call(settle_kernel, "settle", where, pieces, [array(LOW, 4, 8, rows, D)], limit=8)[0]
    return whole.reshape(4, D, D)


def add_kernel(plan, where, *refs):
    count = max(max(pair[0], pair[2]) for pair in plan) + 1
    for out, (left, left_at, right, right_at) in zip(refs[count:], plan):
        out[...] = (
            refs[left][left_at].astype(WIDE) + refs[right][right_at].astype(WIDE)
        ).astype(LOW)


def add(where, operands, plan, wait_for=()):
    outs = []
    for left, left_at, _, _ in plan:
        outs.append(array(LOW, *operands[left].shape[len(left_at) :]))
    return call(partial(add_kernel, plan), "add", where, operands, outs, limit=8, wait_for=wait_for)


def scatter_core(where, parts, *beside, arrived=None):
    if arrived is None:
        arrived = send(parts[1], CORE, *beside)
    plan = [(0, (half, near), 1, (half, near)) for half in (0, 1) for near in (0, 1)]
    return add(where, [parts[0], arrived], plan)


def scatter_far(where, sums, *beside):
    arrived = [send(sums[1], OVER_Y, *beside), send(sums[3], OVER_X, *beside)]
    plan = [(half, (far,), half + 2, (far,)) for half in (0, 1) for far in (0, 1)]
    return add(where, [sums[0], sums[2], *arrived], plan)


def scatter_near(where, sums, *beside, wait_for=()):
    arrived = [send(sums[1], OVER_X, *beside), send(sums[3], OVER_Y, *beside)]
    plan = [(half, (z,), half + 2, (z,)) for half in (0, 1) for z in (0, 1)]
    return add(where, [sums[0], sums[2], *arrived], plan, wait_for)


def scatter_z(sums, *beside):
    return [sums[0]] + [send(sums[s], UP_Z[s], *beside) for s in (1, 2, 3)]


TILE = 2 * HD
HEADS_BLOCK = 3
SIDES = (0, 1, 0)
KEYS = 3 * TILE
OUT = 4 * TILE


def join_columns(query, key, value, out):
    q, v = [[part[:, h * HD : (h + 1) * HD] for h in range(3)] for part in (query, value)]
    return jnp.concatenate([q[0], v[0], v[1], q[1], q[2], v[2], key, out], axis=1)


def query_columns(part):
    return jnp.concatenate([part[:, :HD], part[:, 3 * HD : 5 * HD]], axis=1)


def value_columns(part):
    return jnp.concatenate([part[:, HD : 3 * HD], part[:, 5 * HD : 6 * HD]], axis=1)


def arrange_kernel(where, qkv_ref, out_ref, held):
    parts = [qkv_ref[0], qkv_ref[1], qkv_ref[2], out_ref[...].T]
    held[...] = join_columns(*parts).astype(LOW)


def arrange(where, qkv_weight, out_weight):
    outs = [array(LOW, qkv_weight.shape[1], D)]
    return call(arrange_kernel, "arrange", where, [qkv_weight, out_weight], outs, limit=8)[0]


def arrange_bias_kernel(where, vec_ref, held):
    blocks = held.shape[0]
    width = D // blocks
    none = jnp.zeros((1, width), WIDE)
    for m in range(blocks):
        query = vec_ref[:, m * width : (m + 1) * width]
        value = vec_ref[:, D + m * width : D + (m + 1) * width]
        held[m] = join_columns(query, none, value, none)


def arrange_bias(where, vectors, blocks):
    outs = [array(WIDE, blocks, 1, D)]
    return call(arrange_bias_kernel, "arrange_bias", where, [vectors], outs, limit=8)[0]


def attend_kernel(blocks, chosen, last, where, x_ref, w_ref, bias_ref, vec_ref, seg_ref, *refs):
    if chosen[0] == 0:
        held = None
    else:
        held, refs = refs[0], refs[1:]
    q_out, k_out, v_out, log_out, context_out, *refs = refs
    if last:
        unit_out, inverse_out, low_out, sum_ref = refs
    else:
        (sum_ref,) = refs
    x = x_ref[...]
    lanes = lax.broadcasted_iota(jnp.int32, (L, TILE), 1)
    passage = jnp.broadcast_to(seg_ref[...], (L, TILE))
    sides = []
    for side in SIDES:
        mine = (lanes >= HD) == side
        column = lanes - (0 if side else HD)
        foreign = (column >= 0) & (column < PASS) & (column != passage)
        same = (column >= 0) & (column < PASS) & (column == passage)
        sides.append(
            (
                jnp.where(mine, HD ** (-0.5), 0.0).astype(LOW),
                jnp.where(foreign, masked_value, 0.0).astype(LOW),
                jnp.where(mine, 1.0, 0.0).astype(LOW),
                jnp.where(same, 1.0, 0.0).astype(LOW),
                jnp.where(mine, 0.0, 1.0).astype(LOW),
            )
        )
    sum_ref[...] = held[...] if held is not None else x.astype(WIDE) + vec_ref[:, BO : BO + D]

    def block(i, carry):
        m = block_of(chosen[0] + i, where)
        projected = (dot(x, w_ref[m]) + bias_ref[m]).astype(LOW)
        parts = [jnp.zeros((HD, L), LOW)]
        for h in range(HEADS_BLOCK):
            q_scale, q_tail, k_scale, k_tail, v_scale = sides[h]
            tile = projected[:, h * TILE : (h + 1) * TILE]
            query = tile * q_scale + q_tail
            at = KEYS + h // 2 * TILE
            keys = projected[:, at : at + TILE] * k_scale + k_tail
            value = tile.T[: HD] if SIDES[h] else tile.T[HD:]
            scores = dot(keys, query, (1, 1))
            highest = jnp.max(scores, axis=0, keepdims=True)
            weights = jnp.exp(scores - highest)
            totals = jnp.sum(weights, axis=0, keepdims=True)
            mixed = dot(value, weights.astype(LOW)) * (1.0 / totals)
            parts.append(mixed.astype(LOW))
            q_out[i * HEADS_BLOCK + h] = query
            k_out[i * HEADS_BLOCK + h] = keys
            v_out[i * HEADS_BLOCK + h] = tile * v_scale
            log_out[i * HEADS_BLOCK + h] = highest + jnp.log(totals)
        context = jnp.concatenate(parts, axis=0).T
        context_out[i] = context
        sum_ref[...] += dot(context, w_ref[m, :, OUT:], (1, 1))
        return carry

    lax.fori_loop(0, len(chosen), block, 0)
    if last:
        unit, inverse = normalize(sum_ref[...])
        unit_out[...] = unit
        inverse_out[...] = inverse
        low_out[...] = (unit * vec_ref[:, G1 : G1 + D] + vec_ref[:, C1 : C1 + D]).astype(LOW)


def attend(where, chosen, held, inputs, weight, bias, vectors, segments, wait_for=()):
    blocks = bias.shape[0]
    heads = len(chosen) * HEADS // blocks
    last = chosen[-1] == blocks - 1
    outs = [
        array(LOW, heads, L, TILE),
        array(LOW, heads, L, TILE),
        array(LOW, heads, L, TILE),
        array(WIDE, heads, 1, L),
        array(LOW, len(chosen), L, D - OUT),
    ]
    if last:
        outs += [array(WIDE, L, D), array(WIDE, L, 1), array(LOW, L, D)]
    else:
        outs += [array(WIDE, L, D)]
    return call(
        partial(attend_kernel, blocks, chosen, last),
        "attend",
        where,
        [inputs, weight, bias, vectors, segments] + ([] if held is None else [held]),
        outs,
        [pltpu.VMEM((L, D), WIDE)] if last else [],
        wait_for=wait_for,
    )


def widen_kernel(rows, where, *refs):
    lows, (w_ref, bias_ref, active_out, slope_out) = refs[:rows], refs[rows:]

    def block(m, carry):
        for row in range(rows):
            hidden = dot(lows[row][...], w_ref[m]) + bias_ref[m]
            half = 0.5 * (1.0 + lax.erf(hidden * math.sqrt(0.5)))
            active_out[m, row * L : (row + 1) * L] = (hidden * half).astype(LOW)
            density = jnp.exp(-0.5 * hidden * hidden) * (1.0 / math.sqrt(2.0 * math.pi))
            slope_out[m, row * L : (row + 1) * L] = (half + hidden * density).astype(LOW)
        return carry

    lax.fori_loop(0, w_ref.shape[0], block, 0)


def widen(where, lows, weight, bias, wait_for=()):
    blocks = bias.shape[0]
    rows = len(lows)
    return call(
        partial(widen_kernel, rows),
        "widen",
        where,
        [*lows, weight, bias],
        [array(LOW, blocks, rows * L, D)] * 2,
        wait_for=wait_for,
    )


def early_kernel(rows, blocks, where, active_ref, w_ref, vec_ref, starts_ref, *refs):
    units, (cls_out, active_wide, rows_ref, sum_ref) = refs[:rows], refs[rows:]
    few = cls_out.shape[0]
    each = few // rows
    for p in range(few):
        at = pl.ds(starts_ref[p] - p // each * L, 1)
        sum_ref[p : p + 1] = units[p // each][at, :]
    sum_ref[...] = sum_ref[...] * vec_ref[:, G1 : G1 + D] + (
        vec_ref[:, C1 : C1 + D] + vec_ref[:, B2 : B2 + D]
    )
    for m in range(blocks):
        for p in range(few):
            base = pl.multiple_of(starts_ref[p] // 16 * 16, 16)
            active_wide[...] = active_ref[m, pl.ds(base, 16), :].astype(WIDE)
            rows_ref[p : p + 1] = active_wide[pl.ds(starts_ref[p] - base, 1), :]
        sum_ref[...] += dot(rows_ref[...].astype(LOW), w_ref[m], (1, 1))
    unit, _ = normalize(sum_ref[...])
    output = unit * vec_ref[:, G2 : G2 + D] + vec_ref[:, C2 : C2 + D]
    cls_out[...] = output.astype(LOW).astype(WIDE)


def early(where, active, weight, vectors, starts, units):
    few = starts.shape[0]
    return call(
        partial(early_kernel, len(units), active.shape[0]),
        "early",
        where,
        [active, weight, vectors, starts, *units],
        [array(WIDE, few, D)],
        [pltpu.VMEM((16, D), WIDE), pltpu.VMEM((few, D), WIDE), pltpu.VMEM((few, D), WIDE)],
        limit=8,
    )


def narrow_kernel(row, where, active_ref, w_ref, vec_ref, unit_ref, out, unit_out, inverse_out):
    at = slice(row * L, (row + 1) * L)
    value = unit_ref[...] * vec_ref[:, G1 : G1 + D] + (
        vec_ref[:, C1 : C1 + D] + vec_ref[:, B2 : B2 + D]
    )
    for m in range(w_ref.shape[0]):
        value += dot(active_ref[m, at], w_ref[m], (1, 1))
    unit, inverse = normalize(value)
    unit_out[...] = unit
    inverse_out[...] = inverse
    out[...] = (unit * vec_ref[:, G2 : G2 + D] + vec_ref[:, C2 : C2 + D]).astype(LOW)


def narrow(where, row, active, weight, vectors, unit, wait_for=()):
    return call(
        partial(narrow_kernel, row),
        "narrow",
        where,
        [active, weight, vectors, unit],
        [array(LOW, L, D), array(WIDE, L, D), array(WIDE, L, 1)],
        wait_for=wait_for,
    )


def contrast_kernel(
    rows, where, cot_ref, vec_ref, starts_ref, own_ref, all_ref, ids_ref, ids_own_ref,
    partners_own_ref, *refs
):
    units, inverses, refs = refs[:rows], refs[rows : 2 * rows], refs[2 * rows :]
    (grad_out, low_out, bias_out, gain_out, shift_out, y_ref) = refs
    scale = 2.0 / math.sqrt(D)
    everyone = all_ref[...]
    own = own_ref[...].astype(LOW)
    count = everyone.shape[0]
    scores = dot(everyone, everyone, (1, 1)) * scale
    diagonal = lax.broadcasted_iota(jnp.int32, (count, count), 0) == lax.broadcasted_iota(
        jnp.int32, (count, count), 1
    )
    scores = jnp.where(diagonal, masked_value, scores)
    highest = jnp.max(scores, axis=0, keepdims=True)
    log_all = highest + jnp.log(jnp.sum(jnp.exp(scores - highest), axis=0, keepdims=True))
    here = dot(own, everyone, (1, 1)) * scale
    ids = ids_ref[...]
    here = jnp.where(ids_own_ref[...] == ids, masked_value, here)
    top = jnp.max(here, axis=1, keepdims=True)
    log_own = top + jnp.log(jnp.sum(jnp.exp(here - top), axis=1, keepdims=True))
    pair = (partners_own_ref[...] == ids).astype(WIDE)
    out_grad = grid_weight * (jnp.exp(here - log_own) - pair)
    in_grad = grid_weight * (jnp.exp(here - log_all) - pair)
    cls_grad = scale * (dot(out_grad.astype(LOW), everyone) + dot(in_grad.astype(LOW), everyone))
    y_ref[...] = cot_ref[...].astype(WIDE)
    for p in range(cls_grad.shape[0]):
        y_ref[pl.ds(starts_ref[p], 1), :] += cls_grad[p : p + 1]
    for ref in (bias_out, gain_out, shift_out):
        ref[...] = jnp.zeros_like(ref)
    for part in range(y_ref.shape[0] // PART):
        at = slice(part * PART, (part + 1) * PART)
        row, inner = part * PART // L, slice(part * PART % L, part * PART % L + PART)
        grad = y_ref[at]
        unit = units[row][inner]
        gain_out[...] += column_sum(grad * unit)
        shift_out[...] += column_sum(grad)
        back = norm_back(grad, unit, inverses[row][inner], vec_ref[:, G2 : G2 + D])
        grad_out[at] = back
        low = back.astype(LOW)
        low_out[at] = low
        bias_out[...] += column_sum(low.astype(WIDE))


def contrast(where, cotangent, units, inverses, vectors, starts, own, everyone, ids, ids_own, partners_own):
    tokens = cotangent.shape[0]
    return call(
        partial(contrast_kernel, len(units)),
        "contrast",
        where,
        [
            cotangent, vectors, starts, own, everyone, ids, ids_own, partners_own, *units, *inverses,
        ],
        [
            array(WIDE, tokens, D),
            array(LOW, tokens, D),
            array(WIDE, 1, D),
            array(WIDE, 1, D),
            array(WIDE, 1, D),
        ],
        [pltpu.VMEM((tokens, D), WIDE)],
    )


def down_grad_kernel(summand, where, grad_ref, active_ref, *refs):
    outs, turned = refs[:-1], refs[-1]
    turned[...] = grad_ref[...].T
    for g in range(summand.blocks):
        value = dot(turned[...], active_ref[block_of(g, where)]).astype(LOW)
        summand.write(outs, value, g, where)


def grad_of_down(where, grad_low, active, summand):
    tokens = active.shape[1]
    return call(
        partial(down_grad_kernel, summand),
        "grad_of_down",
        where,
        [grad_low, active],
        summand.shapes,
        [pltpu.VMEM((D, tokens), LOW)],
    )


def up_grad_kernel(summand, rows, where, grad_ref, w_ref, slope_ref, *refs):
    lows, (grad_out, bias_out), refs = refs[:rows], refs[rows : rows + 2], refs[rows + 2 :]
    outs, turned = refs[:-1], refs[-1]
    for row in range(rows):
        turned[:, row * L : (row + 1) * L] = lows[row][...].T
    for g in range(summand.blocks):
        m = block_of(g, where)
        bias = jnp.zeros((1, D), WIDE)
        for row in range(rows):
            at = slice(row * L, (row + 1) * L)
            grad = dot(grad_ref[at], w_ref[m]) * slope_ref[m, at].astype(WIDE)
            grad = grad.astype(LOW)
            grad_out[m, at] = grad
            bias += column_sum(grad.astype(WIDE))
        bias_out[m] = bias
        summand.write(outs, dot(turned[...], grad_out[m]).astype(LOW), g, where)


def grad_of_up(where, grad_low, weight, slope, lows, summand, wait_for=()):
    blocks, tokens, _ = slope.shape
    return call(
        partial(up_grad_kernel, summand, len(lows)),
        "grad_of_up",
        where,
        [grad_low, weight, slope, *lows],
        [array(LOW, blocks, tokens, D), array(WIDE, blocks, 1, D)] + summand.shapes,
        [pltpu.VMEM((D, tokens), LOW)],
        wait_for=wait_for,
    )


def middle_kernel(blocks, rows, where, hidden_ref, up_ref, sum_ref, vec_ref, w_ref, *refs):
    units, inverses, refs = refs[:rows], refs[rows : 2 * rows], refs[2 * rows :]
    grad_out, low_out, bias_out, gain_out, shift_out, context_out = refs
    for ref in (bias_out, gain_out, shift_out):
        ref[...] = jnp.zeros_like(ref)
    for row in range(rows):
        at = slice(row * L, (row + 1) * L)
        grad_out[at] = sum_ref[at]

        def block(m, carry):
            grad_out[at] += dot(hidden_ref[m, at], up_ref[m], (1, 1))
            return carry

        lax.fori_loop(0, blocks, block, 0)
        for part in range(L // PART):
            inner = slice(part * PART, (part + 1) * PART)
            outer = slice(row * L + part * PART, row * L + (part + 1) * PART)
            grad = grad_out[outer]
            unit = units[row][inner]
            gain_out[...] += column_sum(grad * unit)
            shift_out[...] += column_sum(grad)
            back = norm_back(grad, unit, inverses[row][inner], vec_ref[:, G1 : G1 + D])
            grad_out[outer] = back
            low = back.astype(LOW)
            low_out[outer] = low
            bias_out[...] += column_sum(low.astype(WIDE))
        for m in range(blocks):
            context_out[row * blocks + m] = dot(
                low_out[at], w_ref[block_of(m, where), :, OUT:]
            ).astype(LOW)


def middle(where, hidden_grad, up, sum_grad, units, inverses, vectors, weight, wait_for=()):
    blocks, tokens, _ = hidden_grad.shape
    rows = len(units)
    return call(
        partial(middle_kernel, blocks, rows),
        "middle",
        where,
        [hidden_grad, up, sum_grad, vectors, weight, *units, *inverses],
        [
            array(WIDE, tokens, D),
            array(LOW, tokens, D),
            array(WIDE, 1, D),
            array(WIDE, 1, D),
            array(WIDE, 1, D),
            array(LOW, rows * blocks, L, D - OUT),
        ],
        wait_for=wait_for,
    )


def attend_back_kernel(blocks, row, chosen, where, q_ref, k_ref, v_ref, log_ref, grad_ref, out):
    lanes = lax.broadcasted_iota(jnp.int32, (L, TILE), 1)
    low_half = lanes < HD

    def block(i, carry):
        key_grads = []
        for h in range(HEADS_BLOCK):
            n = i * HEADS_BLOCK + h
            queries, keys = q_ref[n], k_ref[n]
            at = (h + 1) // 2 * TILE
            grad = grad_ref[row * blocks + chosen[0] + i, :, at : at + TILE]
            weights = jnp.exp(dot(keys, queries, (1, 1)) - log_ref[n])
            weight_grad = dot(v_ref[n], grad, (1, 1))
            middle_sum = jnp.sum(weight_grad * weights, axis=0, keepdims=True)
            score_grad = (weights * (weight_grad - middle_sum)).astype(LOW)
            query_grad = (dot(keys.T, score_grad) * HD ** (-0.5)).T
            value_grad = dot(weights.astype(LOW), grad)
            key_grads.append(dot(score_grad, queries))
            pair = (value_grad, query_grad) if SIDES[h] else (query_grad, value_grad)
            out[i, :, h * TILE : (h + 1) * TILE] = jnp.where(low_half, *pair).astype(LOW)
        pair = jnp.where(low_half, key_grads[0], key_grads[1])
        out[i, :, KEYS : KEYS + TILE] = pair.astype(LOW)
        out[i, :, OUT : OUT + TILE] = jnp.where(low_half, key_grads[2], 0.0).astype(LOW)
        out[i, :, OUT + TILE :] = jnp.zeros((L, D - OUT - TILE), LOW)
        return carry

    lax.fori_loop(0, len(chosen), block, 0)


def attend_back(where, row, blocks, chosen, queries, keys, values, logs, context_grad, wait_for=()):
    return call(
        partial(attend_back_kernel, blocks, row, chosen),
        "attend_back",
        where,
        [queries, keys, values, logs, context_grad],
        [array(LOW, len(chosen), L, D)],
        wait_for=wait_for,
    )


def attention_grad_kernel(summand, rows, chosen, where, x_ref, low_ref, *refs):
    grads, contexts, refs = refs[:rows], refs[rows : 2 * rows], refs[2 * rows :]
    bias_out, outs, (x_turned, low_turned) = refs[0], refs[1:-2], refs[-2:]
    x_turned[...] = x_ref[...].T
    low_turned[...] = low_ref[...].T
    for i, g in enumerate(chosen):
        bias = jnp.zeros((1, D), WIDE)
        value = jnp.zeros((D, D), WIDE)
        own = jnp.zeros((D, D - OUT), WIDE)
        for row in range(rows):
            at = slice(row * L, (row + 1) * L)
            grad = grads[row][i]
            bias += column_sum(grad.astype(WIDE))
            value += dot(x_turned[:, at], grad)
            own += dot(low_turned[:, at], contexts[row][i])
        bias_out[i] = bias
        value = jnp.concatenate([value[:, :OUT], value[:, OUT:] + own], axis=1).astype(LOW)
        summand.write(outs, value, g, where)


def grad_of_attention(where, chosen, inputs, grad_low, grads, contexts, summand, wait_for=()):
    tokens = inputs.shape[0]
    return call(
        partial(attention_grad_kernel, summand, len(grads), chosen),
        "grad_of_attention",
        where,
        [inputs, grad_low, *grads, *contexts],
        [array(WIDE, len(chosen), 1, D)] + summand.shapes[:1],
        [pltpu.VMEM((D, tokens), LOW)] * 2,
        wait_for=wait_for,
    )


def input_grad_kernel(rows, where, w_ref, first_ref, *refs):
    grads, out = refs[:-1], refs[-1]
    cuts = len(grads) // rows
    for row in range(rows):
        at = slice(row * L, (row + 1) * L)
        value = first_ref[at]
        for c in range(cuts):
            ref = grads[row * cuts + c]
            for i in range(ref.shape[0]):
                value += dot(ref[i], w_ref[block_of(c * ref.shape[0] + i, where)], (1, 1))
        out[at] = value


def grad_of_input(where, rows, grads, weight, first_grad, wait_for=()):
    return call(
        partial(input_grad_kernel, rows),
        "grad_of_input",
        where,
        [weight, first_grad, *grads],
        [array(WIDE, *first_grad.shape)],
        wait_for=wait_for,
    )


def pack_kernel(cuts, where, *refs):
    biases, up_ref, others, out = refs[:cuts], refs[cuts], refs[cuts + 1 : -2], refs[-2]
    rows_ref = refs[-1]
    each = biases[0].shape[0]
    blocks = cuts * each
    for g in range(blocks):
        rows_ref[block_of(g, where)] = biases[g // each][g % each]
    rows = [rows_ref[m] for m in range(blocks)]
    out[:, :D] = jnp.concatenate([query_columns(row) for row in rows], axis=1)
    out[:, D : 2 * D] = jnp.concatenate([value_columns(row) for row in rows], axis=1)
    units = FF // blocks
    for m in range(blocks):
        out[:, 2 * D + m * units : 2 * D + (m + 1) * units] = up_ref[m]
    for i, ref in enumerate(others):
        out[:, TAIL + i * D : TAIL + (i + 1) * D] = ref[...]


def pack(where, biases, up_bias_grad, *others):
    blocks = up_bias_grad.shape[0]
    return call(
        partial(pack_kernel, len(biases)),
        "pack",
        where,
        [*biases, up_bias_grad, *others],
        [array(WIDE, 1, VEC)],
        [pltpu.VMEM((blocks, 1, D), WIDE)],
        limit=8,
    )[0]


def ratio_of(grad, first, second):
    moment = beta_decay * first + (1.0 - beta_decay) * grad
    second_new = beta_decay * second + (1.0 - beta_decay) * grad * grad
    ratio = (
        moment
        / (1.0 - beta_decay**STEP)
        / (jnp.sqrt(second_new / (1.0 - beta_decay**STEP)) + adam_eps)
    )
    return second_new, ratio


def squares(value):
    return jnp.sum(jnp.sum(value * value, axis=0, keepdims=True), axis=1, keepdims=True)


def adapt_kernel(cut, parts, where, *refs):
    total_sum = refs[0][...].astype(WIDE)
    for ref in refs[1:parts]:
        total_sum += ref[...].astype(WIDE)
    refs = refs[parts:]
    count = len(cut)
    firsts, seconds, weights = refs[:count], refs[count : 2 * count], refs[2 * count : 3 * count]
    outs = refs[3 * count :]
    lines = []
    for i, pick in enumerate(cut):
        for part, grad in pick(total_sum):
            def at(ref):
                return ref if part is None else ref.at[part]

            second_new, ratio = ratio_of(grad, at(firsts[i])[...], at(seconds[i])[...])
            weight = at(weights[i])[...]
            update = ratio + weight_decay * weight
            at(outs[3 * i])[...] = grad
            at(outs[3 * i + 1])[...] = second_new
            at(outs[3 * i + 2])[...] = update
            lines.append((squares(weight), squares(update)))
    lanes = lax.broadcasted_iota(jnp.int32, (1, 128), 1)
    held = jnp.zeros((1, 128), WIDE)
    for i, (weight_square, update_square) in enumerate(lines):
        held = jnp.where(lanes == 2 * i, weight_square, held)
        held = jnp.where(lanes == 2 * i + 1, update_square, held)
    outs[-1][...] = held


def adapt(name, where, parts, cut, firsts, seconds, weights):
    outs = [array(WIDE, *w.shape) for w in weights for _ in range(3)] + [array(WIDE, 1, 128)]
    operands = [*parts, *firsts, *seconds, *weights]
    return call(
        partial(adapt_kernel, cut, len(parts)),
        name,
        where,
        operands,
        outs,
    )[:-1]


def renew_kernel(counts, where, sums_ref, grad_ref, first_ref, second_ref, vec_ref, *refs):
    many = len(counts)
    weights, updates, outs = refs[:many], refs[many : 2 * many], refs[2 * many :]
    norms = jnp.sqrt(sums_ref[...])
    outs[-1][...] = norms
    slot = 0
    for i, count in enumerate(counts):
        for part in range(count):
            trust = norms[:, 2 * slot : 2 * slot + 1] / (
                norms[:, 2 * slot + 1 : 2 * slot + 2] + norm_guard
            )
            slot += 1

            def at(ref):
                return ref if count == 1 else ref.at[part]

            new = at(weights[i])[...] - rate_matrix * trust * at(updates[i])[...]
            at(outs[2 * i])[...] = new
            at(outs[2 * i + 1])[...] = new.astype(LOW)
    second_new, ratio = ratio_of(grad_ref[...], first_ref[...], second_ref[...])
    outs[-3][...] = second_new
    outs[-2][...] = vec_ref[...] - rate_vector * ratio


def renew(where, sums, vector_grad, vector_first, vector_second, vectors, weights, updates):
    counts = [3 if w.ndim == 3 else 1 for w in weights]
    outs = [array(dtype, *w.shape) for w in weights for dtype in (WIDE, LOW)]
    outs += [array(WIDE, 1, VEC), array(WIDE, 1, VEC), array(WIDE, 1, 128)]
    operands = [sums, vector_grad, vector_first, vector_second, vectors, *weights, *updates]
    return call(
        partial(renew_kernel, counts),
        "renew",
        where,
        operands,
        outs,
    )[:-1]


def shards(
    block_input,
    cotangent,
    lengths,
    partner,
    qkv_weight,
    out_weight,
    up_weight,
    down_weight,
    qkv_first,
    out_first,
    up_first,
    down_first,
    qkv_second,
    out_second,
    up_second,
    down_second,
    vectors,
    vector_first,
    vector_second,
):
    mp_size = lax.axis_size("mp")
    dp_size = lax.axis_size("dp")
    mp_index = lax.axis_index("mp")
    dp_index = lax.axis_index("dp")
    tokens = cotangent.shape[0]
    rows = tokens // L
    own_rows = rows * PASS
    width = D // mp_size
    where = place()
    down_turned = down_weight.T
    weight_shard = arrange(where, qkv_weight, out_weight)
    up_shard = up_weight.astype(LOW)
    down_shard = down_turned.astype(LOW)
    local_lengths = lax.dynamic_slice_in_dim(lengths, mp_index * rows, rows, 0)
    inputs = lax.dynamic_slice_in_dim(block_input, mp_index * tokens, tokens, 0)
    segments = passage_ids(local_lengths).reshape(tokens, 1)
    starts = jnp.cumsum(local_lengths, axis=1) - local_lengths
    starts = (starts + L * jnp.arange(rows, dtype=jnp.int32)[:, None]).reshape(own_rows)
    partner_own = lax.dynamic_slice_in_dim(partner, mp_index * own_rows, own_rows, 0)
    ids_own = (dp_index * mp_size + mp_index) * own_rows + jnp.arange(own_rows, dtype=jnp.int32)
    ids_all = shared_ids(own_rows)
    vec = vectors.reshape(1, VEC)
    bias = arrange_bias(where, vec, mp_size)
    bias_up = vectors[2 * D : TAIL].reshape(mp_size, 1, D)

    summand = Summand(mp_size, dp_size)

    def attend_part(row, chosen, held, weight, *wait_for):
        at = slice(row * L, (row + 1) * L)
        return attend(
            where, chosen, held, inputs[at], weight, bias, vec, segments[at], wait_for=wait_for
        )

    halves = [range(mp_size // 2), range(mp_size // 2, mp_size)]
    if on_grid():
        weight_z = gather_z(weight_shard)
        weight_near = gather_near(weight_z)
        up_z = gather_z(after(up_shard, *weight_z))
        weight_far = gather_far(weight_near)
        weight_parts = weight_near + weight_far
        weight = settle(where, weight_parts + gather_core(weight_parts))
        up_z = after(up_z, *weight_far)
        kept = [[None, None] for _ in range(rows)]
        kept[0][0] = attend_part(0, halves[0], None, weight, *up_z)
        up_near = gather_near(up_z, kept[0][0][-1])
        down_z = gather_z(after(down_shard, *up_z), kept[0][0][-1])
        kept[0][1] = attend_part(0, halves[1], kept[0][0][5], weight, *up_near)
        kept[1][0] = attend_part(1, halves[0], None, weight, kept[0][1][-1], *down_z)
        up_far = gather_far(up_near, kept[1][0][-1])
        up_cores = gather_core(up_near, kept[1][0][-1])
        down_near = gather_near(after(down_z, *up_near), kept[1][0][-1])
        kept[1][1] = attend_part(1, halves[1], kept[1][0][5], weight, *up_far)
        up_cores += gather_core(up_far, kept[1][1][-1])
        up = settle(where, up_near + up_far + up_cores)
    else:
        weight = gather_plain(weight_shard)
        up = gather_plain(up_shard)
        down_near = []
        kept = []
        for row in range(rows):
            first = attend_part(row, halves[0], None, weight)
            kept.append([first, attend_part(row, halves[1], first[5], weight)])
    units_first, inverses_first, lows = zip(*[kept[row][1][5:8] for row in range(rows)])
    active, slope, widened = widen(where, lows, up, bias_up, wait_for=down_near)
    if on_grid():
        down_far = gather_far(after(down_near, *up_far), widened)
        down_cores = gather_core(down_near, widened) + gather_core(down_far)
        down = settle(where, down_near + down_far + down_cores)
    else:
        down = gather_plain(down_shard)
    cls_own, ended = early(where, active, down, vec, starts, units_first)
    narrowed = []
    if on_grid():
        rounds = share_core(cls_own.astype(LOW))
        narrowed.append(narrow(where, 0, active, down, vec, units_first[0], (ended, rounds)))
        rounds = share_plane(rounds, narrowed[0][-1])
        narrowed.append(narrow(where, 1, active, down, vec, units_first[1], (rounds,)))
        cls_all = share_line(rounds, narrowed[1][-1])
    else:
        for row in range(rows):
            narrowed.append(narrow(where, row, active, down, vec, units_first[row]))
        cls_all = share_plain(cls_own.astype(LOW))
    outputs, units_second, inverses_second, _ = zip(*narrowed)
    block_output = jnp.concatenate(outputs, axis=0)
    sum_grad, branch_low, down_bias_grad, gain_second_grad, shift_second_grad, _ = contrast(
        where, cotangent, units_second, inverses_second, vec, starts, cls_own, cls_all,
        ids_all[None, :], ids_own[:, None], partner_own[:, None],
    )
    *down_part, ended = grad_of_down(where, branch_low, active, summand)
    hidden_grad, up_bias_grad, *up_part, _ = grad_of_up(
        where, branch_low, down, slope, lows, summand, wait_for=(ended,)
    )
    if on_grid():
        *down_sum, added = scatter_core(where, down_part)
    (
        first_grad, attended_low, out_bias_grad, gain_first_grad, shift_first_grad, context_grad, _,
    ) = middle(
        where, hidden_grad, up, sum_grad, units_first, inverses_first, vec, weight,
        wait_for=(added,) if on_grid() else (),
    )

    def back_part(row, half, *wait_for):
        return attend_back(
            where, row, mp_size, halves[half], *kept[row][half][:4], context_grad, wait_for=wait_for
        )

    def grad_part(half, *wait_for):
        return grad_of_attention(
            where, halves[half], inputs, attended_low, [back[row][half] for row in range(rows)],
            [kept[row][half][4] for row in range(rows)], summand, wait_for=wait_for,
        )

    back = [[None, None] for _ in range(rows)]
    if on_grid():
        *down_sum, down_added = scatter_far(where, down_sum)
        *up_sum, up_added = scatter_core(where, up_part)
        back[0][1], ended = back_part(0, 1, down_added, up_added)
        back[1][1], ended = back_part(1, 1, ended)
        bias_other, other_part, ended = grad_part(1)
        *down_sum, down_added = scatter_near(where, down_sum, ended)
        back[0][0], ended = back_part(0, 0, ended, down_added)
        *up_sum, up_added = scatter_far(where, up_sum, ended)
        other_part = send(other_part, CORE)
        back[1][0], ended = back_part(1, 0, up_added, other_part)
        down_parts = scatter_z(down_sum, ended)
        bias_own, own_part, ended = grad_part(0)
        *attention_sum, added = scatter_core(where, [own_part], arrived=other_part)
        *up_sum, up_added = scatter_near(where, up_sum, ended, wait_for=(added,))
    else:
        for row in range(rows):
            for half in (0, 1):
                back[row][half] = back_part(row, half)[0]
        bias_other, other_part, _ = grad_part(1)
        bias_own, own_part, _ = grad_part(0)
    vector_local = pack(
        where,
        [bias_own, bias_other],
        up_bias_grad,
        out_bias_grad,
        down_bias_grad,
        gain_first_grad,
        shift_first_grad,
        gain_second_grad,
        shift_second_grad,
    )
    grads = [back[row][half] for row in range(rows) for half in (0, 1)]
    if on_grid():
        input_grad, ended = grad_of_input(
            where, rows, grads, weight, first_grad, wait_for=(added, up_added)
        )
        up_parts = scatter_z(up_sum, ended)
        *attention_sum, _ = scatter_far(where, attention_sum, ended)
        *attention_sum, _ = scatter_near(where, attention_sum)
        attention_parts = scatter_z(attention_sum)
    else:
        down_parts = [scatter_plain(down_part)]
        up_parts = [scatter_plain(up_part)]
        both = jnp.concatenate([own_part[: mp_size // 2], other_part[mp_size // 2 :]])
        attention_parts = [scatter_plain([both])]
        input_grad, _ = grad_of_input(where, rows, grads, weight, first_grad)
    down_grad, down_second_new, down_update, down_squares = adapt(
        "adapt_down", where, down_parts, [lambda g: [(None, g)]],
        [down_first.T], [down_second.T], [down_turned],
    )
    up_grad, up_second_new, up_update, up_squares = adapt(
        "adapt_up", where, up_parts, [lambda g: [(None, g)]], [up_first], [up_second], [up_weight]
    )
    (
        qkv_grad, qkv_second_new, qkv_update,
        out_grad, out_second_new, out_update, attention_squares,
    ) = adapt(
        "adapt_attention",
        where,
        attention_parts,
        [
            lambda g: [
                (0, query_columns(g)),
                (1, g[:, KEYS : KEYS + width]),
                (2, value_columns(g)),
            ],
            lambda g: [(None, g[:, KEYS + width :].T)],
        ],
        [qkv_first, out_first],
        [qkv_second, out_second],
        [qkv_weight, out_weight],
    )
    summed = total(
        jnp.concatenate(
            [
                vector_local,
                attention_squares[:, :8],
                up_squares[:, :2],
                down_squares[:, :2],
                jnp.zeros((1, 116), WIDE),
            ],
            axis=1,
        )
    )
    vector_grad, sums = summed[:, :VEC], summed[:, VEC:]
    weights = [qkv_weight, out_weight, up_weight, down_turned]
    updates = [qkv_update, out_update, up_update, down_update]
    (
        qkv_new, qkv_copy, out_new, out_copy, up_new, up_copy, down_new, down_copy,
        vector_second_new, vector_new, norms,
    ) = renew(
        where, sums, vector_grad, vector_first.reshape(1, VEC), vector_second.reshape(1, VEC), vec,
        weights, updates,
    )
    return (
        block_output,
        input_grad,
        qkv_grad,
        out_grad,
        up_grad,
        down_grad.T,
        qkv_second_new,
        out_second_new,
        up_second_new,
        down_second_new.T,
        qkv_new,
        out_new,
        up_new,
        down_new.T,
        qkv_copy,
        out_copy,
        up_copy,
        down_copy.T,
        vector_grad.reshape(VEC),
        vector_second_new.reshape(VEC),
        vector_new.reshape(VEC),
        norms[0, :12].reshape(6, 2),
    )


def solution(mesh):
    in_specs = (
        P("dp", None),
        P(("dp", "mp"), None),
        P("dp", None),
        P("dp"),
        P(None, "dp", "mp"),
        P("mp", "dp"),
        P("dp", "mp"),
        P("mp", "dp"),
        P(None, "dp", "mp"),
        P("mp", "dp"),
        P("dp", "mp"),
        P("mp", "dp"),
        P(None, "dp", "mp"),
        P("mp", "dp"),
        P("dp", "mp"),
        P("mp", "dp"),
        P(),
        P(),
        P(),
    )
    out_specs = (
        P(("dp", "mp"), None),
        P(("dp", "mp"), None),
        P(None, "dp", "mp"),
        P("mp", "dp"),
        P("dp", "mp"),
        P("mp", "dp"),
        P(None, "dp", "mp"),
        P("mp", "dp"),
        P("dp", "mp"),
        P("mp", "dp"),
        P(None, "dp", "mp"),
        P("mp", "dp"),
        P("dp", "mp"),
        P("mp", "dp"),
        P(None, "dp", "mp"),
        P("mp", "dp"),
        P("dp", "mp"),
        P("mp", "dp"),
        P(),
        P(),
        P(),
        P(),
    )
    return jax.shard_map(shards, mesh=mesh, in_specs=in_specs, out_specs=out_specs, check_vma=False)
```

```python
from functools import partial
import math

import jax
import jax.numpy as jnp
from jax import lax
from jax.experimental import pallas as pl
from jax.experimental.pallas import tpu as pltpu
from jax.sharding import PartitionSpec as P

D = 768
HEADS = 12
HD = 64
FF = 3072
L = 512
PASS = 4
STEP = 10
ROWS_DEV = 8
MIB = 1 << 20
PART = 256
TAIL = 2 * D + FF


masked_value = -1e30
grid_weight = 4.0
norm_eps = 1e-12
beta_decay = 0.5
adam_eps = 1e-06
norm_guard = 1e-06
weight_decay = 0.01
rate_matrix = 1.0
rate_vector = 0.2


def passage_ids(lengths):
    starts = jnp.cumsum(lengths, axis=1) - lengths
    positions = jnp.arange(L, dtype=jnp.int32)
    return jnp.sum((positions[None, :, None] >= starts[:, None, :]).astype(jnp.int32), axis=2) - 1


AXES = ("dp", "mp")
GRID = (8, 4)


def links(move):
    pairs = []
    for z in range(4):
        for x in range(2):
            for y in range(2):
                for c in range(2):
                    tz, tx, ty, tc = move(z, x, y, c)
                    pairs.append(
                        ((z * 2 + x) * 4 + y * 2 + c, (tz % 4 * 2 + tx) * 4 + ty * 2 + tc)
                    )
    return pairs


CORE = links(lambda z, x, y, c: (z, x, y, 1 - c))
OVER_X = links(lambda z, x, y, c: (z, 1 - x, y, c))
OVER_Y = links(lambda z, x, y, c: (z, x, 1 - y, c))
OVER_XY = links(lambda z, x, y, c: (z, 1 - x, 1 - y, c))
UP_Z = [links(lambda z, x, y, c, s=s: (z + s, x, y, c)) for s in range(4)]


def after(value, *earlier):
    return lax.optimization_barrier((value, earlier))[0] if earlier else value


def send(value, pairs, *beside):
    return after(lax.ppermute(value, AXES, pairs), *beside)


def on_grid():
    return (lax.axis_size("dp"), lax.axis_size("mp")) == GRID


def place():
    dp_index = lax.axis_index("dp")
    mp_index = lax.axis_index("mp")
    return jnp.stack([dp_index // 2, dp_index % 2, mp_index // 2, mp_index % 2, mp_index])


ITEMS = (
    [(x, 0, z) for x in (0, 1) for z in (0, 1)]
    + [(0, y, z) for y in (0, 1) for z in (2, 3)]
    + [(x, 1, z) for x in (0, 1) for z in (0, 1)]
    + [(1, y, z) for y in (0, 1) for z in (2, 3)]
)


def gather_z(shard, *beside):
    return [shard] + [send(shard, UP_Z[s], *beside) for s in (1, 2, 3)]


def gather_near(parts, *beside):
    first, second = jnp.stack(parts[:2]), jnp.stack(parts[2:])
    return [
        jnp.concatenate([first, send(first, OVER_X, *beside)]),
        jnp.concatenate([second, send(second, OVER_Y, *beside)]),
    ]


def gather_far(near, *beside):
    return [send(near[0], OVER_Y, *beside), send(near[1], OVER_X, *beside)]


def gather_core(parts, *beside):
    return [send(part, CORE, *beside) for part in parts]


def gather_plain(shard):
    mp_size = lax.axis_size("mp")
    return lax.all_gather(shard, ("mp", "dp"), axis=0, tiled=True).reshape(mp_size, D, D)


def block_of(g, where):
    if not on_grid():
        return g
    return ((where[2] + g % 2) % 2) * 2 + (where[3] + g // 2) % 2


def scatter_z_both(left, right, *beside):
    parts = [(left[0], right[0])]
    for s in (1, 2, 3):
        pair = send(jnp.stack([left[s], right[s]]), UP_Z[s], *beside)
        parts.append((pair[0], pair[1]))
    return zip(*parts)


def scatter_plain(parts):
    whole = parts[0]
    return lax.psum_scatter(
        whole.reshape(-1, whole.shape[-1]), ("mp", "dp"), scatter_dimension=0, tiled=True
    )


class Summand:
    def __init__(self, blocks, dp_size):
        rows = D // dp_size
        self.groups = dp_size
        self.rows = rows
        self.blocks = blocks
        self.split = on_grid()
        if self.split:
            self.shapes = [jax.ShapeDtypeStruct((2, 2, 2, 2, rows, D), jnp.bfloat16)] * 2
        else:
            self.shapes = [jax.ShapeDtypeStruct((blocks, D, D), jnp.bfloat16)]

    def write(self, outs, value, g, where):
        if not self.split:
            outs[0][g] = value
            return
        core, y = g // 2, g % 2
        for index in range(self.groups):
            x = (index % 2 + where[1]) % 2
            z = (index // 2 + 4 - where[0]) % 4
            half = z // 2
            over_y = half == 0
            first, second = jnp.where(over_y, y, x), jnp.where(over_y, x, y)
            outs[core % len(outs)][half, first, second, z % 2] = value[
                index * self.rows : (index + 1) * self.rows
            ]


def share_plain(value):
    whole = lax.all_gather(value, AXES, axis=0, tiled=True)
    own = lax.axis_index("dp") * lax.axis_size("mp") + lax.axis_index("mp")
    return jnp.roll(whole, -own * value.shape[0], axis=0)


def share_core(value, *beside):
    return jnp.concatenate([value, send(value, CORE, *beside)])


def share_plane(value, *beside):
    sides = [send(value, pairs, *beside) for pairs in (OVER_X, OVER_Y, OVER_XY)]
    return jnp.concatenate([value] + sides)


def share_line(value, *beside):
    return jnp.concatenate([value] + [send(value, UP_Z[s], *beside) for s in (1, 2, 3)])


def shared_ids(own_rows):
    dp_size, mp_size = lax.axis_size("dp"), lax.axis_size("mp")
    dp_index, mp_index = lax.axis_index("dp"), lax.axis_index("mp")
    count = dp_size * mp_size * own_rows
    n = jnp.arange(count, dtype=jnp.int32)
    if not on_grid():
        return (n + (dp_index * mp_size + mp_index) * own_rows) % count
    item = n // own_rows
    core, side, up = item % 2, item // 2 % 4, item // 8
    z, x = (dp_index // 2 + 4 - up) % 4, (dp_index + side) % 2
    y, c = (mp_index // 2 + side // 2) % 2, (mp_index + core) % 2
    return ((z * 2 + x) * mp_size + y * 2 + c) * own_rows + n % own_rows


def total(value):
    if not on_grid():
        return lax.psum(value, AXES)
    value = value + send(value, CORE)
    value = value + sum(send(value, pairs) for pairs in (OVER_X, OVER_Y, OVER_XY))
    return value + sum(send(value, UP_Z[s]) for s in (1, 2, 3))


LOW = jnp.bfloat16
WIDE = jnp.float32
B1, BO, B2, G1, C1, G2, C2 = 2 * D, TAIL, TAIL + D, TAIL + 2 * D, TAIL + 3 * D, TAIL + 4 * D, TAIL + 5 * D
VEC = 8 * D + FF


def dot(left, right, over=(1, 0)):
    return lax.dot_general(
        left, right, (((over[0],), (over[1],)), ((), ())), preferred_element_type=WIDE
    )


def call(kernel, name, where, operands, outs, scratch=(), limit=14, wait_for=()):
    count = len(operands)
    many = len(outs)

    def body(where, *refs):
        results = refs[count + len(wait_for) :]
        results[many][...] = jnp.zeros((8, 128), WIDE)
        kernel(where, *refs[:count], *results[:many], *results[many + 1 :])

    def spec(operand):
        integers = operand.dtype == jnp.int32 and operand.ndim == 1
        return pl.BlockSpec(memory_space=pltpu.SMEM if integers else pltpu.VMEM)

    return pl.pallas_call(
        body,
        in_specs=[pl.BlockSpec(memory_space=pltpu.SMEM)]
        + [spec(operand) for operand in operands]
        + [pl.BlockSpec(memory_space=pl.ANY)] * len(wait_for),
        out_specs=[pl.BlockSpec(memory_space=pltpu.VMEM)] * (many + 1),
        out_shape=list(outs) + [array(WIDE, 8, 128)],
        scratch_shapes=list(scratch),
        compiler_params=pltpu.CompilerParams(vmem_limit_bytes=limit * MIB),
        cost_estimate=pl.CostEstimate(flops=3 * 10**10, bytes_accessed=MIB, transcendentals=0),
        name=name,
    )(where, *operands, *wait_for)


def array(dtype, *shape):
    return jax.ShapeDtypeStruct(shape, dtype)


def normalize(value):
    center = jnp.mean(value, axis=1, keepdims=True)
    offsets = value - center
    inverse = lax.rsqrt(jnp.mean(offsets * offsets, axis=1, keepdims=True) + norm_eps)
    return offsets * inverse, inverse


def norm_back(grad, unit, inverse, gain):
    scaled = grad * gain
    return inverse * (
        scaled
        - jnp.mean(scaled, axis=1, keepdims=True)
        - unit * jnp.mean(scaled * unit, axis=1, keepdims=True)
    )


def column_sum(value):
    return jnp.sum(value, axis=0, keepdims=True)


def settle_kernel(where, *refs):
    pieces, out = refs[:8], refs[8]
    for core in range(2):
        for item, (x, y, z) in enumerate(ITEMS):
            block = (where[2] + y) % 2 * 2 + (where[3] + core) % 2
            row = (where[0] + 4 - z) % 4 * 2 + (where[1] + x) % 2
            out[block, row] = pieces[core * 4 + item // 4][item % 4]


def settle(where, pieces):
    rows = pieces[0].shape[1]
    whole = call(settle_kernel, "settle", where, pieces, [array(LOW, 4, 8, rows, D)], limit=8)[0]
    return whole.reshape(4, D, D)


def add_kernel(plan, where, *refs):
    count = max(max(pair[0], pair[2]) for pair in plan) + 1
    for out, (left, left_at, right, right_at) in zip(refs[count:], plan):
        out[...] = (
            refs[left][left_at].astype(WIDE) + refs[right][right_at].astype(WIDE)
        ).astype(LOW)


def add(where, operands, plan, wait_for=()):
    outs = []
    for left, left_at, _, _ in plan:
        outs.append(array(LOW, *operands[left].shape[len(left_at) :]))
    return call(partial(add_kernel, plan), "add", where, operands, outs, limit=8, wait_for=wait_for)


def scatter_core(where, parts, *beside, arrived=None):
    if arrived is None:
        arrived = send(parts[1], CORE, *beside)
    plan = [(0, (half, near), 1, (half, near)) for half in (0, 1) for near in (0, 1)]
    return add(where, [parts[0], arrived], plan)


def scatter_far(where, sums, *beside):
    arrived = [send(sums[1], OVER_Y, *beside), send(sums[3], OVER_X, *beside)]
    plan = [(half, (far,), half + 2, (far,)) for half in (0, 1) for far in (0, 1)]
    return add(where, [sums[0], sums[2], *arrived], plan)


def scatter_near(where, sums, *beside, wait_for=()):
    arrived = [send(sums[1], OVER_X, *beside), send(sums[3], OVER_Y, *beside)]
    plan = [(half, (z,), half + 2, (z,)) for half in (0, 1) for z in (0, 1)]
    return add(where, [sums[0], sums[2], *arrived], plan, wait_for)


def scatter_z(sums, *beside):
    return [sums[0]] + [send(sums[s], UP_Z[s], *beside) for s in (1, 2, 3)]


TILE = 2 * HD
HEADS_BLOCK = 3
SIDES = (0, 1, 0)
KEYS = 3 * TILE
OUT = 4 * TILE


def join_columns(query, key, value, out):
    q, v = [[part[:, h * HD : (h + 1) * HD] for h in range(3)] for part in (query, value)]
    return jnp.concatenate([q[0], v[0], v[1], q[1], q[2], v[2], key, out], axis=1)


def query_columns(part):
    return jnp.concatenate([part[:, :HD], part[:, 3 * HD : 5 * HD]], axis=1)


def value_columns(part):
    return jnp.concatenate([part[:, HD : 3 * HD], part[:, 5 * HD : 6 * HD]], axis=1)


def arrange_kernel(where, qkv_ref, out_ref, held):
    parts = [qkv_ref[0], qkv_ref[1], qkv_ref[2], out_ref[...].T]
    held[...] = join_columns(*parts).astype(LOW)


def arrange(where, qkv_weight, out_weight):
    outs = [array(LOW, qkv_weight.shape[1], D)]
    return call(arrange_kernel, "arrange", where, [qkv_weight, out_weight], outs, limit=8)[0]


def arrange_bias_kernel(where, vec_ref, held):
    blocks = held.shape[0]
    width = D // blocks
    none = jnp.zeros((1, width), WIDE)
    for m in range(blocks):
        query = vec_ref[:, m * width : (m + 1) * width]
        value = vec_ref[:, D + m * width : D + (m + 1) * width]
        held[m] = join_columns(query, none, value, none)


def arrange_bias(where, vectors, blocks):
    outs = [array(WIDE, blocks, 1, D)]
    return call(arrange_bias_kernel, "arrange_bias", where, [vectors], outs, limit=8)[0]


def attend_kernel(blocks, chosen, last, where, x_ref, w_ref, bias_ref, vec_ref, seg_ref, *refs):
    if chosen[0] == 0:
        held = None
    else:
        held, refs = refs[0], refs[1:]
    q_out, k_out, v_out, log_out, context_out, *refs = refs
    if last:
        unit_out, inverse_out, low_out, sum_ref = refs
    else:
        (sum_ref,) = refs
    x = x_ref[...]
    lanes = lax.broadcasted_iota(jnp.int32, (L, TILE), 1)
    passage = jnp.broadcast_to(seg_ref[...], (L, TILE))
    sides = []
    for side in SIDES:
        mine = (lanes >= HD) == side
        column = lanes - (0 if side else HD)
        foreign = (column >= 0) & (column < PASS) & (column != passage)
        same = (column >= 0) & (column < PASS) & (column == passage)
        sides.append(
            (
                jnp.where(mine, HD ** (-0.5), 0.0).astype(LOW),
                jnp.where(foreign, masked_value, 0.0).astype(LOW),
                jnp.where(mine, 1.0, 0.0).astype(LOW),
                jnp.where(same, 1.0, 0.0).astype(LOW),
                jnp.where(mine, 0.0, 1.0).astype(LOW),
            )
        )
    sum_ref[...] = held[...] if held is not None else x.astype(WIDE) + vec_ref[:, BO : BO + D]

    def block(i, carry):
        m = block_of(chosen[0] + i, where)
        projected = (dot(x, w_ref[m]) + bias_ref[m]).astype(LOW)
        parts = [jnp.zeros((HD, L), LOW)]
        scores, values = [], []
        for h in range(HEADS_BLOCK):
            q_scale, q_tail, k_scale, k_tail, v_scale = sides[h]
            tile = projected[:, h * TILE : (h + 1) * TILE]
            query = tile * q_scale + q_tail
            at = KEYS + h // 2 * TILE
            keys = projected[:, at : at + TILE] * k_scale + k_tail
            values.append(tile.T[:HD] if SIDES[h] else tile.T[HD:])
            scores.append(dot(keys, query, (1, 1)))
            q_out[i * HEADS_BLOCK + h] = query
            k_out[i * HEADS_BLOCK + h] = keys
            v_out[i * HEADS_BLOCK + h] = tile * v_scale
        for h in range(HEADS_BLOCK):
            highest = jnp.max(scores[h], axis=0, keepdims=True)
            weights = jnp.exp(scores[h] - highest)
            totals = jnp.sum(weights, axis=0, keepdims=True)
            mixed = dot(values[h], weights.astype(LOW)) * (1.0 / totals)
            parts.append(mixed.astype(LOW))
            log_out[i * HEADS_BLOCK + h] = highest + jnp.log(totals)
        context = jnp.concatenate(parts, axis=0).T
        context_out[i] = context
        sum_ref[...] += dot(context, w_ref[m, :, OUT:], (1, 1))
        return carry

    for i in range(len(chosen)):
        block(i, 0)
    if last:
        unit, inverse = normalize(sum_ref[...])
        unit_out[...] = unit
        inverse_out[...] = inverse
        low_out[...] = (unit * vec_ref[:, G1 : G1 + D] + vec_ref[:, C1 : C1 + D]).astype(LOW)


def attend(where, chosen, held, inputs, weight, bias, vectors, segments, wait_for=()):
    blocks = bias.shape[0]
    heads = len(chosen) * HEADS // blocks
    last = chosen[-1] == blocks - 1
    outs = [
        array(LOW, heads, L, TILE),
        array(LOW, heads, L, TILE),
        array(LOW, heads, L, TILE),
        array(WIDE, heads, 1, L),
        array(LOW, len(chosen), L, D - OUT),
    ]
    if last:
        outs += [array(WIDE, L, D), array(WIDE, L, 1), array(LOW, L, D)]
    else:
        outs += [array(WIDE, L, D)]
    return call(
        partial(attend_kernel, blocks, chosen, last),
        "attend",
        where,
        [inputs, weight, bias, vectors, segments] + ([] if held is None else [held]),
        outs,
        [pltpu.VMEM((L, D), WIDE)] if last else [],
        wait_for=wait_for,
    )


def widen_kernel(rows, where, *refs):
    lows, (w_ref, bias_ref, active_out, slope_out) = refs[:rows], refs[rows:]

    def block(m, carry):
        hiddens = [dot(lows[row][...], w_ref[m]) + bias_ref[m] for row in range(rows)]
        for row in range(rows):
            hidden = hiddens[row]
            half = 0.5 * (1.0 + lax.erf(hidden * math.sqrt(0.5)))
            active_out[m, row * L : (row + 1) * L] = (hidden * half).astype(LOW)
            density = jnp.exp(-0.5 * hidden * hidden) * (1.0 / math.sqrt(2.0 * math.pi))
            slope_out[m, row * L : (row + 1) * L] = (half + hidden * density).astype(LOW)
        return carry

    for i in range(w_ref.shape[0]):
        block(i, 0)


def widen(where, lows, weight, bias, wait_for=()):
    blocks = bias.shape[0]
    rows = len(lows)
    return call(
        partial(widen_kernel, rows),
        "widen",
        where,
        [*lows, weight, bias],
        [array(LOW, blocks, rows * L, D)] * 2,
        wait_for=wait_for,
    )


def early_kernel(rows, blocks, where, active_ref, w_ref, vec_ref, starts_ref, *refs):
    units, (cls_out, active_wide, rows_ref, sum_ref) = refs[:rows], refs[rows:]
    few = cls_out.shape[0]
    each = few // rows
    for p in range(few):
        at = pl.ds(starts_ref[p] - p // each * L, 1)
        sum_ref[p : p + 1] = units[p // each][at, :]
    sum_ref[...] = sum_ref[...] * vec_ref[:, G1 : G1 + D] + (
        vec_ref[:, C1 : C1 + D] + vec_ref[:, B2 : B2 + D]
    )
    for m in range(blocks):
        for p in range(few):
            base = pl.multiple_of(starts_ref[p] // 16 * 16, 16)
            active_wide[...] = active_ref[m, pl.ds(base, 16), :].astype(WIDE)
            rows_ref[p : p + 1] = active_wide[pl.ds(starts_ref[p] - base, 1), :]
        sum_ref[...] += dot(rows_ref[...].astype(LOW), w_ref[m], (1, 1))
    unit, _ = normalize(sum_ref[...])
    output = unit * vec_ref[:, G2 : G2 + D] + vec_ref[:, C2 : C2 + D]
    cls_out[...] = output.astype(LOW).astype(WIDE)


def early(where, active, weight, vectors, starts, units):
    few = starts.shape[0]
    return call(
        partial(early_kernel, len(units), active.shape[0]),
        "early",
        where,
        [active, weight, vectors, starts, *units],
        [array(WIDE, few, D)],
        [pltpu.VMEM((16, D), WIDE), pltpu.VMEM((few, D), WIDE), pltpu.VMEM((few, D), WIDE)],
        limit=8,
    )


def narrow_kernel(row, where, active_ref, w_ref, vec_ref, unit_ref, out, unit_out, inverse_out):
    at = slice(row * L, (row + 1) * L)
    value = unit_ref[...] * vec_ref[:, G1 : G1 + D] + (
        vec_ref[:, C1 : C1 + D] + vec_ref[:, B2 : B2 + D]
    )
    for m in range(w_ref.shape[0]):
        value += dot(active_ref[m, at], w_ref[m], (1, 1))
    unit, inverse = normalize(value)
    unit_out[...] = unit
    inverse_out[...] = inverse
    out[...] = (unit * vec_ref[:, G2 : G2 + D] + vec_ref[:, C2 : C2 + D]).astype(LOW)


def narrow(where, row, active, weight, vectors, unit, wait_for=()):
    return call(
        partial(narrow_kernel, row),
        "narrow",
        where,
        [active, weight, vectors, unit],
        [array(LOW, L, D), array(WIDE, L, D), array(WIDE, L, 1)],
        wait_for=wait_for,
    )


def contrast_kernel(
    rows, where, cot_ref, vec_ref, starts_ref, own_ref, all_ref, ids_ref, ids_own_ref,
    partners_own_ref, *refs
):
    units, inverses, refs = refs[:rows], refs[rows : 2 * rows], refs[2 * rows :]
    (grad_out, low_out, bias_out, gain_out, shift_out, y_ref) = refs
    scale = 2.0 / math.sqrt(D)
    everyone = all_ref[...]
    own = own_ref[...].astype(LOW)
    count = everyone.shape[0]
    scores = dot(everyone, everyone, (1, 1)) * scale
    diagonal = lax.broadcasted_iota(jnp.int32, (count, count), 0) == lax.broadcasted_iota(
        jnp.int32, (count, count), 1
    )
    scores = jnp.where(diagonal, masked_value, scores)
    highest = jnp.max(scores, axis=0, keepdims=True)
    log_all = highest + jnp.log(jnp.sum(jnp.exp(scores - highest), axis=0, keepdims=True))
    here = dot(own, everyone, (1, 1)) * scale
    ids = ids_ref[...]
    here = jnp.where(ids_own_ref[...] == ids, masked_value, here)
    top = jnp.max(here, axis=1, keepdims=True)
    log_own = top + jnp.log(jnp.sum(jnp.exp(here - top), axis=1, keepdims=True))
    pair = (partners_own_ref[...] == ids).astype(WIDE)
    out_grad = grid_weight * (jnp.exp(here - log_own) - pair)
    in_grad = grid_weight * (jnp.exp(here - log_all) - pair)
    cls_grad = scale * (dot(out_grad.astype(LOW), everyone) + dot(in_grad.astype(LOW), everyone))
    y_ref[...] = cot_ref[...].astype(WIDE)
    for p in range(cls_grad.shape[0]):
        y_ref[pl.ds(starts_ref[p], 1), :] += cls_grad[p : p + 1]
    for ref in (bias_out, gain_out, shift_out):
        ref[...] = jnp.zeros_like(ref)
    for part in range(y_ref.shape[0] // PART):
        at = slice(part * PART, (part + 1) * PART)
        row, inner = part * PART // L, slice(part * PART % L, part * PART % L + PART)
        grad = y_ref[at]
        unit = units[row][inner]
        gain_out[...] += column_sum(grad * unit)
        shift_out[...] += column_sum(grad)
        back = norm_back(grad, unit, inverses[row][inner], vec_ref[:, G2 : G2 + D])
        grad_out[at] = back
        low = back.astype(LOW)
        low_out[at] = low
        bias_out[...] += column_sum(low.astype(WIDE))


def contrast(where, cotangent, units, inverses, vectors, starts, own, everyone, ids, ids_own, partners_own):
    tokens = cotangent.shape[0]
    return call(
        partial(contrast_kernel, len(units)),
        "contrast",
        where,
        [
            cotangent, vectors, starts, own, everyone, ids, ids_own, partners_own, *units, *inverses,
        ],
        [
            array(WIDE, tokens, D),
            array(LOW, tokens, D),
            array(WIDE, 1, D),
            array(WIDE, 1, D),
            array(WIDE, 1, D),
        ],
        [pltpu.VMEM((tokens, D), WIDE)],
    )


def down_grad_kernel(summand, where, grad_ref, active_ref, *refs):
    outs, turned = refs[:-1], refs[-1]
    turned[...] = grad_ref[...].T
    for g in range(summand.blocks):
        value = dot(turned[...], active_ref[block_of(g, where)]).astype(LOW)
        summand.write(outs, value, g, where)


def grad_of_down(where, grad_low, active, summand):
    tokens = active.shape[1]
    return call(
        partial(down_grad_kernel, summand),
        "grad_of_down",
        where,
        [grad_low, active],
        summand.shapes,
        [pltpu.VMEM((D, tokens), LOW)],
    )


def up_grad_kernel(summand, rows, where, grad_ref, w_ref, slope_ref, *refs):
    lows, (grad_out, bias_out), refs = refs[:rows], refs[rows : rows + 2], refs[rows + 2 :]
    outs, turned = refs[:-1], refs[-1]
    for row in range(rows):
        turned[:, row * L : (row + 1) * L] = lows[row][...].T
    for g in range(summand.blocks):
        m = block_of(g, where)
        bias = jnp.zeros((1, D), WIDE)
        for row in range(rows):
            at = slice(row * L, (row + 1) * L)
            grad = dot(grad_ref[at], w_ref[m]) * slope_ref[m, at].astype(WIDE)
            grad = grad.astype(LOW)
            grad_out[m, at] = grad
            bias += column_sum(grad.astype(WIDE))
        bias_out[m] = bias
        summand.write(outs, dot(turned[...], grad_out[m]).astype(LOW), g, where)


def grad_of_up(where, grad_low, weight, slope, lows, summand, wait_for=()):
    blocks, tokens, _ = slope.shape
    return call(
        partial(up_grad_kernel, summand, len(lows)),
        "grad_of_up",
        where,
        [grad_low, weight, slope, *lows],
        [array(LOW, blocks, tokens, D), array(WIDE, blocks, 1, D)] + summand.shapes,
        [pltpu.VMEM((D, tokens), LOW)],
        wait_for=wait_for,
    )


def middle_kernel(blocks, rows, where, hidden_ref, up_ref, sum_ref, vec_ref, w_ref, *refs):
    units, inverses, refs = refs[:rows], refs[rows : 2 * rows], refs[2 * rows :]
    grad_out, low_out, bias_out, gain_out, shift_out, context_out = refs
    for ref in (bias_out, gain_out, shift_out):
        ref[...] = jnp.zeros_like(ref)
    for row in range(rows):
        at = slice(row * L, (row + 1) * L)
        value = sum_ref[at]
        for m in range(blocks):
            value += dot(hidden_ref[m, at], up_ref[m], (1, 1))
        grad_out[at] = value
        for part in range(L // PART):
            inner = slice(part * PART, (part + 1) * PART)
            outer = slice(row * L + part * PART, row * L + (part + 1) * PART)
            grad = grad_out[outer]
            unit = units[row][inner]
            gain_out[...] += column_sum(grad * unit)
            shift_out[...] += column_sum(grad)
            back = norm_back(grad, unit, inverses[row][inner], vec_ref[:, G1 : G1 + D])
            grad_out[outer] = back
            low = back.astype(LOW)
            low_out[outer] = low
            bias_out[...] += column_sum(low.astype(WIDE))
        for m in range(blocks):
            context_out[row * blocks + m] = dot(
                low_out[at], w_ref[block_of(m, where), :, OUT:]
            ).astype(LOW)


def middle(where, hidden_grad, up, sum_grad, units, inverses, vectors, weight, wait_for=()):
    blocks, tokens, _ = hidden_grad.shape
    rows = len(units)
    return call(
        partial(middle_kernel, blocks, rows),
        "middle",
        where,
        [hidden_grad, up, sum_grad, vectors, weight, *units, *inverses],
        [
            array(WIDE, tokens, D),
            array(LOW, tokens, D),
            array(WIDE, 1, D),
            array(WIDE, 1, D),
            array(WIDE, 1, D),
            array(LOW, rows * blocks, L, D - OUT),
        ],
        wait_for=wait_for,
    )


def attend_back_kernel(blocks, row, chosen, where, q_ref, k_ref, v_ref, log_ref, grad_ref, out):
    lanes = lax.broadcasted_iota(jnp.int32, (L, TILE), 1)
    low_half = lanes < HD

    def block(i, carry):
        key_grads, scores, weight_grads, grads = [], [], [], []
        for h in range(HEADS_BLOCK):
            n = i * HEADS_BLOCK + h
            at = (h + 1) // 2 * TILE
            grads.append(grad_ref[row * blocks + chosen[0] + i, :, at : at + TILE])
            scores.append(dot(k_ref[n], q_ref[n], (1, 1)))
            weight_grads.append(dot(v_ref[n], grads[h], (1, 1)))
        for h in range(HEADS_BLOCK):
            n = i * HEADS_BLOCK + h
            weights = jnp.exp(scores[h] - log_ref[n])
            middle_sum = jnp.sum(weight_grads[h] * weights, axis=0, keepdims=True)
            score_grad = (weights * (weight_grads[h] - middle_sum)).astype(LOW)
            query_grad = (dot(k_ref[n].T, score_grad) * HD ** (-0.5)).T
            value_grad = dot(weights.astype(LOW), grads[h])
            key_grads.append(dot(score_grad, q_ref[n]))
            pair = (value_grad, query_grad) if SIDES[h] else (query_grad, value_grad)
            out[i, :, h * TILE : (h + 1) * TILE] = jnp.where(low_half, *pair).astype(LOW)
        pair = jnp.where(low_half, key_grads[0], key_grads[1])
        out[i, :, KEYS : KEYS + TILE] = pair.astype(LOW)
        out[i, :, OUT : OUT + TILE] = jnp.where(low_half, key_grads[2], 0.0).astype(LOW)
        out[i, :, OUT + TILE :] = jnp.zeros((L, D - OUT - TILE), LOW)
        return carry

    for i in range(len(chosen)):
        block(i, 0)


def attend_back(where, row, blocks, chosen, queries, keys, values, logs, context_grad, wait_for=()):
    return call(
        partial(attend_back_kernel, blocks, row, chosen),
        "attend_back",
        where,
        [queries, keys, values, logs, context_grad],
        [array(LOW, len(chosen), L, D)],
        wait_for=wait_for,
    )


def attention_grad_kernel(summand, rows, chosen, where, x_ref, low_ref, *refs):
    grads, contexts, refs = refs[:rows], refs[rows : 2 * rows], refs[2 * rows :]
    bias_out, outs, (x_turned, low_turned) = refs[0], refs[1:-2], refs[-2:]
    x_turned[...] = x_ref[...].T
    low_turned[...] = low_ref[...].T
    for i, g in enumerate(chosen):
        bias = jnp.zeros((1, D), WIDE)
        value = jnp.zeros((D, D), WIDE)
        own = jnp.zeros((D, D - OUT), WIDE)
        for row in range(rows):
            at = slice(row * L, (row + 1) * L)
            grad = grads[row][i]
            bias += column_sum(grad.astype(WIDE))
            value += dot(x_turned[:, at], grad)
            own += dot(low_turned[:, at], contexts[row][i])
        bias_out[i] = bias
        value = jnp.concatenate([value[:, :OUT], value[:, OUT:] + own], axis=1).astype(LOW)
        summand.write(outs, value, g, where)


def grad_of_attention(where, chosen, inputs, grad_low, grads, contexts, summand, wait_for=()):
    tokens = inputs.shape[0]
    return call(
        partial(attention_grad_kernel, summand, len(grads), chosen),
        "grad_of_attention",
        where,
        [inputs, grad_low, *grads, *contexts],
        [array(WIDE, len(chosen), 1, D)] + summand.shapes[:1],
        [pltpu.VMEM((D, tokens), LOW)] * 2,
        wait_for=wait_for,
    )


def input_grad_kernel(rows, where, w_ref, first_ref, *refs):
    grads, out = refs[:-1], refs[-1]
    cuts = len(grads) // rows
    for row in range(rows):
        at = slice(row * L, (row + 1) * L)
        value = first_ref[at]
        for c in range(cuts):
            ref = grads[row * cuts + c]
            for i in range(ref.shape[0]):
                value += dot(ref[i], w_ref[block_of(c * ref.shape[0] + i, where)], (1, 1))
        out[at] = value


def grad_of_input(where, rows, grads, weight, first_grad, wait_for=()):
    return call(
        partial(input_grad_kernel, rows),
        "grad_of_input",
        where,
        [weight, first_grad, *grads],
        [array(WIDE, *first_grad.shape)],
        wait_for=wait_for,
    )


def pack_kernel(cuts, where, *refs):
    biases, up_ref, others, out = refs[:cuts], refs[cuts], refs[cuts + 1 : -2], refs[-2]
    rows_ref = refs[-1]
    each = biases[0].shape[0]
    blocks = cuts * each
    for g in range(blocks):
        rows_ref[block_of(g, where)] = biases[g // each][g % each]
    rows = [rows_ref[m] for m in range(blocks)]
    out[:, :D] = jnp.concatenate([query_columns(row) for row in rows], axis=1)
    out[:, D : 2 * D] = jnp.concatenate([value_columns(row) for row in rows], axis=1)
    units = FF // blocks
    for m in range(blocks):
        out[:, 2 * D + m * units : 2 * D + (m + 1) * units] = up_ref[m]
    for i, ref in enumerate(others):
        out[:, TAIL + i * D : TAIL + (i + 1) * D] = ref[...]


def pack(where, biases, up_bias_grad, *others):
    blocks = up_bias_grad.shape[0]
    return call(
        partial(pack_kernel, len(biases)),
        "pack",
        where,
        [*biases, up_bias_grad, *others],
        [array(WIDE, 1, VEC)],
        [pltpu.VMEM((blocks, 1, D), WIDE)],
        limit=8,
    )[0]


def ratio_of(grad, first, second):
    moment = beta_decay * first + (1.0 - beta_decay) * grad
    second_new = beta_decay * second + (1.0 - beta_decay) * grad * grad
    ratio = (
        moment
        / (1.0 - beta_decay**STEP)
        / (jnp.sqrt(second_new / (1.0 - beta_decay**STEP)) + adam_eps)
    )
    return second_new, ratio


def squares(value):
    return jnp.sum(jnp.sum(value * value, axis=0, keepdims=True), axis=1, keepdims=True)


def adapt_kernel(cut, parts, where, *refs):
    total_sum = refs[0][...].astype(WIDE)
    for ref in refs[1:parts]:
        total_sum += ref[...].astype(WIDE)
    refs = refs[parts:]
    count = len(cut)
    firsts, seconds, weights = refs[:count], refs[count : 2 * count], refs[2 * count : 3 * count]
    outs = refs[3 * count :]
    lines = []
    for i, pick in enumerate(cut):
        for part, grad in pick(total_sum):
            def at(ref):
                return ref if part is None else ref.at[part]

            second_new, ratio = ratio_of(grad, at(firsts[i])[...], at(seconds[i])[...])
            weight = at(weights[i])[...]
            update = ratio + weight_decay * weight
            at(outs[3 * i])[...] = grad
            at(outs[3 * i + 1])[...] = second_new
            at(outs[3 * i + 2])[...] = update
            lines.append((squares(weight), squares(update)))
    lanes = lax.broadcasted_iota(jnp.int32, (1, 128), 1)
    held = jnp.zeros((1, 128), WIDE)
    for i, (weight_square, update_square) in enumerate(lines):
        held = jnp.where(lanes == 2 * i, weight_square, held)
        held = jnp.where(lanes == 2 * i + 1, update_square, held)
    outs[-1][...] = held


def adapt(name, where, parts, cut, firsts, seconds, weights):
    outs = [array(WIDE, *w.shape) for w in weights for _ in range(3)] + [array(WIDE, 1, 128)]
    operands = [*parts, *firsts, *seconds, *weights]
    return call(
        partial(adapt_kernel, cut, len(parts)),
        name,
        where,
        operands,
        outs,
    )[:-1]


def renew_kernel(counts, where, sums_ref, grad_ref, first_ref, second_ref, vec_ref, *refs):
    many = len(counts)
    weights, updates, outs = refs[:many], refs[many : 2 * many], refs[2 * many :]
    norms = jnp.sqrt(sums_ref[...])
    outs[-1][...] = norms
    slot = 0
    for i, count in enumerate(counts):
        for part in range(count):
            trust = norms[:, 2 * slot : 2 * slot + 1] / (
                norms[:, 2 * slot + 1 : 2 * slot + 2] + norm_guard
            )
            slot += 1

            def at(ref):
                return ref if count == 1 else ref.at[part]

            new = at(weights[i])[...] - rate_matrix * trust * at(updates[i])[...]
            at(outs[2 * i])[...] = new
            at(outs[2 * i + 1])[...] = new.astype(LOW)
    second_new, ratio = ratio_of(grad_ref[...], first_ref[...], second_ref[...])
    outs[-3][...] = second_new
    outs[-2][...] = vec_ref[...] - rate_vector * ratio


def renew(where, sums, vector_grad, vector_first, vector_second, vectors, weights, updates):
    counts = [3 if w.ndim == 3 else 1 for w in weights]
    outs = [array(dtype, *w.shape) for w in weights for dtype in (WIDE, LOW)]
    outs += [array(WIDE, 1, VEC), array(WIDE, 1, VEC), array(WIDE, 1, 128)]
    operands = [sums, vector_grad, vector_first, vector_second, vectors, *weights, *updates]
    return call(
        partial(renew_kernel, counts),
        "renew",
        where,
        operands,
        outs,
    )[:-1]


def shards(
    block_input,
    cotangent,
    lengths,
    partner,
    qkv_weight,
    out_weight,
    up_weight,
    down_weight,
    qkv_first,
    out_first,
    up_first,
    down_first,
    qkv_second,
    out_second,
    up_second,
    down_second,
    vectors,
    vector_first,
    vector_second,
):
    mp_size = lax.axis_size("mp")
    dp_size = lax.axis_size("dp")
    mp_index = lax.axis_index("mp")
    dp_index = lax.axis_index("dp")
    tokens = cotangent.shape[0]
    rows = tokens // L
    own_rows = rows * PASS
    width = D // mp_size
    where = place()
    down_turned = down_weight.T
    weight_shard = arrange(where, qkv_weight, out_weight)
    up_shard = up_weight.astype(LOW)
    down_shard = down_turned.astype(LOW)
    local_lengths = lax.dynamic_slice_in_dim(lengths, mp_index * rows, rows, 0)
    inputs = lax.dynamic_slice_in_dim(block_input, mp_index * tokens, tokens, 0)
    segments = passage_ids(local_lengths).reshape(tokens, 1)
    starts = jnp.cumsum(local_lengths, axis=1) - local_lengths
    starts = (starts + L * jnp.arange(rows, dtype=jnp.int32)[:, None]).reshape(own_rows)
    partner_own = lax.dynamic_slice_in_dim(partner, mp_index * own_rows, own_rows, 0)
    ids_own = (dp_index * mp_size + mp_index) * own_rows + jnp.arange(own_rows, dtype=jnp.int32)
    ids_all = shared_ids(own_rows)
    vec = vectors.reshape(1, VEC)
    bias = arrange_bias(where, vec, mp_size)
    bias_up = vectors[2 * D : TAIL].reshape(mp_size, 1, D)

    summand = Summand(mp_size, dp_size)

    def attend_part(row, chosen, held, weight, *wait_for):
        at = slice(row * L, (row + 1) * L)
        return attend(
            where, chosen, held, inputs[at], weight, bias, vec, segments[at], wait_for=wait_for
        )

    halves = [range(mp_size // 2), range(mp_size // 2, mp_size)]
    if on_grid():
        weight_z = gather_z(weight_shard)
        weight_near = gather_near(weight_z)
        up_z = gather_z(after(up_shard, *weight_z))
        weight_far = gather_far(weight_near)
        weight_parts = weight_near + weight_far
        weight = settle(where, weight_parts + gather_core(weight_parts))
        up_z = after(up_z, *weight_far)
        kept = [[None, None] for _ in range(rows)]
        kept[0][0] = attend_part(0, halves[0], None, weight, *up_z)
        up_near = gather_near(up_z, kept[0][0][-1])
        down_z = gather_z(after(down_shard, kept[0][0][-1]), kept[0][0][-1])
        kept[0][1] = attend_part(0, halves[1], kept[0][0][5], weight, *up_near)
        kept[1][0] = attend_part(1, halves[0], None, weight, kept[0][1][-1], *down_z)
        up_far = gather_far(up_near, kept[1][0][-1])
        up_cores = gather_core(up_near, kept[1][0][-1])
        down_near = gather_near(after(down_z, *up_near), kept[1][0][-1])
        kept[1][1] = attend_part(1, halves[1], kept[1][0][5], weight, *up_far)
        up_cores += gather_core(up_far, kept[1][1][-1])
        up = settle(where, up_near + up_far + up_cores)
    else:
        weight = gather_plain(weight_shard)
        up = gather_plain(up_shard)
        down_near = []
        kept = []
        for row in range(rows):
            first = attend_part(row, halves[0], None, weight)
            kept.append([first, attend_part(row, halves[1], first[5], weight)])
    units_first, inverses_first, lows = zip(*[kept[row][1][5:8] for row in range(rows)])
    active, slope, widened = widen(where, lows, up, bias_up, wait_for=down_near)
    if on_grid():
        down_far = gather_far(after(down_near, *up_far), widened)
        down_cores = gather_core(down_near, widened) + gather_core(down_far)
        down = settle(where, down_near + down_far + down_cores)
    else:
        down = gather_plain(down_shard)
    cls_own, ended = early(where, active, down, vec, starts, units_first)
    narrowed = []
    if on_grid():
        rounds = share_core(cls_own.astype(LOW))
        narrowed.append(narrow(where, 0, active, down, vec, units_first[0], (ended, rounds)))
        rounds = share_plane(rounds, narrowed[0][-1])
        narrowed.append(narrow(where, 1, active, down, vec, units_first[1], (rounds,)))
        cls_all = share_line(rounds, narrowed[1][-1])
    else:
        for row in range(rows):
            narrowed.append(narrow(where, row, active, down, vec, units_first[row]))
        cls_all = share_plain(cls_own.astype(LOW))
    outputs, units_second, inverses_second, _ = zip(*narrowed)
    block_output = jnp.concatenate(outputs, axis=0)
    sum_grad, branch_low, down_bias_grad, gain_second_grad, shift_second_grad, _ = contrast(
        where, cotangent, units_second, inverses_second, vec, starts, cls_own, cls_all,
        ids_all[None, :], ids_own[:, None], partner_own[:, None],
    )
    *down_part, ended = grad_of_down(where, branch_low, active, summand)
    hidden_grad, up_bias_grad, *up_part, _ = grad_of_up(
        where, branch_low, down, slope, lows, summand, wait_for=(ended,)
    )
    if on_grid():
        *down_sum, added = scatter_core(where, down_part)
    (
        first_grad, attended_low, out_bias_grad, gain_first_grad, shift_first_grad, context_grad, _,
    ) = middle(
        where, hidden_grad, up, sum_grad, units_first, inverses_first, vec, weight,
        wait_for=(added,) if on_grid() else (),
    )

    def back_part(row, half, *wait_for):
        return attend_back(
            where, row, mp_size, halves[half], *kept[row][half][:4], context_grad, wait_for=wait_for
        )

    def grad_part(half, *wait_for):
        return grad_of_attention(
            where, halves[half], inputs, attended_low, [back[row][half] for row in range(rows)],
            [kept[row][half][4] for row in range(rows)], summand, wait_for=wait_for,
        )

    back = [[None, None] for _ in range(rows)]
    if on_grid():
        *down_sum, down_added = scatter_far(where, down_sum)
        *up_sum, up_added = scatter_core(where, up_part)
        back[0][1], ended = back_part(0, 1, down_added, up_added)
        back[1][1], ended = back_part(1, 1, ended)
        bias_other, other_part, ended = grad_part(1)
        *down_sum, down_added = scatter_near(where, down_sum, ended)
        back[0][0], ended = back_part(0, 0, ended, down_added)
        *up_sum, up_added = scatter_far(where, up_sum, ended)
        other_part = send(other_part, CORE)
        back[1][0], ended = back_part(1, 0, up_added, other_part)
        bias_own, own_part, ended = grad_part(0)
        *attention_sum, added = scatter_core(where, [own_part], arrived=other_part)
        *up_sum, up_added = scatter_near(where, up_sum, ended, wait_for=(added,))
    else:
        for row in range(rows):
            for half in (0, 1):
                back[row][half] = back_part(row, half)[0]
        bias_other, other_part, _ = grad_part(1)
        bias_own, own_part, _ = grad_part(0)
    vector_local = pack(
        where,
        [bias_own, bias_other],
        up_bias_grad,
        out_bias_grad,
        down_bias_grad,
        gain_first_grad,
        shift_first_grad,
        gain_second_grad,
        shift_second_grad,
    )
    grads = [back[row][half] for row in range(rows) for half in (0, 1)]
    if on_grid():
        input_grad, ended = grad_of_input(
            where, rows, grads, weight, first_grad, wait_for=(added, up_added)
        )
        *attention_sum, _ = scatter_far(where, attention_sum, ended)
        *attention_sum, ended = scatter_near(where, attention_sum)
        down_parts, up_parts = [list(p) for p in scatter_z_both(down_sum, up_sum, ended)]
        attention_parts = scatter_z(attention_sum)
    else:
        down_parts = [scatter_plain(down_part)]
        up_parts = [scatter_plain(up_part)]
        both = jnp.concatenate([own_part[: mp_size // 2], other_part[mp_size // 2 :]])
        attention_parts = [scatter_plain([both])]
        input_grad, _ = grad_of_input(where, rows, grads, weight, first_grad)
    down_grad, down_second_new, down_update, down_squares = adapt(
        "adapt_down", where, down_parts, [lambda g: [(None, g)]],
        [down_first.T], [down_second.T], [down_turned],
    )
    up_grad, up_second_new, up_update, up_squares = adapt(
        "adapt_up", where, up_parts, [lambda g: [(None, g)]], [up_first], [up_second], [up_weight]
    )
    (
        qkv_grad, qkv_second_new, qkv_update,
        out_grad, out_second_new, out_update, attention_squares,
    ) = adapt(
        "adapt_attention",
        where,
        attention_parts,
        [
            lambda g: [
                (0, query_columns(g)),
                (1, g[:, KEYS : KEYS + width]),
                (2, value_columns(g)),
            ],
            lambda g: [(None, g[:, KEYS + width :].T)],
        ],
        [qkv_first, out_first],
        [qkv_second, out_second],
        [qkv_weight, out_weight],
    )
    summed = total(
        jnp.concatenate(
            [
                vector_local,
                attention_squares[:, :8],
                up_squares[:, :2],
                down_squares[:, :2],
                jnp.zeros((1, 116), WIDE),
            ],
            axis=1,
        )
    )
    vector_grad, sums = summed[:, :VEC], summed[:, VEC:]
    weights = [qkv_weight, out_weight, up_weight, down_turned]
    updates = [qkv_update, out_update, up_update, down_update]
    (
        qkv_new, qkv_copy, out_new, out_copy, up_new, up_copy, down_new, down_copy,
        vector_second_new, vector_new, norms,
    ) = renew(
        where, sums, vector_grad, vector_first.reshape(1, VEC), vector_second.reshape(1, VEC), vec,
        weights, updates,
    )
    return (
        block_output,
        input_grad,
        qkv_grad,
        out_grad,
        up_grad,
        down_grad.T,
        qkv_second_new,
        out_second_new,
        up_second_new,
        down_second_new.T,
        qkv_new,
        out_new,
        up_new,
        down_new.T,
        qkv_copy,
        out_copy,
        up_copy,
        down_copy.T,
        vector_grad.reshape(VEC),
        vector_second_new.reshape(VEC),
        vector_new.reshape(VEC),
        norms[0, :12].reshape(6, 2),
    )


def solution(mesh):
    in_specs = (
        P("dp", None),
        P(("dp", "mp"), None),
        P("dp", None),
        P("dp"),
        P(None, "dp", "mp"),
        P("mp", "dp"),
        P("dp", "mp"),
        P("mp", "dp"),
        P(None, "dp", "mp"),
        P("mp", "dp"),
        P("dp", "mp"),
        P("mp", "dp"),
        P(None, "dp", "mp"),
        P("mp", "dp"),
        P("dp", "mp"),
        P("mp", "dp"),
        P(),
        P(),
        P(),
    )
    out_specs = (
        P(("dp", "mp"), None),
        P(("dp", "mp"), None),
        P(None, "dp", "mp"),
        P("mp", "dp"),
        P("dp", "mp"),
        P("mp", "dp"),
        P(None, "dp", "mp"),
        P("mp", "dp"),
        P("dp", "mp"),
        P("mp", "dp"),
        P(None, "dp", "mp"),
        P("mp", "dp"),
        P("dp", "mp"),
        P("mp", "dp"),
        P(None, "dp", "mp"),
        P("mp", "dp"),
        P("dp", "mp"),
        P("mp", "dp"),
        P(),
        P(),
        P(),
        P(),
    )
    return jax.shard_map(shards, mesh=mesh, in_specs=in_specs, out_specs=out_specs, check_vma=False)
```

```python
from functools import partial
import math

import jax
import jax.numpy as jnp
from jax import lax
from jax.experimental import pallas as pl
from jax.experimental.pallas import tpu as pltpu
from jax.sharding import PartitionSpec as P

D = 768
HEADS = 12
HD = 64
FF = 3072
L = 512
PASS = 4
STEP = 10
ROWS_DEV = 8
MIB = 1 << 20
PART = 256
TAIL = 2 * D + FF


masked_value = -1e30
grid_weight = 4.0
norm_eps = 1e-12
beta_decay = 0.5
adam_eps = 1e-06
norm_guard = 1e-06
weight_decay = 0.01
rate_matrix = 1.0
rate_vector = 0.2


def passage_ids(lengths):
    starts = jnp.cumsum(lengths, axis=1) - lengths
    positions = jnp.arange(L, dtype=jnp.int32)
    return jnp.sum((positions[None, :, None] >= starts[:, None, :]).astype(jnp.int32), axis=2) - 1


AXES = ("dp", "mp")
GRID = (8, 4)


def links(move):
    pairs = []
    for z in range(4):
        for x in range(2):
            for y in range(2):
                for c in range(2):
                    tz, tx, ty, tc = move(z, x, y, c)
                    pairs.append(
                        ((z * 2 + x) * 4 + y * 2 + c, (tz % 4 * 2 + tx) * 4 + ty * 2 + tc)
                    )
    return pairs


CORE = links(lambda z, x, y, c: (z, x, y, 1 - c))
OVER_X = links(lambda z, x, y, c: (z, 1 - x, y, c))
OVER_Y = links(lambda z, x, y, c: (z, x, 1 - y, c))
OVER_XY = links(lambda z, x, y, c: (z, 1 - x, 1 - y, c))
UP_Z = [links(lambda z, x, y, c, s=s: (z + s, x, y, c)) for s in range(4)]


def after(value, *earlier):
    return lax.optimization_barrier((value, earlier))[0] if earlier else value


def send(value, pairs, *beside):
    return after(lax.ppermute(value, AXES, pairs), *beside)


def on_grid():
    return (lax.axis_size("dp"), lax.axis_size("mp")) == GRID


def place():
    dp_index = lax.axis_index("dp")
    mp_index = lax.axis_index("mp")
    return jnp.stack([dp_index // 2, dp_index % 2, mp_index // 2, mp_index % 2, mp_index])


ITEMS = (
    [(x, 0, z) for x in (0, 1) for z in (0, 1)]
    + [(0, y, z) for y in (0, 1) for z in (2, 3)]
    + [(x, 1, z) for x in (0, 1) for z in (0, 1)]
    + [(1, y, z) for y in (0, 1) for z in (2, 3)]
)


def gather_z(shard, *beside):
    return [shard] + [send(shard, UP_Z[s], *beside) for s in (1, 2, 3)]


def gather_near(parts, *beside):
    first, second = jnp.stack(parts[:2]), jnp.stack(parts[2:])
    return [
        jnp.concatenate([first, send(first, OVER_X, *beside)]),
        jnp.concatenate([second, send(second, OVER_Y, *beside)]),
    ]


def gather_far(near, *beside):
    return [send(near[0], OVER_Y, *beside), send(near[1], OVER_X, *beside)]


def gather_core(parts, *beside):
    return [send(part, CORE, *beside) for part in parts]


def gather_plain(shard):
    mp_size = lax.axis_size("mp")
    return lax.all_gather(shard, ("mp", "dp"), axis=0, tiled=True).reshape(mp_size, D, D)


def block_of(g, where):
    if not on_grid():
        return g
    return ((where[2] + g % 2) % 2) * 2 + (where[3] + g // 2) % 2


def scatter_z_both(left, right, *beside):
    parts = [(left[0], right[0])]
    for s in (1, 2, 3):
        pair = send(jnp.stack([left[s], right[s]]), UP_Z[s], *beside)
        parts.append((pair[0], pair[1]))
    return zip(*parts)


def scatter_plain(parts):
    whole = parts[0]
    return lax.psum_scatter(
        whole.reshape(-1, whole.shape[-1]), ("mp", "dp"), scatter_dimension=0, tiled=True
    )


class Summand:
    def __init__(self, blocks, dp_size):
        rows = D // dp_size
        self.groups = dp_size
        self.rows = rows
        self.blocks = blocks
        self.split = on_grid()
        if self.split:
            self.shapes = [jax.ShapeDtypeStruct((2, 2, 2, 2, rows, D), jnp.bfloat16)] * 2
        else:
            self.shapes = [jax.ShapeDtypeStruct((blocks, D, D), jnp.bfloat16)]

    def write(self, outs, value, g, where):
        if not self.split:
            outs[0][g] = value
            return
        core, y = g // 2, g % 2
        for index in range(self.groups):
            x = (index % 2 + where[1]) % 2
            z = (index // 2 + 4 - where[0]) % 4
            half = z // 2
            over_y = half == 0
            first, second = jnp.where(over_y, y, x), jnp.where(over_y, x, y)
            outs[core % len(outs)][half, first, second, z % 2] = value[
                index * self.rows : (index + 1) * self.rows
            ]


def share_plain(value):
    whole = lax.all_gather(value, AXES, axis=0, tiled=True)
    own = lax.axis_index("dp") * lax.axis_size("mp") + lax.axis_index("mp")
    return jnp.roll(whole, -own * value.shape[0], axis=0)


def share_core(value, *beside):
    return jnp.concatenate([value, send(value, CORE, *beside)])


def share_plane(value, *beside):
    sides = [send(value, pairs, *beside) for pairs in (OVER_X, OVER_Y, OVER_XY)]
    return jnp.concatenate([value] + sides)


def share_line(value, *beside):
    return jnp.concatenate([value] + [send(value, UP_Z[s], *beside) for s in (1, 2, 3)])


def shared_ids(own_rows):
    dp_size, mp_size = lax.axis_size("dp"), lax.axis_size("mp")
    dp_index, mp_index = lax.axis_index("dp"), lax.axis_index("mp")
    count = dp_size * mp_size * own_rows
    n = jnp.arange(count, dtype=jnp.int32)
    if not on_grid():
        return (n + (dp_index * mp_size + mp_index) * own_rows) % count
    item = n // own_rows
    core, side, up = item % 2, item // 2 % 4, item // 8
    z, x = (dp_index // 2 + 4 - up) % 4, (dp_index + side) % 2
    y, c = (mp_index // 2 + side // 2) % 2, (mp_index + core) % 2
    return ((z * 2 + x) * mp_size + y * 2 + c) * own_rows + n % own_rows


def total(value):
    if not on_grid():
        return lax.psum(value, AXES)
    value = value + send(value, CORE)
    value = value + sum(send(value, pairs) for pairs in (OVER_X, OVER_Y, OVER_XY))
    return value + sum(send(value, UP_Z[s]) for s in (1, 2, 3))


LOW = jnp.bfloat16
WIDE = jnp.float32
B1, BO, B2, G1, C1, G2, C2 = 2 * D, TAIL, TAIL + D, TAIL + 2 * D, TAIL + 3 * D, TAIL + 4 * D, TAIL + 5 * D
VEC = 8 * D + FF


def dot(left, right, over=(1, 0)):
    return lax.dot_general(
        left, right, (((over[0],), (over[1],)), ((), ())), preferred_element_type=WIDE
    )


def call(kernel, name, where, operands, outs, scratch=(), limit=14, wait_for=()):
    count = len(operands)
    many = len(outs)

    def body(where, *refs):
        results = refs[count + len(wait_for) :]
        results[many][...] = jnp.zeros((8, 128), WIDE)
        kernel(where, *refs[:count], *results[:many], *results[many + 1 :])

    def spec(operand):
        integers = operand.dtype == jnp.int32 and operand.ndim == 1
        return pl.BlockSpec(memory_space=pltpu.SMEM if integers else pltpu.VMEM)

    return pl.pallas_call(
        body,
        in_specs=[pl.BlockSpec(memory_space=pltpu.SMEM)]
        + [spec(operand) for operand in operands]
        + [pl.BlockSpec(memory_space=pl.ANY)] * len(wait_for),
        out_specs=[pl.BlockSpec(memory_space=pltpu.VMEM)] * (many + 1),
        out_shape=list(outs) + [array(WIDE, 8, 128)],
        scratch_shapes=list(scratch),
        compiler_params=pltpu.CompilerParams(vmem_limit_bytes=limit * MIB),
        cost_estimate=pl.CostEstimate(flops=3 * 10**10, bytes_accessed=MIB, transcendentals=0),
        name=name,
    )(where, *operands, *wait_for)


def array(dtype, *shape):
    return jax.ShapeDtypeStruct(shape, dtype)


def normalize(value):
    center = jnp.mean(value, axis=1, keepdims=True)
    offsets = value - center
    inverse = lax.rsqrt(jnp.mean(offsets * offsets, axis=1, keepdims=True) + norm_eps)
    return offsets * inverse, inverse


def norm_back(grad, unit, inverse, gain):
    scaled = grad * gain
    return inverse * (
        scaled
        - jnp.mean(scaled, axis=1, keepdims=True)
        - unit * jnp.mean(scaled * unit, axis=1, keepdims=True)
    )


def column_sum(value):
    return jnp.sum(value, axis=0, keepdims=True)


def settle_kernel(where, *refs):
    pieces, out = refs[:8], refs[8]
    for core in range(2):
        for item, (x, y, z) in enumerate(ITEMS):
            block = (where[2] + y) % 2 * 2 + (where[3] + core) % 2
            row = (where[0] + 4 - z) % 4 * 2 + (where[1] + x) % 2
            out[block, row] = pieces[core * 4 + item // 4][item % 4]


def settle(where, pieces):
    rows = pieces[0].shape[1]
    whole = call(settle_kernel, "settle", where, pieces, [array(LOW, 4, 8, rows, D)], limit=8)[0]
    return whole.reshape(4, D, D)


def add_kernel(plan, where, *refs):
    count = max(max(pair[0], pair[2]) for pair in plan) + 1
    for out, (left, left_at, right, right_at) in zip(refs[count:], plan):
        out[...] = (
            refs[left][left_at].astype(WIDE) + refs[right][right_at].astype(WIDE)
        ).astype(LOW)


def add(where, operands, plan, wait_for=()):
    outs = []
    for left, left_at, _, _ in plan:
        outs.append(array(LOW, *operands[left].shape[len(left_at) :]))
    return call(partial(add_kernel, plan), "add", where, operands, outs, limit=8, wait_for=wait_for)


def scatter_core(where, parts, *beside, arrived=None):
    if arrived is None:
        arrived = send(parts[1], CORE, *beside)
    plan = [(0, (half, near), 1, (half, near)) for half in (0, 1) for near in (0, 1)]
    return add(where, [parts[0], arrived], plan)


def scatter_far(where, sums, *beside):
    arrived = [send(sums[1], OVER_Y, *beside), send(sums[3], OVER_X, *beside)]
    plan = [(half, (far,), half + 2, (far,)) for half in (0, 1) for far in (0, 1)]
    return add(where, [sums[0], sums[2], *arrived], plan)


def scatter_near(where, sums, *beside, wait_for=()):
    arrived = [send(sums[1], OVER_X, *beside), send(sums[3], OVER_Y, *beside)]
    plan = [(half, (z,), half + 2, (z,)) for half in (0, 1) for z in (0, 1)]
    return add(where, [sums[0], sums[2], *arrived], plan, wait_for)


def scatter_z(sums, *beside):
    return [sums[0]] + [send(sums[s], UP_Z[s], *beside) for s in (1, 2, 3)]


TILE = 2 * HD
HEADS_BLOCK = 3
SIDES = (0, 1, 0)
KEYS = 3 * TILE
OUT = 4 * TILE


def join_columns(query, key, value, out):
    q, v = [[part[:, h * HD : (h + 1) * HD] for h in range(3)] for part in (query, value)]
    return jnp.concatenate([q[0], v[0], v[1], q[1], q[2], v[2], key, out], axis=1)


def query_columns(part):
    return jnp.concatenate([part[:, :HD], part[:, 3 * HD : 5 * HD]], axis=1)


def value_columns(part):
    return jnp.concatenate([part[:, HD : 3 * HD], part[:, 5 * HD : 6 * HD]], axis=1)


def arrange_kernel(where, qkv_ref, out_ref, held):
    parts = [qkv_ref[0], qkv_ref[1], qkv_ref[2], out_ref[...].T]
    held[...] = join_columns(*parts).astype(LOW)


def arrange(where, qkv_weight, out_weight):
    outs = [array(LOW, qkv_weight.shape[1], D)]
    return call(arrange_kernel, "arrange", where, [qkv_weight, out_weight], outs, limit=8)[0]


def arrange_bias_kernel(where, vec_ref, held):
    blocks = held.shape[0]
    width = D // blocks
    none = jnp.zeros((1, width), WIDE)
    for m in range(blocks):
        query = vec_ref[:, m * width : (m + 1) * width]
        value = vec_ref[:, D + m * width : D + (m + 1) * width]
        held[m] = join_columns(query, none, value, none)


def arrange_bias(where, vectors, blocks):
    outs = [array(WIDE, blocks, 1, D)]
    return call(arrange_bias_kernel, "arrange_bias", where, [vectors], outs, limit=8)[0]


def attend_kernel(blocks, chosen, last, where, x_ref, w_ref, bias_ref, vec_ref, seg_ref, *refs):
    if chosen[0] == 0:
        held = None
    else:
        held, refs = refs[0], refs[1:]
    q_out, k_out, v_out, log_out, context_out, *refs = refs
    if last:
        unit_out, inverse_out, low_out, sum_ref = refs
    else:
        (sum_ref,) = refs
    x = x_ref[...]
    lanes = lax.broadcasted_iota(jnp.int32, (L, TILE), 1)
    passage = jnp.broadcast_to(seg_ref[...], (L, TILE))
    sides = []
    for side in SIDES:
        mine = (lanes >= HD) == side
        column = lanes - (0 if side else HD)
        foreign = (column >= 0) & (column < PASS) & (column != passage)
        same = (column >= 0) & (column < PASS) & (column == passage)
        sides.append(
            (
                jnp.where(mine, HD ** (-0.5), 0.0).astype(LOW),
                jnp.where(foreign, masked_value, 0.0).astype(LOW),
                jnp.where(mine, 1.0, 0.0).astype(LOW),
                jnp.where(same, 1.0, 0.0).astype(LOW),
                jnp.where(mine, 0.0, 1.0).astype(LOW),
            )
        )
    sum_ref[...] = held[...] if held is not None else x.astype(WIDE) + vec_ref[:, BO : BO + D]

    def block(i, carry):
        m = block_of(chosen[0] + i, where)
        projected = (dot(x, w_ref[m]) + bias_ref[m]).astype(LOW)
        parts = [jnp.zeros((HD, L), LOW)]
        scores, values = [], []
        for h in range(HEADS_BLOCK):
            q_scale, q_tail, k_scale, k_tail, v_scale = sides[h]
            tile = projected[:, h * TILE : (h + 1) * TILE]
            query = tile * q_scale + q_tail
            at = KEYS + h // 2 * TILE
            keys = projected[:, at : at + TILE] * k_scale + k_tail
            values.append(tile.T[:HD] if SIDES[h] else tile.T[HD:])
            scores.append(dot(keys, query, (1, 1)))
            q_out[i * HEADS_BLOCK + h] = query
            k_out[i * HEADS_BLOCK + h] = keys
            v_out[i * HEADS_BLOCK + h] = tile * v_scale
        for h in range(HEADS_BLOCK):
            highest = jnp.max(scores[h], axis=0, keepdims=True)
            weights = jnp.exp(scores[h] - highest)
            totals = jnp.sum(weights, axis=0, keepdims=True)
            mixed = dot(values[h], weights.astype(LOW)) * (1.0 / totals)
            parts.append(mixed.astype(LOW))
            log_out[i * HEADS_BLOCK + h] = highest + jnp.log(totals)
        context = jnp.concatenate(parts, axis=0).T
        context_out[i] = context
        sum_ref[...] += dot(context, w_ref[m, :, OUT:], (1, 1))
        return carry

    for i in range(len(chosen)):
        block(i, 0)
    if last:
        unit, inverse = normalize(sum_ref[...])
        unit_out[...] = unit
        inverse_out[...] = inverse
        low_out[...] = (unit * vec_ref[:, G1 : G1 + D] + vec_ref[:, C1 : C1 + D]).astype(LOW)


def attend(where, chosen, held, inputs, weight, bias, vectors, segments, wait_for=()):
    blocks = bias.shape[0]
    heads = len(chosen) * HEADS // blocks
    last = chosen[-1] == blocks - 1
    outs = [
        array(LOW, heads, L, TILE),
        array(LOW, heads, L, TILE),
        array(LOW, heads, L, TILE),
        array(WIDE, heads, 1, L),
        array(LOW, len(chosen), L, D - OUT),
    ]
    if last:
        outs += [array(WIDE, L, D), array(WIDE, L, 1), array(LOW, L, D)]
    else:
        outs += [array(WIDE, L, D)]
    return call(
        partial(attend_kernel, blocks, chosen, last),
        "attend",
        where,
        [inputs, weight, bias, vectors, segments] + ([] if held is None else [held]),
        outs,
        [pltpu.VMEM((L, D), WIDE)] if last else [],
        wait_for=wait_for,
    )


def widen_kernel(rows, where, *refs):
    lows, (w_ref, bias_ref, active_out, slope_out) = refs[:rows], refs[rows:]

    def block(m, carry):
        hiddens = [dot(lows[row][...], w_ref[m]) + bias_ref[m] for row in range(rows)]
        for row in range(rows):
            hidden = hiddens[row]
            half = 0.5 * (1.0 + lax.erf(hidden * math.sqrt(0.5)))
            active_out[m, row * L : (row + 1) * L] = (hidden * half).astype(LOW)
            density = jnp.exp(-0.5 * hidden * hidden) * (1.0 / math.sqrt(2.0 * math.pi))
            slope_out[m, row * L : (row + 1) * L] = (half + hidden * density).astype(LOW)
        return carry

    for i in range(w_ref.shape[0]):
        block(i, 0)


def widen(where, lows, weight, bias, wait_for=()):
    blocks = bias.shape[0]
    rows = len(lows)
    return call(
        partial(widen_kernel, rows),
        "widen",
        where,
        [*lows, weight, bias],
        [array(LOW, blocks, rows * L, D)] * 2,
        wait_for=wait_for,
    )


def early_kernel(rows, blocks, where, active_ref, w_ref, vec_ref, starts_ref, *refs):
    units, (cls_out, active_wide, rows_ref, sum_ref) = refs[:rows], refs[rows:]
    few = cls_out.shape[0]
    each = few // rows
    for p in range(few):
        at = pl.ds(starts_ref[p] - p // each * L, 1)
        sum_ref[p : p + 1] = units[p // each][at, :]
    sum_ref[...] = sum_ref[...] * vec_ref[:, G1 : G1 + D] + (
        vec_ref[:, C1 : C1 + D] + vec_ref[:, B2 : B2 + D]
    )
    for m in range(blocks):
        for p in range(few):
            base = pl.multiple_of(starts_ref[p] // 16 * 16, 16)
            active_wide[...] = active_ref[m, pl.ds(base, 16), :].astype(WIDE)
            rows_ref[p : p + 1] = active_wide[pl.ds(starts_ref[p] - base, 1), :]
        sum_ref[...] += dot(rows_ref[...].astype(LOW), w_ref[m], (1, 1))
    unit, _ = normalize(sum_ref[...])
    output = unit * vec_ref[:, G2 : G2 + D] + vec_ref[:, C2 : C2 + D]
    cls_out[...] = output.astype(LOW).astype(WIDE)


def early(where, active, weight, vectors, starts, units):
    few = starts.shape[0]
    return call(
        partial(early_kernel, len(units), active.shape[0]),
        "early",
        where,
        [active, weight, vectors, starts, *units],
        [array(WIDE, few, D)],
        [pltpu.VMEM((16, D), WIDE), pltpu.VMEM((few, D), WIDE), pltpu.VMEM((few, D), WIDE)],
        limit=8,
    )


def narrow_kernel(row, where, active_ref, w_ref, vec_ref, unit_ref, out, unit_out, inverse_out):
    at = slice(row * L, (row + 1) * L)
    value = unit_ref[...] * vec_ref[:, G1 : G1 + D] + (
        vec_ref[:, C1 : C1 + D] + vec_ref[:, B2 : B2 + D]
    )
    for m in range(w_ref.shape[0]):
        value += dot(active_ref[m, at], w_ref[m], (1, 1))
    unit, inverse = normalize(value)
    unit_out[...] = unit
    inverse_out[...] = inverse
    out[...] = (unit * vec_ref[:, G2 : G2 + D] + vec_ref[:, C2 : C2 + D]).astype(LOW)


def narrow(where, row, active, weight, vectors, unit, wait_for=()):
    return call(
        partial(narrow_kernel, row),
        "narrow",
        where,
        [active, weight, vectors, unit],
        [array(LOW, L, D), array(WIDE, L, D), array(WIDE, L, 1)],
        wait_for=wait_for,
    )


def contrast_kernel(
    rows, where, cot_ref, vec_ref, starts_ref, own_ref, all_ref, ids_ref, ids_own_ref,
    partners_own_ref, *refs
):
    units, inverses, refs = refs[:rows], refs[rows : 2 * rows], refs[2 * rows :]
    (grad_out, low_out, bias_out, gain_out, shift_out, y_ref) = refs
    scale = 2.0 / math.sqrt(D)
    everyone = all_ref[...]
    own = own_ref[...].astype(LOW)
    count = everyone.shape[0]
    scores = dot(everyone, everyone, (1, 1)) * scale
    diagonal = lax.broadcasted_iota(jnp.int32, (count, count), 0) == lax.broadcasted_iota(
        jnp.int32, (count, count), 1
    )
    scores = jnp.where(diagonal, masked_value, scores)
    highest = jnp.max(scores, axis=0, keepdims=True)
    log_all = highest + jnp.log(jnp.sum(jnp.exp(scores - highest), axis=0, keepdims=True))
    here = dot(own, everyone, (1, 1)) * scale
    ids = ids_ref[...]
    here = jnp.where(ids_own_ref[...] == ids, masked_value, here)
    top = jnp.max(here, axis=1, keepdims=True)
    log_own = top + jnp.log(jnp.sum(jnp.exp(here - top), axis=1, keepdims=True))
    pair = (partners_own_ref[...] == ids).astype(WIDE)
    out_grad = grid_weight * (jnp.exp(here - log_own) - pair)
    in_grad = grid_weight * (jnp.exp(here - log_all) - pair)
    cls_grad = scale * (dot(out_grad.astype(LOW), everyone) + dot(in_grad.astype(LOW), everyone))
    y_ref[...] = cot_ref[...].astype(WIDE)
    for p in range(cls_grad.shape[0]):
        y_ref[pl.ds(starts_ref[p], 1), :] += cls_grad[p : p + 1]
    for ref in (bias_out, gain_out, shift_out):
        ref[...] = jnp.zeros_like(ref)
    for part in range(y_ref.shape[0] // PART):
        at = slice(part * PART, (part + 1) * PART)
        row, inner = part * PART // L, slice(part * PART % L, part * PART % L + PART)
        grad = y_ref[at]
        unit = units[row][inner]
        gain_out[...] += column_sum(grad * unit)
        shift_out[...] += column_sum(grad)
        back = norm_back(grad, unit, inverses[row][inner], vec_ref[:, G2 : G2 + D])
        grad_out[at] = back
        low = back.astype(LOW)
        low_out[at] = low
        bias_out[...] += column_sum(low.astype(WIDE))


def contrast(where, cotangent, units, inverses, vectors, starts, own, everyone, ids, ids_own, partners_own):
    tokens = cotangent.shape[0]
    return call(
        partial(contrast_kernel, len(units)),
        "contrast",
        where,
        [
            cotangent, vectors, starts, own, everyone, ids, ids_own, partners_own, *units, *inverses,
        ],
        [
            array(WIDE, tokens, D),
            array(LOW, tokens, D),
            array(WIDE, 1, D),
            array(WIDE, 1, D),
            array(WIDE, 1, D),
        ],
        [pltpu.VMEM((tokens, D), WIDE)],
    )


def down_grad_kernel(summand, where, grad_ref, active_ref, *refs):
    outs, turned = refs[:-1], refs[-1]
    turned[...] = grad_ref[...].T
    for g in range(summand.blocks):
        value = dot(turned[...], active_ref[block_of(g, where)]).astype(LOW)
        summand.write(outs, value, g, where)


def grad_of_down(where, grad_low, active, summand):
    tokens = active.shape[1]
    return call(
        partial(down_grad_kernel, summand),
        "grad_of_down",
        where,
        [grad_low, active],
        summand.shapes,
        [pltpu.VMEM((D, tokens), LOW)],
    )


def up_grad_kernel(summand, rows, where, grad_ref, w_ref, slope_ref, *refs):
    lows, (grad_out, bias_out), refs = refs[:rows], refs[rows : rows + 2], refs[rows + 2 :]
    outs, turned = refs[:-1], refs[-1]
    for row in range(rows):
        turned[:, row * L : (row + 1) * L] = lows[row][...].T
    for g in range(summand.blocks):
        m = block_of(g, where)
        bias = jnp.zeros((1, D), WIDE)
        for row in range(rows):
            at = slice(row * L, (row + 1) * L)
            grad = dot(grad_ref[at], w_ref[m]) * slope_ref[m, at].astype(WIDE)
            grad = grad.astype(LOW)
            grad_out[m, at] = grad
            bias += column_sum(grad.astype(WIDE))
        bias_out[m] = bias
        summand.write(outs, dot(turned[...], grad_out[m]).astype(LOW), g, where)


def grad_of_up(where, grad_low, weight, slope, lows, summand, wait_for=()):
    blocks, tokens, _ = slope.shape
    return call(
        partial(up_grad_kernel, summand, len(lows)),
        "grad_of_up",
        where,
        [grad_low, weight, slope, *lows],
        [array(LOW, blocks, tokens, D), array(WIDE, blocks, 1, D)] + summand.shapes,
        [pltpu.VMEM((D, tokens), LOW)],
        wait_for=wait_for,
    )


def middle_kernel(blocks, rows, where, hidden_ref, up_ref, sum_ref, vec_ref, w_ref, *refs):
    units, inverses, refs = refs[:rows], refs[rows : 2 * rows], refs[2 * rows :]
    grad_out, low_out, bias_out, gain_out, shift_out, context_out = refs
    for ref in (bias_out, gain_out, shift_out):
        ref[...] = jnp.zeros_like(ref)
    for row in range(rows):
        at = slice(row * L, (row + 1) * L)
        value = sum_ref[at]
        for m in range(blocks):
            value += dot(hidden_ref[m, at], up_ref[m], (1, 1))
        grad_out[at] = value
        for part in range(L // PART):
            inner = slice(part * PART, (part + 1) * PART)
            outer = slice(row * L + part * PART, row * L + (part + 1) * PART)
            grad = grad_out[outer]
            unit = units[row][inner]
            gain_out[...] += column_sum(grad * unit)
            shift_out[...] += column_sum(grad)
            back = norm_back(grad, unit, inverses[row][inner], vec_ref[:, G1 : G1 + D])
            grad_out[outer] = back
            low = back.astype(LOW)
            low_out[outer] = low
            bias_out[...] += column_sum(low.astype(WIDE))
        for m in range(blocks):
            context_out[row * blocks + m] = dot(
                low_out[at], w_ref[block_of(m, where), :, OUT:]
            ).astype(LOW)


def middle(where, hidden_grad, up, sum_grad, units, inverses, vectors, weight, wait_for=()):
    blocks, tokens, _ = hidden_grad.shape
    rows = len(units)
    return call(
        partial(middle_kernel, blocks, rows),
        "middle",
        where,
        [hidden_grad, up, sum_grad, vectors, weight, *units, *inverses],
        [
            array(WIDE, tokens, D),
            array(LOW, tokens, D),
            array(WIDE, 1, D),
            array(WIDE, 1, D),
            array(WIDE, 1, D),
            array(LOW, rows * blocks, L, D - OUT),
        ],
        wait_for=wait_for,
    )


def attend_back_kernel(blocks, row, chosen, where, q_ref, k_ref, v_ref, log_ref, grad_ref, out):
    lanes = lax.broadcasted_iota(jnp.int32, (L, TILE), 1)
    low_half = lanes < HD

    def block(i, carry):
        key_grads, scores, weight_grads, grads = [], [], [], []
        for h in range(HEADS_BLOCK):
            n = i * HEADS_BLOCK + h
            at = (h + 1) // 2 * TILE
            grads.append(grad_ref[row * blocks + chosen[0] + i, :, at : at + TILE])
            scores.append(dot(k_ref[n], q_ref[n], (1, 1)))
            weight_grads.append(dot(v_ref[n], grads[h], (1, 1)))
        for h in range(HEADS_BLOCK):
            n = i * HEADS_BLOCK + h
            weights = jnp.exp(scores[h] - log_ref[n])
            middle_sum = jnp.sum(weight_grads[h] * weights, axis=0, keepdims=True)
            score_grad = (weights * (weight_grads[h] - middle_sum)).astype(LOW)
            query_grad = (dot(k_ref[n].T, score_grad) * HD ** (-0.5)).T
            value_grad = dot(weights.astype(LOW), grads[h])
            key_grads.append(dot(score_grad, q_ref[n]))
            pair = (value_grad, query_grad) if SIDES[h] else (query_grad, value_grad)
            out[i, :, h * TILE : (h + 1) * TILE] = jnp.where(low_half, *pair).astype(LOW)
        pair = jnp.where(low_half, key_grads[0], key_grads[1])
        out[i, :, KEYS : KEYS + TILE] = pair.astype(LOW)
        out[i, :, OUT : OUT + TILE] = jnp.where(low_half, key_grads[2], 0.0).astype(LOW)
        out[i, :, OUT + TILE :] = jnp.zeros((L, D - OUT - TILE), LOW)
        return carry

    for i in range(len(chosen)):
        block(i, 0)


def attend_back(where, row, blocks, chosen, queries, keys, values, logs, context_grad, wait_for=()):
    return call(
        partial(attend_back_kernel, blocks, row, chosen),
        "attend_back",
        where,
        [queries, keys, values, logs, context_grad],
        [array(LOW, len(chosen), L, D)],
        wait_for=wait_for,
    )


def attention_grad_kernel(summand, rows, chosen, where, x_ref, low_ref, *refs):
    grads, contexts, refs = refs[:rows], refs[rows : 2 * rows], refs[2 * rows :]
    bias_out, outs, (x_turned, low_turned) = refs[0], refs[1:-2], refs[-2:]
    x_turned[...] = x_ref[...].T
    low_turned[...] = low_ref[...].T
    for i, g in enumerate(chosen):
        bias = jnp.zeros((1, D), WIDE)
        value = jnp.zeros((D, D), WIDE)
        own = jnp.zeros((D, D - OUT), WIDE)
        for row in range(rows):
            at = slice(row * L, (row + 1) * L)
            grad = grads[row][i]
            bias += column_sum(grad.astype(WIDE))
            value += dot(x_turned[:, at], grad)
            own += dot(low_turned[:, at], contexts[row][i])
        bias_out[i] = bias
        value = jnp.concatenate([value[:, :OUT], value[:, OUT:] + own], axis=1).astype(LOW)
        summand.write(outs, value, g, where)


def grad_of_attention(where, chosen, inputs, grad_low, grads, contexts, summand, wait_for=()):
    tokens = inputs.shape[0]
    return call(
        partial(attention_grad_kernel, summand, len(grads), chosen),
        "grad_of_attention",
        where,
        [inputs, grad_low, *grads, *contexts],
        [array(WIDE, len(chosen), 1, D)] + summand.shapes[:1],
        [pltpu.VMEM((D, tokens), LOW)] * 2,
        wait_for=wait_for,
    )


def input_grad_kernel(rows, where, w_ref, first_ref, *refs):
    grads, out = refs[:-1], refs[-1]
    cuts = len(grads) // rows
    for row in range(rows):
        at = slice(row * L, (row + 1) * L)
        value = first_ref[at]
        for c in range(cuts):
            ref = grads[row * cuts + c]
            for i in range(ref.shape[0]):
                value += dot(ref[i], w_ref[block_of(c * ref.shape[0] + i, where)], (1, 1))
        out[at] = value


def grad_of_input(where, rows, grads, weight, first_grad, wait_for=()):
    return call(
        partial(input_grad_kernel, rows),
        "grad_of_input",
        where,
        [weight, first_grad, *grads],
        [array(WIDE, *first_grad.shape)],
        wait_for=wait_for,
    )


def pack_kernel(cuts, where, *refs):
    biases, up_ref, others, out = refs[:cuts], refs[cuts], refs[cuts + 1 : -2], refs[-2]
    rows_ref = refs[-1]
    each = biases[0].shape[0]
    blocks = cuts * each
    for g in range(blocks):
        rows_ref[block_of(g, where)] = biases[g // each][g % each]
    rows = [rows_ref[m] for m in range(blocks)]
    out[:, :D] = jnp.concatenate([query_columns(row) for row in rows], axis=1)
    out[:, D : 2 * D] = jnp.concatenate([value_columns(row) for row in rows], axis=1)
    units = FF // blocks
    for m in range(blocks):
        out[:, 2 * D + m * units : 2 * D + (m + 1) * units] = up_ref[m]
    for i, ref in enumerate(others):
        out[:, TAIL + i * D : TAIL + (i + 1) * D] = ref[...]


def pack(where, biases, up_bias_grad, *others):
    blocks = up_bias_grad.shape[0]
    return call(
        partial(pack_kernel, len(biases)),
        "pack",
        where,
        [*biases, up_bias_grad, *others],
        [array(WIDE, 1, VEC)],
        [pltpu.VMEM((blocks, 1, D), WIDE)],
        limit=8,
    )[0]


def ratio_of(grad, first, second):
    moment = beta_decay * first + (1.0 - beta_decay) * grad
    second_new = beta_decay * second + (1.0 - beta_decay) * grad * grad
    ratio = (
        moment
        / (1.0 - beta_decay**STEP)
        / (jnp.sqrt(second_new / (1.0 - beta_decay**STEP)) + adam_eps)
    )
    return second_new, ratio


def squares(value):
    return jnp.sum(jnp.sum(value * value, axis=0, keepdims=True), axis=1, keepdims=True)


def adapt_kernel(cut, parts, joined, where, *refs):
    total_sum = refs[0][...].astype(WIDE)
    for ref in refs[1:parts]:
        total_sum += ref[...].astype(WIDE)
    refs = refs[parts:]
    count = len(cut)
    firsts, seconds, weights = refs[:count], refs[count : 2 * count], refs[2 * count : 3 * count]
    extra, outs = refs[3 * count : 3 * count + joined], refs[3 * count + joined :]
    lines = []
    for i, pick in enumerate(cut):
        for part, grad in pick(total_sum):
            def at(ref):
                return ref if part is None else ref.at[part]

            second_new, ratio = ratio_of(grad, at(firsts[i])[...], at(seconds[i])[...])
            weight = at(weights[i])[...]
            update = ratio + weight_decay * weight
            at(outs[3 * i])[...] = grad
            at(outs[3 * i + 1])[...] = second_new
            at(outs[3 * i + 2])[...] = update
            lines.append((squares(weight), squares(update)))
    lanes = lax.broadcasted_iota(jnp.int32, (1, 128), 1)
    held = jnp.zeros((1, 128), WIDE)
    for i, (weight_square, update_square) in enumerate(lines):
        held = jnp.where(lanes == 2 * i, weight_square, held)
        held = jnp.where(lanes == 2 * i + 1, update_square, held)
    if joined:
        vector_ref, *others = extra
        for i, ref in enumerate(others):
            for side in range(2):
                value = ref[:, side : side + 1]
                held = jnp.where(lanes == 2 * (len(lines) + i) + side, value, held)
        outs[-1][:, :VEC] = vector_ref[...]
        outs[-1][:, VEC:] = held
    else:
        outs[-1][...] = held


def adapt(name, where, parts, cut, firsts, seconds, weights, joined=()):
    outs = [array(WIDE, *w.shape) for w in weights for _ in range(3)]
    outs += [array(WIDE, 1, VEC + 128 if joined else 128)]
    operands = [*parts, *firsts, *seconds, *weights, *joined]
    return call(
        partial(adapt_kernel, cut, len(parts), len(joined)),
        name,
        where,
        operands,
        outs,
    )[:-1]


def renew_kernel(counts, where, sums_ref, grad_ref, first_ref, second_ref, vec_ref, *refs):
    many = len(counts)
    weights, updates, outs = refs[:many], refs[many : 2 * many], refs[2 * many :]
    norms = jnp.sqrt(sums_ref[...])
    outs[-1][...] = norms
    slot = 0
    for i, count in enumerate(counts):
        for part in range(count):
            trust = norms[:, 2 * slot : 2 * slot + 1] / (
                norms[:, 2 * slot + 1 : 2 * slot + 2] + norm_guard
            )
            slot += 1

            def at(ref):
                return ref if count == 1 else ref.at[part]

            new = at(weights[i])[...] - rate_matrix * trust * at(updates[i])[...]
            at(outs[2 * i])[...] = new
            at(outs[2 * i + 1])[...] = new.astype(LOW)
    second_new, ratio = ratio_of(grad_ref[...], first_ref[...], second_ref[...])
    outs[-3][...] = second_new
    outs[-2][...] = vec_ref[...] - rate_vector * ratio


def renew(where, sums, vector_grad, vector_first, vector_second, vectors, weights, updates):
    counts = [3 if w.ndim == 3 else 1 for w in weights]
    outs = [array(dtype, *w.shape) for w in weights for dtype in (WIDE, LOW)]
    outs += [array(WIDE, 1, VEC), array(WIDE, 1, VEC), array(WIDE, 1, 128)]
    operands = [sums, vector_grad, vector_first, vector_second, vectors, *weights, *updates]
    return call(
        partial(renew_kernel, counts),
        "renew",
        where,
        operands,
        outs,
    )[:-1]


def shards(
    block_input,
    cotangent,
    lengths,
    partner,
    qkv_weight,
    out_weight,
    up_weight,
    down_weight,
    qkv_first,
    out_first,
    up_first,
    down_first,
    qkv_second,
    out_second,
    up_second,
    down_second,
    vectors,
    vector_first,
    vector_second,
):
    mp_size = lax.axis_size("mp")
    dp_size = lax.axis_size("dp")
    mp_index = lax.axis_index("mp")
    dp_index = lax.axis_index("dp")
    tokens = cotangent.shape[0]
    rows = tokens // L
    own_rows = rows * PASS
    width = D // mp_size
    where = place()
    down_turned = down_weight.T
    weight_shard = arrange(where, qkv_weight, out_weight)
    up_shard = up_weight.astype(LOW)
    down_shard = down_turned.astype(LOW)
    local_lengths = lax.dynamic_slice_in_dim(lengths, mp_index * rows, rows, 0)
    inputs = lax.dynamic_slice_in_dim(block_input, mp_index * tokens, tokens, 0)
    segments = passage_ids(local_lengths).reshape(tokens, 1)
    starts = jnp.cumsum(local_lengths, axis=1) - local_lengths
    starts = (starts + L * jnp.arange(rows, dtype=jnp.int32)[:, None]).reshape(own_rows)
    partner_own = lax.dynamic_slice_in_dim(partner, mp_index * own_rows, own_rows, 0)
    ids_own = (dp_index * mp_size + mp_index) * own_rows + jnp.arange(own_rows, dtype=jnp.int32)
    ids_all = shared_ids(own_rows)
    vec = vectors.reshape(1, VEC)
    bias = arrange_bias(where, vec, mp_size)
    bias_up = vectors[2 * D : TAIL].reshape(mp_size, 1, D)

    summand = Summand(mp_size, dp_size)

    def attend_part(row, chosen, held, weight, *wait_for):
        at = slice(row * L, (row + 1) * L)
        return attend(
            where, chosen, held, inputs[at], weight, bias, vec, segments[at], wait_for=wait_for
        )

    halves = [range(mp_size // 2), range(mp_size // 2, mp_size)]
    if on_grid():
        weight_z = gather_z(weight_shard)
        weight_near = gather_near(weight_z)
        up_z = gather_z(after(up_shard, *weight_z))
        weight_far = gather_far(weight_near)
        weight_parts = weight_near + weight_far
        weight = settle(where, weight_parts + gather_core(weight_parts))
        up_z = after(up_z, *weight_far)
        kept = [[None, None] for _ in range(rows)]
        kept[0][0] = attend_part(0, halves[0], None, weight, *up_z)
        up_near = gather_near(up_z, kept[0][0][-1])
        down_z = gather_z(after(down_shard, kept[0][0][-1]), kept[0][0][-1])
        kept[0][1] = attend_part(0, halves[1], kept[0][0][5], weight, *up_near)
        kept[1][0] = attend_part(1, halves[0], None, weight, kept[0][1][-1], *down_z)
        up_far = gather_far(up_near, kept[1][0][-1])
        up_cores = gather_core(up_near, kept[1][0][-1])
        down_near = gather_near(after(down_z, *up_near), kept[1][0][-1])
        kept[1][1] = attend_part(1, halves[1], kept[1][0][5], weight, *up_far)
        up_cores += gather_core(up_far, kept[1][1][-1])
        up = settle(where, up_near + up_far + up_cores)
    else:
        weight = gather_plain(weight_shard)
        up = gather_plain(up_shard)
        down_near = []
        kept = []
        for row in range(rows):
            first = attend_part(row, halves[0], None, weight)
            kept.append([first, attend_part(row, halves[1], first[5], weight)])
    units_first, inverses_first, lows = zip(*[kept[row][1][5:8] for row in range(rows)])
    active, slope, widened = widen(where, lows, up, bias_up, wait_for=down_near)
    if on_grid():
        down_far = gather_far(after(down_near, *up_far), widened)
        down_cores = gather_core(down_near, widened) + gather_core(down_far)
        down = settle(where, down_near + down_far + down_cores)
    else:
        down = gather_plain(down_shard)
    cls_own, ended = early(where, active, down, vec, starts, units_first)
    narrowed = []
    if on_grid():
        rounds = share_core(cls_own.astype(LOW))
        narrowed.append(narrow(where, 0, active, down, vec, units_first[0], (ended, rounds)))
        rounds = share_plane(rounds, narrowed[0][-1])
        narrowed.append(narrow(where, 1, active, down, vec, units_first[1], (rounds,)))
        cls_all = share_line(rounds, narrowed[1][-1])
    else:
        for row in range(rows):
            narrowed.append(narrow(where, row, active, down, vec, units_first[row]))
        cls_all = share_plain(cls_own.astype(LOW))
    outputs, units_second, inverses_second, _ = zip(*narrowed)
    block_output = jnp.concatenate(outputs, axis=0)
    sum_grad, branch_low, down_bias_grad, gain_second_grad, shift_second_grad, _ = contrast(
        where, cotangent, units_second, inverses_second, vec, starts, cls_own, cls_all,
        ids_all[None, :], ids_own[:, None], partner_own[:, None],
    )
    *down_part, ended = grad_of_down(where, branch_low, active, summand)
    hidden_grad, up_bias_grad, *up_part, _ = grad_of_up(
        where, branch_low, down, slope, lows, summand, wait_for=(ended,)
    )
    if on_grid():
        *down_sum, added = scatter_core(where, down_part)
    (
        first_grad, attended_low, out_bias_grad, gain_first_grad, shift_first_grad, context_grad, _,
    ) = middle(
        where, hidden_grad, up, sum_grad, units_first, inverses_first, vec, weight,
        wait_for=(added,) if on_grid() else (),
    )

    def back_part(row, half, *wait_for):
        return attend_back(
            where, row, mp_size, halves[half], *kept[row][half][:4], context_grad, wait_for=wait_for
        )

    def grad_part(half, *wait_for):
        return grad_of_attention(
            where, halves[half], inputs, attended_low, [back[row][half] for row in range(rows)],
            [kept[row][half][4] for row in range(rows)], summand, wait_for=wait_for,
        )

    back = [[None, None] for _ in range(rows)]
    if on_grid():
        *down_sum, down_added = scatter_far(where, down_sum)
        *up_sum, up_added = scatter_core(where, up_part)
        back[0][1], ended = back_part(0, 1, down_added, up_added)
        back[1][1], ended = back_part(1, 1, ended)
        bias_other, other_part, ended = grad_part(1)
        *down_sum, down_added = scatter_near(where, down_sum, ended)
        back[0][0], ended = back_part(0, 0, ended, down_added)
        *up_sum, up_added = scatter_far(where, up_sum, ended)
        other_part = send(other_part, CORE)
        back[1][0], ended = back_part(1, 0, up_added, other_part)
        bias_own, own_part, ended = grad_part(0)
        *attention_sum, added = scatter_core(where, [own_part], arrived=other_part)
        *up_sum, up_added = scatter_near(where, up_sum, ended, wait_for=(added,))
    else:
        for row in range(rows):
            for half in (0, 1):
                back[row][half] = back_part(row, half)[0]
        bias_other, other_part, _ = grad_part(1)
        bias_own, own_part, _ = grad_part(0)
    vector_local = pack(
        where,
        [bias_own, bias_other],
        up_bias_grad,
        out_bias_grad,
        down_bias_grad,
        gain_first_grad,
        shift_first_grad,
        gain_second_grad,
        shift_second_grad,
    )
    grads = [back[row][half] for row in range(rows) for half in (0, 1)]
    if on_grid():
        input_grad, ended = grad_of_input(
            where, rows, grads, weight, first_grad, wait_for=(added, up_added)
        )
        *attention_sum, _ = scatter_far(where, attention_sum, ended)
        *attention_sum, ended = scatter_near(where, attention_sum)
        down_parts, up_parts = [list(p) for p in scatter_z_both(down_sum, up_sum, ended)]
        attention_parts = scatter_z(attention_sum)
    else:
        down_parts = [scatter_plain(down_part)]
        up_parts = [scatter_plain(up_part)]
        both = jnp.concatenate([own_part[: mp_size // 2], other_part[mp_size // 2 :]])
        attention_parts = [scatter_plain([both])]
        input_grad, _ = grad_of_input(where, rows, grads, weight, first_grad)
    down_grad, down_second_new, down_update, down_squares = adapt(
        "adapt_down", where, down_parts, [lambda g: [(None, g)]],
        [down_first.T], [down_second.T], [down_turned],
    )
    up_grad, up_second_new, up_update, up_squares = adapt(
        "adapt_up", where, up_parts, [lambda g: [(None, g)]], [up_first], [up_second], [up_weight]
    )
    (
        qkv_grad, qkv_second_new, qkv_update,
        out_grad, out_second_new, out_update, joined,
    ) = adapt(
        "adapt_attention",
        where,
        attention_parts,
        [
            lambda g: [
                (0, query_columns(g)),
                (1, g[:, KEYS : KEYS + width]),
                (2, value_columns(g)),
            ],
            lambda g: [(None, g[:, KEYS + width :].T)],
        ],
        [qkv_first, out_first],
        [qkv_second, out_second],
        [qkv_weight, out_weight],
        [vector_local, up_squares, down_squares],
    )
    summed = total(joined)
    vector_grad, sums = summed[:, :VEC], summed[:, VEC:]
    weights = [qkv_weight, out_weight, up_weight, down_turned]
    updates = [qkv_update, out_update, up_update, down_update]
    (
        qkv_new, qkv_copy, out_new, out_copy, up_new, up_copy, down_new, down_copy,
        vector_second_new, vector_new, norms,
    ) = renew(
        where, sums, vector_grad, vector_first.reshape(1, VEC), vector_second.reshape(1, VEC), vec,
        weights, updates,
    )
    return (
        block_output,
        input_grad,
        qkv_grad,
        out_grad,
        up_grad,
        down_grad.T,
        qkv_second_new,
        out_second_new,
        up_second_new,
        down_second_new.T,
        qkv_new,
        out_new,
        up_new,
        down_new.T,
        qkv_copy,
        out_copy,
        up_copy,
        down_copy.T,
        vector_grad.reshape(VEC),
        vector_second_new.reshape(VEC),
        vector_new.reshape(VEC),
        norms[0, :12].reshape(6, 2),
    )


def solution(mesh):
    in_specs = (
        P("dp", None),
        P(("dp", "mp"), None),
        P("dp", None),
        P("dp"),
        P(None, "dp", "mp"),
        P("mp", "dp"),
        P("dp", "mp"),
        P("mp", "dp"),
        P(None, "dp", "mp"),
        P("mp", "dp"),
        P("dp", "mp"),
        P("mp", "dp"),
        P(None, "dp", "mp"),
        P("mp", "dp"),
        P("dp", "mp"),
        P("mp", "dp"),
        P(),
        P(),
        P(),
    )
    out_specs = (
        P(("dp", "mp"), None),
        P(("dp", "mp"), None),
        P(None, "dp", "mp"),
        P("mp", "dp"),
        P("dp", "mp"),
        P("mp", "dp"),
        P(None, "dp", "mp"),
        P("mp", "dp"),
        P("dp", "mp"),
        P("mp", "dp"),
        P(None, "dp", "mp"),
        P("mp", "dp"),
        P("dp", "mp"),
        P("mp", "dp"),
        P(None, "dp", "mp"),
        P("mp", "dp"),
        P("dp", "mp"),
        P("mp", "dp"),
        P(),
        P(),
        P(),
        P(),
    )
    return jax.shard_map(shards, mesh=mesh, in_specs=in_specs, out_specs=out_specs, check_vma=False)
```
